32 devices in a mesh: seq: 2 (over x), dp: 16 (over z, y, core).
Axes of the slice: x: 2, y: 2, z: 4, core: 2. Of those that a mesh axis runs over, the one named last changes fastest.
Arguments:
- tokens: bfloat16 [16, 512, 1024], P('dp', 'seq'), may hold values from -6 to 6
- cotangent: bfloat16 [16, 512, 1024], P('dp', 'seq'), may hold values from -6 to 6
- doc_lengths: int32 [16, 4], P('dp'), may hold values from 64 to 320, as said below
- attend_weight: bfloat16 [1024, 3072], P(('seq', 'dp')), may hold values from -0.25 to 0.25
- query_bias: bfloat16 [1024], P(('seq', 'dp')), may hold values from -4 to 4
- value_bias: bfloat16 [1024], P(('seq', 'dp')), may hold values from -3 to 3
- output_weight: bfloat16 [1024, 1024], P(('seq', 'dp')), may hold values from -0.75 to 0.75
- output_bias: bfloat16 [1024], P(('seq', 'dp')), may hold values from -4 to 4
- first_gain: bfloat16 [1024], P(('seq', 'dp')), may hold values from 0.25 to 1.75
- first_shift: bfloat16 [1024], P(('seq', 'dp')), may hold values from -4 to 4
- inner_weight: bfloat16 [1024, 4096], P(('seq', 'dp')), may hold values from -0.1875 to 0.1875
- inner_bias: bfloat16 [4096], P(('seq', 'dp')), may hold values from -4 to 4
- outer_weight: bfloat16 [4096, 1024], P(('seq', 'dp')), may hold values from -0.09375 to 0.09375
- outer_bias: bfloat16 [1024], P(('seq', 'dp')), may hold values from -4 to 4
- second_gain: bfloat16 [1024], P(('seq', 'dp')), may hold values from 0.25 to 1.75
- second_shift: bfloat16 [1024], P(('seq', 'dp')), may hold values from -4 to 4
Outputs:
- layer_output: bfloat16 [16, 512, 1024], P('dp', 'seq')
- input_grad: float32 [16, 512, 1024], P('dp', 'seq')
- attend_weight_grad: float32 [1024, 3072], P(('seq', 'dp'))
- query_bias_grad: float32 [1024], P(('seq', 'dp'))
- value_bias_grad: float32 [1024], P(('seq', 'dp'))
- output_weight_grad: float32 [1024, 1024], P(('seq', 'dp'))
- output_bias_grad: float32 [1024], P(('seq', 'dp'))
- first_gain_grad: float32 [1024], P(('seq', 'dp'))
- first_shift_grad: float32 [1024], P(('seq', 'dp'))
- inner_weight_grad: float32 [1024, 4096], P(('seq', 'dp'))
- inner_bias_grad: float32 [4096], P(('seq', 'dp'))
- outer_weight_grad: float32 [4096, 1024], P(('seq', 'dp'))
- outer_bias_grad: float32 [1024], P(('seq', 'dp'))
- second_gain_grad: float32 [1024], P(('seq', 'dp'))
- second_shift_grad: float32 [1024], P(('seq', 'dp'))
The draws below stay inside these ranges and needn't reach their ends.
Inputs may be any that keep to these rules, and one draw needn't show every extreme that they name: `doc_lengths`: each row sums to 512; in each row the document at place 1 or 2, drawn per row, starts among the first 256 tokens and ends among the last 256; each of the other three holds 64 to 127 tokens.
All inputs are finite; a program needn't handle non-finite values.
Results may differ from the reference program's by a relative error of at most 0.029.
Values may be sent and summed in bfloat16 or wider, within the bound.
No kernel may reach another device: no remote copies, remote signals or barrier semaphores. Data moves between devices by JAX's collectives and lax.ppermute only.
A program may use at most 192 MiB of HBM per device.

```python
import jax
import jax.numpy as jnp
from jax import lax

D = 1024
HEADS = 16
HEAD = 64
FF = 4096
GROUP = 256
NDOC = 4
LEN = 512
NSEQ = 16


def draw_doc_lengths(key, part):
    key = jax.random.fold_in(key, 11)
    short_key = jax.random.fold_in(key, 1)
    place_key = jax.random.fold_in(key, 2)
    short_docs = jax.random.randint(short_key, (NSEQ, NDOC), GROUP // 4, GROUP // 2)
    row_index = jnp.arange(NSEQ, dtype=jnp.int32)[:, None]
    short_docs = jnp.where(row_index == 0, GROUP // 4, short_docs)
    long_place = jax.random.randint(place_key, (NSEQ, 1), 1, NDOC - 1)
    columns = jnp.arange(NDOC, dtype=jnp.int32)[None, :]
    chosen = columns == long_place
    others = jnp.sum(jnp.where(chosen, 0, short_docs), axis=1, keepdims=True)
    long_doc = LEN - others
    return jnp.where(chosen, long_doc, short_docs).astype(jnp.int32)


def shard_levels(stream_key, dims, cuts, low, high):
    factor_of = 1.0
    for position, blocks in cuts:
        draws = jax.random.uniform(jax.random.fold_in(jax.random.fold_in(stream_key, 6), position), (blocks,), jnp.float32, low / len(cuts), high / len(cuts))
        factor_of = factor_of * jnp.repeat(jnp.exp(draws), dims[position] // blocks).reshape((-1,) + (1,) * (len(dims) - 1 - position))
    return factor_of


def noise(stream_key, shape, scale, most, split=(), kind=jnp.bfloat16):
    array = scale * jax.random.normal(stream_key, shape, jnp.float32)
    if split:
        array = array * shard_levels(stream_key, shape, split, -0.22, 0.18)
    return jnp.clip(array, -most, most).astype(kind)


def setup_inputs(seed: int = 0) -> dict:
    seeds = jax.random.split(jax.random.key(seed), 17)
    return {
        "tokens": noise(seeds[0], (NSEQ, LEN, D), 1.0, 6.0, ((0, 16), (1, 2))),
        "cotangent": noise(seeds[1], (NSEQ, LEN, D), 1.0, 6.0, ((0, 16), (1, 2))),
        "doc_lengths": draw_doc_lengths(jax.random.fold_in(seeds[16], 71), 0),
        "attend_weight": noise(seeds[3], (D, 3 * D), (D // 2) ** -0.5, 0.25, ((0, 32),)),
        "query_bias": noise(seeds[4], (D,), 0.3, 4.0, ((0, 32),)),
        "value_bias": noise(seeds[5], (D,), 0.2, 3.0, ((0, 32),)),
        "output_weight": noise(seeds[6], (D, D), (D // 16) ** -0.5, 0.75, ((0, 32),)),
        "output_bias": noise(seeds[7], (D,), 0.3, 4.0, ((0, 32),)),
        "first_gain": jnp.clip(1.0 + 0.15 * jax.random.normal(seeds[8], (D,), jnp.float32), 0.25, 1.75).astype(jnp.bfloat16),
        "first_shift": noise(seeds[9], (D,), 0.3, 4.0, ((0, 32),)),
        "inner_weight": noise(seeds[10], (D, FF), D ** -0.5, 0.1875, ((0, 32),)),
        "inner_bias": noise(seeds[11], (FF,), 0.3, 4.0, ((0, 32),)),
        "outer_weight": noise(seeds[12], (FF, D), FF ** -0.5, 0.09375, ((0, 32),)),
        "outer_bias": noise(seeds[13], (D,), 0.3, 4.0, ((0, 32),)),
        "second_gain": jnp.clip(1.0 + 0.15 * jax.random.normal(seeds[14], (D,), jnp.float32), 0.25, 1.75).astype(jnp.bfloat16),
        "second_shift": noise(seeds[15], (D,), 0.3, 4.0, ((0, 32),)),
    }


@jax.custom_vjp
def low(v):
    return lax.optimization_barrier(v.astype(jnp.bfloat16)).astype(jnp.float32)

@jax.custom_vjp
def low_back(v):
    return v

def low_keep(v):
    return (low(v), None)

def low_pass(kept, grad):
    return (grad,)

def back_keep(v):
    return (v, None)

def back_low(kept, grad):
    return (low(grad),)
low.defvjp(low_keep, low_pass)
low_back.defvjp(back_keep, back_low)
highest = lax.Precision.HIGHEST
epsilon = 1e-12
masked_score = -1e+30

def rounded(value):
    return low(low_back(value))

def layer_norm(value, gain, shift):
    mean_value = lax.optimization_barrier(jnp.mean(value, axis=-1, keepdims=True))
    center = value - mean_value
    inverse = lax.rsqrt(lax.optimization_barrier(jnp.mean(center * center, axis=-1, keepdims=True)) + epsilon)
    return center * inverse * gain + shift

def doc_numbers(lengths_row):
    doc_ends = jnp.cumsum(lengths_row).astype(jnp.int32)
    positions = jnp.arange(LEN, dtype=jnp.int32)
    return lax.optimization_barrier(jnp.sum((positions[:, None] >= doc_ends[None, :]).astype(jnp.int32), axis=1)).astype(jnp.int32)

def split_heads(matrix):
    return matrix.reshape(LEN, HEADS, HEAD).transpose(1, 0, 2)

def sequence_attention(inputs):
    queries, keys, values, doc_ids = inputs
    allowed = doc_ids[:, None] == doc_ids[None, :]

    def one_head(head_inputs):
        head_query, head_key, head_value = head_inputs
        raw = low_back(jnp.dot(head_query, head_key.T, precision=highest) * HEAD ** (-0.5))
        scores = jnp.where(allowed, raw, masked_score)
        row_peak = lax.optimization_barrier(jnp.max(scores, axis=-1, keepdims=True))
        expo_terms = jnp.exp(scores - row_peak)
        weights = low(expo_terms / lax.optimization_barrier(jnp.sum(expo_terms, axis=-1, keepdims=True)))
        return jnp.dot(weights, head_value, precision=highest)
    heads_out = lax.map(jax.checkpoint(one_head), (split_heads(queries), split_heads(keys), split_heads(values)))
    return heads_out.transpose(1, 0, 2).reshape(LEN, D)

def forward(tokens_flat, doc_ids, attend_weight, query_bias, value_bias, output_weight, output_bias, first_gain, first_shift, inner_weight, inner_bias, outer_weight, outer_bias, second_gain, second_shift):
    bias_row = jnp.concatenate([query_bias, jnp.zeros_like(query_bias), value_bias])
    projected = jnp.dot(tokens_flat, attend_weight, precision=highest) + bias_row
    queries = rounded(projected[:, :D])
    keys = rounded(projected[:, D:2 * D])
    values = rounded(projected[:, 2 * D:])
    attended = lax.map(jax.checkpoint(sequence_attention), (queries.reshape(NSEQ, LEN, D), keys.reshape(NSEQ, LEN, D), values.reshape(NSEQ, LEN, D), doc_ids))
    attended = rounded(attended.reshape(NSEQ * LEN, D))
    branch = low_back(jnp.dot(attended, output_weight, precision=highest) + output_bias)
    first_out = layer_norm(tokens_flat + branch, first_gain, first_shift)
    pre_act = low_back(jnp.dot(low(first_out), inner_weight, precision=highest) + inner_bias)
    activated = low(jax.nn.gelu(pre_act, approximate=False))
    mlp_out = low_back(jnp.dot(activated, outer_weight, precision=highest) + outer_bias)
    return layer_norm(first_out + mlp_out, second_gain, second_shift)

def reference(tokens, cotangent, doc_lengths, attend_weight, query_bias, value_bias, output_weight, output_bias, first_gain, first_shift, inner_weight, inner_bias, outer_weight, outer_bias, second_gain, second_shift):
    doc_ids = jax.vmap(doc_numbers)(doc_lengths)
    params = tuple((item.astype(jnp.float32) for item in (attend_weight, query_bias, value_bias, output_weight, output_bias, first_gain, first_shift, inner_weight, inner_bias, outer_weight, outer_bias, second_gain, second_shift)))
    tokens_flat = tokens.reshape(NSEQ * LEN, D).astype(jnp.float32)

    def wrapped(tokens_in, *param_list):
        return forward(tokens_in, doc_ids, *param_list)
    layer_out, pull = jax.vjp(wrapped, tokens_flat, *params)
    grads = pull(cotangent.reshape(NSEQ * LEN, D).astype(jnp.float32))
    return (layer_out.astype(jnp.bfloat16).reshape(NSEQ, LEN, D), grads[0].reshape(NSEQ, LEN, D), grads[1], grads[2], grads[3], grads[4], grads[5], grads[6], grads[7], grads[8], grads[9], grads[10], grads[11], grads[12], grads[13])
```

```python
import functools

import jax
import jax.numpy as jnp
from jax import lax
from jax.experimental import pallas as pl
from jax.experimental.pallas import tpu as pltpu
from jax.sharding import PartitionSpec as P

D = 1024
HEADS = 16
HEAD = 64
GROUP = 256


epsilon = 1e-12
masked_score = -1e30


def norm_forward(value, gain, shift):
    mean_value = jnp.mean(value, axis=-1, keepdims=True)
    center = value - mean_value
    inverse = lax.rsqrt(jnp.mean(center * center, axis=-1, keepdims=True) + epsilon)
    normed = center * inverse
    return (normed * gain + shift, normed, inverse)


def norm_backward(upstream, normed, inverse, gain):
    scaled = upstream * gain
    first_mean = jnp.mean(scaled, axis=-1, keepdims=True)
    second_mean = jnp.mean(scaled * normed, axis=-1, keepdims=True)
    return inverse * (scaled - first_mean - normed * second_mean)


def exact_gelu(value):
    return jax.nn.gelu(value, approximate=False)


def pair_scores(query_pair, key_pair, allowed, factor):
    raw = (
        jnp.einsum("qhd,khd->hqk", query_pair, key_pair, preferred_element_type=jnp.float32)
        * factor
    )
    return jnp.where(allowed[None], raw, masked_score)


def column_pair(matrix, column_start, row_count):
    return lax.dynamic_slice_in_dim(matrix, column_start, 2 * HEAD, 1).reshape(row_count, 2, HEAD)


def general_local(
    tokens,
    cotangent,
    doc_lengths,
    attend_weight,
    query_bias,
    value_bias,
    output_weight,
    output_bias,
    first_gain,
    first_shift,
    inner_weight,
    inner_bias,
    outer_weight,
    outer_bias,
    second_gain,
    second_shift,
):
    (
        attend_mat,
        query_add,
        value_add,
        output_mat,
        output_add,
        first_scale,
        first_offset,
        inner_mat,
        inner_add,
        outer_mat,
        outer_add,
        second_scale,
        second_offset,
    ) = (
        lax.all_gather(attend_weight, ("seq", "dp"), axis=0, tiled=True),
        lax.all_gather(query_bias, ("seq", "dp"), axis=0, tiled=True),
        lax.all_gather(value_bias, ("seq", "dp"), axis=0, tiled=True),
        lax.all_gather(output_weight, ("seq", "dp"), axis=0, tiled=True),
        lax.all_gather(output_bias, ("seq", "dp"), axis=0, tiled=True),
        lax.all_gather(first_gain, ("seq", "dp"), axis=0, tiled=True),
        lax.all_gather(first_shift, ("seq", "dp"), axis=0, tiled=True),
        lax.all_gather(inner_weight, ("seq", "dp"), axis=0, tiled=True),
        lax.all_gather(inner_bias, ("seq", "dp"), axis=0, tiled=True),
        lax.all_gather(outer_weight, ("seq", "dp"), axis=0, tiled=True),
        lax.all_gather(outer_bias, ("seq", "dp"), axis=0, tiled=True),
        lax.all_gather(second_gain, ("seq", "dp"), axis=0, tiled=True),
        lax.all_gather(second_shift, ("seq", "dp"), axis=0, tiled=True),
    )
    token_rows = tokens.reshape(GROUP, D)
    key_total = GROUP * lax.axis_size("seq")
    group_index = lax.axis_index("seq")
    doc_ends = jnp.cumsum(doc_lengths[0])
    positions = lax.iota(jnp.int32, key_total)
    key_docs = jnp.sum((positions[:, None] >= doc_ends[None, :]).astype(jnp.int32), axis=1)
    query_docs = lax.dynamic_slice_in_dim(key_docs, group_index * GROUP, GROUP)
    allowed = query_docs[:, None] == key_docs[None, :]
    factor = HEAD ** (-0.5)
    pair_count = HEADS // 2
    bias_row = jnp.concatenate(
        [query_add.astype(jnp.float32), jnp.zeros((D,), jnp.float32), value_add.astype(jnp.float32)]
    )
    projected = jnp.dot(token_rows, attend_mat, preferred_element_type=jnp.float32) + bias_row
    queries = projected[:, :D].astype(jnp.bfloat16)
    keys_mine = projected[:, D : 2 * D].astype(jnp.bfloat16)
    values_mine = projected[:, 2 * D :].astype(jnp.bfloat16)
    keys_all, values_all = (
        lax.all_gather(keys_mine, "seq", axis=0, tiled=True),
        lax.all_gather(values_mine, "seq", axis=0, tiled=True),
    )

    def forward_pair(pair_index, state_tuple):
        mixed_heads, logsum = state_tuple
        column_start = pair_index * 2 * HEAD
        query_pair = column_pair(queries, column_start, GROUP)
        key_pair = column_pair(keys_all, column_start, key_total)
        value_pair = column_pair(values_all, column_start, key_total)
        scores = pair_scores(query_pair, key_pair, allowed, factor)
        row_peak = jnp.max(scores, axis=-1, keepdims=True)
        expo_terms = jnp.exp(scores - row_peak)
        row_total = jnp.sum(expo_terms, axis=-1, keepdims=True)
        weights = (expo_terms / row_total).astype(jnp.bfloat16)
        result = jnp.einsum(
            "hqk,khd->qhd", weights, value_pair, preferred_element_type=jnp.float32
        ).reshape(GROUP, 2 * HEAD)
        mixed_heads = lax.dynamic_update_slice_in_dim(mixed_heads, result, column_start, 1)
        logsum = lax.dynamic_update_slice_in_dim(
            logsum, row_peak + jnp.log(row_total), pair_index * 2, 0
        )
        return (mixed_heads, logsum)

    mixed_heads, logsum = lax.fori_loop(
        0,
        pair_count,
        forward_pair,
        (jnp.zeros((GROUP, D), jnp.float32), jnp.zeros((HEADS, GROUP, 1), jnp.float32)),
    )
    attended = mixed_heads.astype(jnp.bfloat16)
    branch = jnp.dot(attended, output_mat, preferred_element_type=jnp.float32) + output_add.astype(
        jnp.float32
    )
    first_out, first_normed, first_inverse = norm_forward(
        token_rows.astype(jnp.float32) + branch,
        first_scale.astype(jnp.float32),
        first_offset.astype(jnp.float32),
    )
    first_low = first_out.astype(jnp.bfloat16)
    pre_act = jnp.dot(first_low, inner_mat, preferred_element_type=jnp.float32) + inner_add.astype(
        jnp.float32
    )
    activated = exact_gelu(pre_act).astype(jnp.bfloat16)
    mlp_out = jnp.dot(activated, outer_mat, preferred_element_type=jnp.float32) + outer_add.astype(
        jnp.float32
    )
    second_out, second_normed, second_inverse = norm_forward(
        first_out + mlp_out, second_scale.astype(jnp.float32), second_offset.astype(jnp.float32)
    )
    layer_output = second_out.astype(jnp.bfloat16).reshape(1, GROUP, D)
    (
        attend_mat,
        query_add,
        value_add,
        output_mat,
        output_add,
        first_scale,
        first_offset,
        inner_mat,
        inner_add,
        outer_mat,
        outer_add,
        second_scale,
        second_offset,
    ) = (
        lax.all_gather(attend_weight, ("seq", "dp"), axis=0, tiled=True),
        lax.all_gather(query_bias, ("seq", "dp"), axis=0, tiled=True),
        lax.all_gather(value_bias, ("seq", "dp"), axis=0, tiled=True),
        lax.all_gather(output_weight, ("seq", "dp"), axis=0, tiled=True),
        lax.all_gather(output_bias, ("seq", "dp"), axis=0, tiled=True),
        lax.all_gather(first_gain, ("seq", "dp"), axis=0, tiled=True),
        lax.all_gather(first_shift, ("seq", "dp"), axis=0, tiled=True),
        lax.all_gather(inner_weight, ("seq", "dp"), axis=0, tiled=True),
        lax.all_gather(inner_bias, ("seq", "dp"), axis=0, tiled=True),
        lax.all_gather(outer_weight, ("seq", "dp"), axis=0, tiled=True),
        lax.all_gather(outer_bias, ("seq", "dp"), axis=0, tiled=True),
        lax.all_gather(second_gain, ("seq", "dp"), axis=0, tiled=True),
        lax.all_gather(second_shift, ("seq", "dp"), axis=0, tiled=True),
    )
    upstream = cotangent.reshape(GROUP, D).astype(jnp.float32)
    grad_second_scale = jnp.sum(upstream * second_normed, axis=0)
    grad_second_offset = jnp.sum(upstream, axis=0)
    grad_two = norm_backward(
        upstream, second_normed, second_inverse, second_scale.astype(jnp.float32)
    )
    grad_mlp = grad_two.astype(jnp.bfloat16)
    grad_outer_add = jnp.sum(grad_mlp.astype(jnp.float32), axis=0)
    grad_outer_mat = jnp.einsum(
        "tf,td->fd", activated, grad_mlp, preferred_element_type=jnp.float32
    )
    grad_act = jnp.einsum("td,fd->tf", grad_mlp, outer_mat, preferred_element_type=jnp.float32)
    unused_value, gelu_pull = jax.vjp(exact_gelu, pre_act)
    grad_pre = gelu_pull(grad_act)[0].astype(jnp.bfloat16)
    grad_inner_add = jnp.sum(grad_pre.astype(jnp.float32), axis=0)
    grad_inner_mat = jnp.einsum(
        "td,tf->df", first_low, grad_pre, preferred_element_type=jnp.float32
    )
    grad_first = (
        jnp.einsum("tf,df->td", grad_pre, inner_mat, preferred_element_type=jnp.float32) + grad_two
    )
    grad_first_scale = jnp.sum(grad_first * first_normed, axis=0)
    grad_first_offset = jnp.sum(grad_first, axis=0)
    grad_hidden = norm_backward(
        grad_first, first_normed, first_inverse, first_scale.astype(jnp.float32)
    )
    grad_branch = grad_hidden.astype(jnp.bfloat16)
    grad_output_add = jnp.sum(grad_branch.astype(jnp.float32), axis=0)
    grad_output_mat = jnp.einsum(
        "td,te->de", attended, grad_branch, preferred_element_type=jnp.float32
    )
    grad_attended = jnp.einsum(
        "te,de->td", grad_branch, output_mat, preferred_element_type=jnp.float32
    ).astype(jnp.bfloat16)

    def backward_pair(pair_index, state_tuple):
        grad_queries, grad_keys, grad_values = state_tuple
        column_start = pair_index * 2 * HEAD
        query_pair = column_pair(queries, column_start, GROUP)
        key_pair = column_pair(keys_all, column_start, key_total)
        value_pair = column_pair(values_all, column_start, key_total)
        upstream_pair = column_pair(grad_attended, column_start, GROUP)
        scores = pair_scores(query_pair, key_pair, allowed, factor)
        pair_logsum = lax.dynamic_slice_in_dim(logsum, pair_index * 2, 2, 0)
        pair_probs = jnp.exp(scores - pair_logsum)
        weights = pair_probs.astype(jnp.bfloat16)
        grad_weights = jnp.einsum(
            "qhd,khd->hqk", upstream_pair, value_pair, preferred_element_type=jnp.float32
        )
        row_dot = jnp.sum(grad_weights * pair_probs, axis=-1, keepdims=True)
        grad_scores = (pair_probs * (grad_weights - row_dot)).astype(jnp.bfloat16)
        query_part = (
            jnp.einsum("hqk,khd->qhd", grad_scores, key_pair, preferred_element_type=jnp.float32)
            * factor
        )
        key_part = (
            jnp.einsum("hqk,qhd->khd", grad_scores, query_pair, preferred_element_type=jnp.float32)
            * factor
        )
        value_part = jnp.einsum(
            "hqk,qhd->khd", weights, upstream_pair, preferred_element_type=jnp.float32
        )
        grad_queries = lax.dynamic_update_slice_in_dim(
            grad_queries, query_part.reshape(GROUP, 2 * HEAD), column_start, 1
        )
        grad_keys = lax.dynamic_update_slice_in_dim(
            grad_keys, key_part.reshape(key_total, 2 * HEAD), column_start, 1
        )
        grad_values = lax.dynamic_update_slice_in_dim(
            grad_values, value_part.reshape(key_total, 2 * HEAD), column_start, 1
        )
        return (grad_queries, grad_keys, grad_values)

    grad_queries, grad_keys, grad_values = lax.fori_loop(
        0,
        pair_count,
        backward_pair,
        (
            jnp.zeros((GROUP, D), jnp.float32),
            jnp.zeros((key_total, D), jnp.float32),
            jnp.zeros((key_total, D), jnp.float32),
        ),
    )
    key_share, value_share = (
        lax.psum_scatter(
            grad_keys.astype(jnp.bfloat16), "seq", scatter_dimension=0, tiled=True
        ).astype(jnp.float32),
        lax.psum_scatter(
            grad_values.astype(jnp.bfloat16), "seq", scatter_dimension=0, tiled=True
        ).astype(jnp.float32),
    )
    grad_projected = jnp.concatenate(
        [
            grad_queries.astype(jnp.bfloat16),
            key_share.astype(jnp.bfloat16),
            value_share.astype(jnp.bfloat16),
        ],
        axis=1,
    )
    grad_query_add = jnp.sum(grad_projected[:, :D].astype(jnp.float32), axis=0)
    grad_value_add = jnp.sum(grad_projected[:, 2 * D :].astype(jnp.float32), axis=0)
    grad_attend_mat = jnp.einsum(
        "td,te->de", token_rows, grad_projected, preferred_element_type=jnp.float32
    )
    input_grad = grad_hidden + jnp.einsum(
        "te,de->td", grad_projected, attend_mat, preferred_element_type=jnp.float32
    )
    (
        sum_attend_mat,
        sum_query_add,
        sum_value_add,
        sum_output_mat,
        sum_output_add,
        sum_first_scale,
        sum_first_offset,
        sum_inner_mat,
        sum_inner_add,
        sum_outer_mat,
        sum_outer_add,
        sum_second_scale,
        sum_second_offset,
    ) = (
        lax.psum_scatter(grad_attend_mat, ("seq", "dp"), scatter_dimension=0, tiled=True),
        lax.psum_scatter(grad_query_add, ("seq", "dp"), scatter_dimension=0, tiled=True),
        lax.psum_scatter(grad_value_add, ("seq", "dp"), scatter_dimension=0, tiled=True),
        lax.psum_scatter(grad_output_mat, ("seq", "dp"), scatter_dimension=0, tiled=True),
        lax.psum_scatter(grad_output_add, ("seq", "dp"), scatter_dimension=0, tiled=True),
        lax.psum_scatter(grad_first_scale, ("seq", "dp"), scatter_dimension=0, tiled=True),
        lax.psum_scatter(grad_first_offset, ("seq", "dp"), scatter_dimension=0, tiled=True),
        lax.psum_scatter(grad_inner_mat, ("seq", "dp"), scatter_dimension=0, tiled=True),
        lax.psum_scatter(grad_inner_add, ("seq", "dp"), scatter_dimension=0, tiled=True),
        lax.psum_scatter(grad_outer_mat, ("seq", "dp"), scatter_dimension=0, tiled=True),
        lax.psum_scatter(grad_outer_add, ("seq", "dp"), scatter_dimension=0, tiled=True),
        lax.psum_scatter(grad_second_scale, ("seq", "dp"), scatter_dimension=0, tiled=True),
        lax.psum_scatter(grad_second_offset, ("seq", "dp"), scatter_dimension=0, tiled=True),
    )
    return (
        layer_output,
        input_grad.reshape(1, GROUP, D),
        sum_attend_mat,
        sum_query_add,
        sum_value_add,
        sum_output_mat,
        sum_output_add,
        sum_first_scale,
        sum_first_offset,
        sum_inner_mat,
        sum_inner_add,
        sum_outer_mat,
        sum_outer_add,
        sum_second_scale,
        sum_second_offset,
    )


AXES = ("seq", "dp")
DEVICES = 32
ORDER_ONE = ((3, 2, 1, 4), (3, 2, 4, 1))
ORDER_TWO = ((1, 3, 2, 4), (4, 3, 2, 1))
REMOTE = GROUP - 64
ROWS = GROUP + REMOTE


def swap(value, masks):
    pairs = [(i, i ^ masks[i & 1]) for i in range(DEVICES)]
    return lax.ppermute(value, AXES, pairs)


def stage_masks(order, stage):
    return (1 << order[0][stage], 1 << order[1][stage])


def chip_mask(bits, place):
    return sum(1 << b for t, b in enumerate(bits) if place >> t & 1)


def gather_pieces(weight, me, order):
    rows, columns = weight.shape
    half = columns // 2
    core = me & 1
    mine = lax.dynamic_slice(weight, (0, core * half), (rows, half))
    other = lax.dynamic_slice(weight, (0, (1 - core) * half), (rows, half))
    first = jnp.stack([mine, swap(other, (1, 1))])
    second = jnp.concatenate([first, swap(first, stage_masks(order, 0))])
    quad = jnp.concatenate([second, swap(second, stage_masks(order, 1))])
    quad_two = swap(quad, stage_masks(order, 2))
    quad_three = swap(quad, stage_masks(order, 3))
    quad_four = swap(quad_two, stage_masks(order, 3))
    own = [quad, quad_two, quad_three, quad_four]
    return own + [swap(piece, (1, 1)) for piece in own]


def assemble_body(order, me_ref, *refs):
    piece_refs, out_ref, sems = refs[:8], refs[8], refs[9]
    me = me_ref[0]
    _, rows, half = piece_refs[0].shape
    copies = []
    for number, piece in enumerate(piece_refs):
        base = me ^ (number // 4)
        core = base & 1
        for sub in range(8):
            place = (number % 4) * 4 + sub // 2
            mask = jnp.where(core == 0, chip_mask(order[0], place), chip_mask(order[1], place))
            shard = (base ^ mask) ^ (sub & 1)
            target = out_ref.at[
                pl.ds(pl.multiple_of(shard * rows, rows), rows),
                pl.ds(pl.multiple_of(core * half, half), half),
            ]
            copies.append(
                pltpu.make_async_copy(piece.at[sub], target, sems.at[number * 8 + sub])
            )
    for copy in copies:
        copy.start()
    for copy in copies:
        copy.wait()


def gather(weight, me, order):
    rows, columns = weight.shape
    pieces = gather_pieces(weight, me, order)
    return pl.pallas_call(
        functools.partial(assemble_body, order),
        out_shape=jax.ShapeDtypeStruct((rows * DEVICES, columns), weight.dtype),
        in_specs=[pl.BlockSpec(memory_space=pltpu.SMEM)]
        + [pl.BlockSpec(memory_space=pl.ANY)] * 8,
        out_specs=pl.BlockSpec(memory_space=pltpu.VMEM),
        scratch_shapes=[pltpu.SemaphoreType.DMA((64,))],
        compiler_params=pltpu.CompilerParams(vmem_limit_bytes=24 * 2**20),
        cost_estimate=pl.CostEstimate(
            flops=0, bytes_accessed=4 * rows * DEVICES * columns, transcendentals=0
        ),
    )(me.reshape(1), *pieces)


def place_of(bits, shard):
    place = shard & 1
    for t, b in enumerate(bits):
        place = place | ((shard >> b) & 1) << (t + 1)
    return place


def weight_grad_body(order, tile, me_ref, left_ref, right_ref, keep_ref, send_ref):
    me = me_ref[0]
    _, rows, half = keep_ref.shape
    per_tile = tile // rows

    def step(i, carry):
        left = left_ref[:, pl.ds(pl.multiple_of(i * tile, tile), tile)]
        for side, out_ref in ((1, send_ref), (0, keep_ref)):
            base = me ^ side
            core = base & 1
            right = right_ref[:, pl.ds(pl.multiple_of(core * half, half), half)]
            product = lax.dot_general(
                left, right, (((0,), (0,)), ((), ())), preferred_element_type=jnp.float32
            ).astype(jnp.bfloat16)
            for sub in range(per_tile):
                shard = (i * per_tile + sub) ^ base
                place = jnp.where(
                    core == 0, place_of(order[0], shard), place_of(order[1], shard)
                )
                out_ref[place] = product[sub * rows : (sub + 1) * rows]
        return carry

    lax.fori_loop(0, left_ref.shape[1] // tile, step, 0)


def weight_grad(left, right, me, order):
    tokens, depth = left.shape
    columns = right.shape[1]
    rows, half = depth // DEVICES, columns // 2
    shape = jax.ShapeDtypeStruct((DEVICES, rows, half), jnp.bfloat16)
    return pl.pallas_call(
        functools.partial(weight_grad_body, order, 256),
        out_shape=(shape, shape),
        in_specs=[pl.BlockSpec(memory_space=pltpu.SMEM)]
        + [pl.BlockSpec(memory_space=pltpu.VMEM)] * 2,
        out_specs=(pl.BlockSpec(memory_space=pltpu.VMEM),) * 2,
        compiler_params=pltpu.CompilerParams(vmem_limit_bytes=40 * 2**20),
        cost_estimate=pl.CostEstimate(
            flops=2 * tokens * depth * columns,
            bytes_accessed=2 * (depth * columns + tokens * (depth + columns)),
            transcendentals=0,
        ),
    )(me.reshape(1), left, right)


def add_low(one, two):
    return (one.astype(jnp.float32) + two.astype(jnp.float32)).astype(jnp.bfloat16)


def scatter_sum(left, right, me, order):
    keep, send = weight_grad(left, right, me, order)
    total = add_low(keep, swap(send, (1, 1)))
    for stage in (3, 2, 1, 0):
        half = 2 << stage
        arrived = swap(total[half:], stage_masks(order, stage))
        total = add_low(total[:half], arrived)
    mine = total[0].astype(jnp.float32)
    other = swap(total[1], (1, 1)).astype(jnp.float32)
    return jnp.where(
        (me & 1) == 0,
        jnp.concatenate([mine, other], axis=1),
        jnp.concatenate([other, mine], axis=1),
    )


def attend_forward_body(query_docs, key_docs, query_ref, key_ref, value_ref, mixed_ref, log_ref):
    allowed = query_docs[...] == key_docs[...]
    queries, keys, values = query_ref[...], key_ref[...], value_ref[...]
    lanes = lax.broadcasted_iota(jnp.int32, queries.shape, 1)
    results, logs = [], []
    for head in range(2):
        chosen = (lanes < HEAD) if head == 0 else (lanes >= HEAD)
        raw = lax.dot_general(
            jnp.where(chosen, queries, jnp.zeros_like(queries)),
            keys,
            (((1,), (1,)), ((), ())),
            preferred_element_type=jnp.float32,
        )
        scores = jnp.where(allowed, raw * HEAD**-0.5, masked_score)
        peak = jnp.max(scores, axis=-1, keepdims=True)
        terms = jnp.exp(scores - peak)
        total = jnp.sum(terms, axis=-1, keepdims=True)
        weights = (terms * (1.0 / total)).astype(jnp.bfloat16)
        results.append(jnp.dot(weights, values, preferred_element_type=jnp.float32))
        logs.append(peak + jnp.log(total))
    mixed_ref[...] = jnp.where(lanes < HEAD, results[0], results[1]).astype(jnp.bfloat16)
    log_ref[0] = jnp.where(lanes < HEAD, logs[0], logs[1])


def attend_forward(query_docs, key_docs, projected):
    pairs = HEADS // 2
    return pl.pallas_call(
        attend_forward_body,
        grid=(pairs,),
        in_specs=[
            pl.BlockSpec((GROUP, 1), lambda i: (0, 0)),
            pl.BlockSpec((1, ROWS), lambda i: (0, 0)),
            pl.BlockSpec((GROUP, 128), lambda i: (0, i)),
            pl.BlockSpec((ROWS, 128), lambda i: (0, pairs + i)),
            pl.BlockSpec((ROWS, 128), lambda i: (0, 2 * pairs + i)),
        ],
        out_specs=[
            pl.BlockSpec((GROUP, 128), lambda i: (0, i)),
            pl.BlockSpec((1, GROUP, 128), lambda i: (i, 0, 0)),
        ],
        out_shape=[
            jax.ShapeDtypeStruct((GROUP, D), jnp.bfloat16),
            jax.ShapeDtypeStruct((pairs, GROUP, 128), jnp.float32),
        ],
        compiler_params=pltpu.CompilerParams(vmem_limit_bytes=32 * 2**20),
        cost_estimate=pl.CostEstimate(
            flops=4 * GROUP * ROWS * 128 * HEADS,
            bytes_accessed=2 * 2 * ROWS * 3 * D,
            transcendentals=HEADS * GROUP * ROWS,
        ),
    )(query_docs, key_docs, projected, projected, projected)


def attend_backward_body(
    query_docs, key_docs, query_ref, key_ref, value_ref, upstream_ref, log_ref, grad_ref
):
    pair = pl.program_id(0)
    allowed = query_docs[...] == key_docs[...]
    queries, keys, values = query_ref[...], key_ref[...], value_ref[...]
    upstream = upstream_ref[...]
    lanes = lax.broadcasted_iota(jnp.int32, queries.shape, 1)
    zeros = jnp.zeros_like(queries)
    across = (((1,), (1,)), ((), ()))
    down = (((0,), (0,)), ((), ()))
    query_parts, key_parts, value_parts = [], [], []
    for head in range(2):
        chosen = (lanes < HEAD) if head == 0 else (lanes >= HEAD)
        raw = lax.dot_general(
            jnp.where(chosen, queries, zeros), keys, across, preferred_element_type=jnp.float32
        )
        scores = jnp.where(allowed, raw * HEAD**-0.5, masked_score)
        probs = jnp.exp(scores - log_ref[0, :, head * HEAD : head * HEAD + 1])
        grad_weights = lax.dot_general(
            jnp.where(chosen, upstream, zeros), values, across, preferred_element_type=jnp.float32
        )
        row_dot = jnp.sum(grad_weights * probs, axis=-1, keepdims=True)
        grad_scores = (probs * (grad_weights - row_dot)).astype(jnp.bfloat16)
        weights = probs.astype(jnp.bfloat16)
        query_parts.append(jnp.dot(grad_scores, keys, preferred_element_type=jnp.float32))
        key_parts.append(
            lax.dot_general(grad_scores, queries, down, preferred_element_type=jnp.float32)
        )
        value_parts.append(
            lax.dot_general(weights, upstream, down, preferred_element_type=jnp.float32)
        )
    wide = lax.broadcasted_iota(jnp.int32, keys.shape, 1) < HEAD
    grad_queries = jnp.where(lanes < HEAD, query_parts[0], query_parts[1]) * HEAD**-0.5
    grad_keys = jnp.where(wide, key_parts[0], key_parts[1]) * HEAD**-0.5
    grad_values = jnp.where(wide, value_parts[0], value_parts[1])
    column = pl.multiple_of(pair * 128, 128)
    grad_ref[:GROUP, pl.ds(column, 128)] = grad_queries.astype(jnp.bfloat16)
    grad_ref[GROUP:, pl.ds(column, 128)] = jnp.zeros((REMOTE, 128), jnp.bfloat16)
    grad_ref[:, pl.ds(pl.multiple_of(D + pair * 128, 128), 128)] = grad_keys.astype(jnp.bfloat16)
    grad_ref[:, pl.ds(pl.multiple_of(2 * D + pair * 128, 128), 128)] = grad_values.astype(
        jnp.bfloat16
    )


def attend_backward(query_docs, key_docs, projected, upstream, logs):
    pairs = HEADS // 2
    return pl.pallas_call(
        attend_backward_body,
        grid=(pairs,),
        in_specs=[
            pl.BlockSpec((GROUP, 1), lambda i: (0, 0)),
            pl.BlockSpec((1, ROWS), lambda i: (0, 0)),
            pl.BlockSpec((GROUP, 128), lambda i: (0, i)),
            pl.BlockSpec((ROWS, 128), lambda i: (0, pairs + i)),
            pl.BlockSpec((ROWS, 128), lambda i: (0, 2 * pairs + i)),
            pl.BlockSpec((GROUP, 128), lambda i: (0, i)),
            pl.BlockSpec((1, GROUP, 128), lambda i: (i, 0, 0)),
        ],
        out_specs=pl.BlockSpec((ROWS, 3 * D), lambda i: (0, 0)),
        out_shape=jax.ShapeDtypeStruct((ROWS, 3 * D), jnp.bfloat16),
        compiler_params=pltpu.CompilerParams(vmem_limit_bytes=32 * 2**20),
        cost_estimate=pl.CostEstimate(
            flops=10 * GROUP * ROWS * 128 * HEADS,
            bytes_accessed=2 * 3 * ROWS * 3 * D,
            transcendentals=HEADS * GROUP * ROWS,
        ),
    )(query_docs, key_docs, projected, projected, projected, upstream, logs)


def gather_small(vectors, me):
    total = jnp.concatenate(vectors)[None, :]
    for bit in range(5):
        total = jnp.concatenate([total, swap(total, (1 << bit, 1 << bit))])
    shards = lax.iota(jnp.int32, DEVICES)
    chosen = ((shards[:, None] ^ me) == shards[None, :]).astype(jnp.bfloat16)
    ordered = jnp.dot(chosen, total, preferred_element_type=jnp.float32)
    results, start = [], 0
    for vector in vectors:
        size = vector.shape[0]
        results.append(ordered[:, start : start + size].reshape(1, DEVICES * size))
        start += size
    return results


def scatter_small(vectors, me):
    sizes = [vector.shape[0] // DEVICES for vector in vectors]
    natural = jnp.concatenate(
        [vector.reshape(DEVICES, size) for vector, size in zip(vectors, sizes)], axis=1
    )
    shards = lax.iota(jnp.int32, DEVICES)
    chosen = ((shards[:, None] ^ me) == shards[None, :]).astype(jnp.float32)
    total = jnp.dot(
        chosen, natural, precision=lax.Precision.HIGHEST, preferred_element_type=jnp.float32
    )
    for bit in (4, 3, 2, 1, 0):
        half = 1 << bit
        total = total[:half] + swap(total[half:], (half, half))
    results, start = [], 0
    for size in sizes:
        results.append(total[0, start : start + size])
        start += size
    return results


def fast_local(
    tokens,
    cotangent,
    doc_lengths,
    attend_weight,
    query_bias,
    value_bias,
    output_weight,
    output_bias,
    first_gain,
    first_shift,
    inner_weight,
    inner_bias,
    outer_weight,
    outer_bias,
    second_gain,
    second_shift,
):
    me = lax.axis_index(AXES)
    group_index = me >> 4
    near = tokens.reshape(GROUP, D)
    far = lax.ppermute(
        lax.dynamic_slice(near, (64 * (1 - group_index), 0), (REMOTE, D)),
        "seq",
        [(0, 1), (1, 0)],
    )
    token_rows = jnp.concatenate([near, far])
    (
        query_add,
        value_add,
        output_add,
        first_scale,
        first_offset,
        inner_add,
        outer_add,
        second_scale,
        second_offset,
    ) = gather_small(
        [
            query_bias,
            value_bias,
            output_bias,
            first_gain,
            first_shift,
            inner_bias,
            outer_bias,
            second_gain,
            second_shift,
        ],
        me,
    )
    attend_mat = gather(attend_weight, me, ORDER_ONE)
    output_mat = gather(output_weight, me, ORDER_ONE)
    inner_mat = gather(inner_weight, me, ORDER_TWO)
    outer_mat = gather(outer_weight, me, ORDER_TWO)

    doc_ends = jnp.cumsum(doc_lengths[0])
    near_at = group_index * GROUP + lax.iota(jnp.int32, GROUP)
    far_at = jnp.where(group_index == 0, GROUP, 64) + lax.iota(jnp.int32, REMOTE)
    row_at = jnp.concatenate([near_at, far_at])
    row_docs = jnp.sum((row_at[:, None] >= doc_ends[None, :]).astype(jnp.int32), axis=1)
    query_docs, key_docs = row_docs[:GROUP, None], row_docs[None, :]

    bias_row = jnp.concatenate([query_add, jnp.zeros((1, D), jnp.float32), value_add], axis=1)
    projected = (
        jnp.dot(token_rows, attend_mat, preferred_element_type=jnp.float32) + bias_row
    ).astype(jnp.bfloat16)
    attended, logs = attend_forward(query_docs, key_docs, projected)
    branch = jnp.dot(attended, output_mat, preferred_element_type=jnp.float32) + output_add
    first_out, first_normed, first_inverse = norm_forward(
        near.astype(jnp.float32) + branch, first_scale, first_offset
    )
    first_low = first_out.astype(jnp.bfloat16)
    pre_act = jnp.dot(first_low, inner_mat, preferred_element_type=jnp.float32) + inner_add
    cdf = 0.5 * (1.0 + lax.erf(pre_act * 0.5**0.5))
    activated = (pre_act * cdf).astype(jnp.bfloat16)
    gelu_slope = cdf + pre_act * jnp.exp(-0.5 * pre_act * pre_act) * 0.3989422804014327
    mlp_out = jnp.dot(activated, outer_mat, preferred_element_type=jnp.float32) + outer_add
    second_out, second_normed, second_inverse = norm_forward(
        first_out + mlp_out, second_scale, second_offset
    )
    layer_output = second_out.astype(jnp.bfloat16).reshape(1, GROUP, D)

    upstream = cotangent.reshape(GROUP, D).astype(jnp.float32)
    grad_second_scale = jnp.sum(upstream * second_normed, axis=0)
    grad_second_offset = jnp.sum(upstream, axis=0)
    grad_two = norm_backward(upstream, second_normed, second_inverse, second_scale)
    grad_mlp = grad_two.astype(jnp.bfloat16)
    grad_outer_add = jnp.sum(grad_mlp.astype(jnp.float32), axis=0)
    sum_outer_mat = scatter_sum(activated, grad_mlp, me, ORDER_TWO)
    grad_act = jnp.einsum("td,fd->tf", grad_mlp, outer_mat, preferred_element_type=jnp.float32)
    grad_pre = (grad_act * gelu_slope).astype(jnp.bfloat16)
    grad_inner_add = jnp.sum(grad_pre.astype(jnp.float32), axis=0)
    sum_inner_mat = scatter_sum(first_low, grad_pre, me, ORDER_TWO)
    grad_first = (
        jnp.einsum("tf,df->td", grad_pre, inner_mat, preferred_element_type=jnp.float32) + grad_two
    )
    grad_first_scale = jnp.sum(grad_first * first_normed, axis=0)
    grad_first_offset = jnp.sum(grad_first, axis=0)
    grad_hidden = norm_backward(grad_first, first_normed, first_inverse, first_scale)
    grad_branch = grad_hidden.astype(jnp.bfloat16)
    grad_output_add = jnp.sum(grad_branch.astype(jnp.float32), axis=0)
    sum_output_mat = scatter_sum(attended, grad_branch, me, ORDER_ONE)
    grad_attended = jnp.einsum(
        "te,de->td", grad_branch, output_mat, preferred_element_type=jnp.float32
    ).astype(jnp.bfloat16)
    grad_projected = attend_backward(query_docs, key_docs, projected, grad_attended, logs)
    sum_attend_mat = scatter_sum(token_rows, grad_projected, me, ORDER_ONE)
    wide_grad = grad_projected.astype(jnp.float32)
    grad_query_add = jnp.sum(wide_grad[:, :D], axis=0)
    grad_value_add = jnp.sum(wide_grad[:, 2 * D :], axis=0)
    row_grad = jnp.einsum(
        "te,de->td", grad_projected, attend_mat, preferred_element_type=jnp.float32
    )
    far_grad = lax.ppermute(
        row_grad[GROUP:].astype(jnp.bfloat16), "seq", [(0, 1), (1, 0)]
    ).astype(jnp.float32)
    filler = jnp.zeros((64, D), jnp.float32)
    far_grad = jnp.where(
        group_index == 0,
        jnp.concatenate([filler, far_grad]),
        jnp.concatenate([far_grad, filler]),
    )
    input_grad = grad_hidden + row_grad[:GROUP] + far_grad
    (
        sum_query_add,
        sum_value_add,
        sum_output_add,
        sum_first_scale,
        sum_first_offset,
        sum_inner_add,
        sum_outer_add,
        sum_second_scale,
        sum_second_offset,
    ) = scatter_small(
        [
            grad_query_add,
            grad_value_add,
            grad_output_add,
            grad_first_scale,
            grad_first_offset,
            grad_inner_add,
            grad_outer_add,
            grad_second_scale,
            grad_second_offset,
        ],
        me,
    )
    return (
        layer_output,
        input_grad.reshape(1, GROUP, D),
        sum_attend_mat,
        sum_query_add,
        sum_value_add,
        sum_output_mat,
        sum_output_add,
        sum_first_scale,
        sum_first_offset,
        sum_inner_mat,
        sum_inner_add,
        sum_outer_mat,
        sum_outer_add,
        sum_second_scale,
        sum_second_offset,
    )


def solution(mesh):
    sizes = (mesh.shape["seq"], mesh.shape["dp"])
    return jax.shard_map(
        fast_local if sizes == (2, 16) else general_local,
        mesh=mesh,
        in_specs=(
            P("dp", "seq", None),
            P("dp", "seq", None),
            P("dp", None),
            P(("seq", "dp"), None),
            P(("seq", "dp")),
            P(("seq", "dp")),
            P(("seq", "dp"), None),
            P(("seq", "dp")),
            P(("seq", "dp")),
            P(("seq", "dp")),
            P(("seq", "dp"), None),
            P(("seq", "dp")),
            P(("seq", "dp"), None),
            P(("seq", "dp")),
            P(("seq", "dp")),
            P(("seq", "dp")),
        ),
        out_specs=(
            P("dp", "seq", None),
            P("dp", "seq", None),
            P(("seq", "dp"), None),
            P(("seq", "dp")),
            P(("seq", "dp")),
            P(("seq", "dp"), None),
            P(("seq", "dp")),
            P(("seq", "dp")),
            P(("seq", "dp")),
            P(("seq", "dp"), None),
            P(("seq", "dp")),
            P(("seq", "dp"), None),
            P(("seq", "dp")),
            P(("seq", "dp")),
            P(("seq", "dp")),
        ),
        check_vma=False,
    )
```

```python
import functools

import jax
import jax.numpy as jnp
from jax import lax
from jax.experimental import pallas as pl
from jax.experimental.pallas import tpu as pltpu
from jax.sharding import PartitionSpec as P

D = 1024
HEADS = 16
HEAD = 64
GROUP = 256


epsilon = 1e-12
masked_score = -1e30


def norm_forward(value, gain, shift):
    mean_value = jnp.mean(value, axis=-1, keepdims=True)
    center = value - mean_value
    inverse = lax.rsqrt(jnp.mean(center * center, axis=-1, keepdims=True) + epsilon)
    normed = center * inverse
    return (normed * gain + shift, normed, inverse)


def norm_backward(upstream, normed, inverse, gain):
    scaled = upstream * gain
    first_mean = jnp.mean(scaled, axis=-1, keepdims=True)
    second_mean = jnp.mean(scaled * normed, axis=-1, keepdims=True)
    return inverse * (scaled - first_mean - normed * second_mean)


def exact_gelu(value):
    return jax.nn.gelu(value, approximate=False)


def pair_scores(query_pair, key_pair, allowed, factor):
    raw = (
        jnp.einsum("qhd,khd->hqk", query_pair, key_pair, preferred_element_type=jnp.float32)
        * factor
    )
    return jnp.where(allowed[None], raw, masked_score)


def column_pair(matrix, column_start, row_count):
    return lax.dynamic_slice_in_dim(matrix, column_start, 2 * HEAD, 1).reshape(row_count, 2, HEAD)


def general_local(
    tokens,
    cotangent,
    doc_lengths,
    attend_weight,
    query_bias,
    value_bias,
    output_weight,
    output_bias,
    first_gain,
    first_shift,
    inner_weight,
    inner_bias,
    outer_weight,
    outer_bias,
    second_gain,
    second_shift,
):
    (
        attend_mat,
        query_add,
        value_add,
        output_mat,
        output_add,
        first_scale,
        first_offset,
        inner_mat,
        inner_add,
        outer_mat,
        outer_add,
        second_scale,
        second_offset,
    ) = (
        lax.all_gather(attend_weight, ("seq", "dp"), axis=0, tiled=True),
        lax.all_gather(query_bias, ("seq", "dp"), axis=0, tiled=True),
        lax.all_gather(value_bias, ("seq", "dp"), axis=0, tiled=True),
        lax.all_gather(output_weight, ("seq", "dp"), axis=0, tiled=True),
        lax.all_gather(output_bias, ("seq", "dp"), axis=0, tiled=True),
        lax.all_gather(first_gain, ("seq", "dp"), axis=0, tiled=True),
        lax.all_gather(first_shift, ("seq", "dp"), axis=0, tiled=True),
        lax.all_gather(inner_weight, ("seq", "dp"), axis=0, tiled=True),
        lax.all_gather(inner_bias, ("seq", "dp"), axis=0, tiled=True),
        lax.all_gather(outer_weight, ("seq", "dp"), axis=0, tiled=True),
        lax.all_gather(outer_bias, ("seq", "dp"), axis=0, tiled=True),
        lax.all_gather(second_gain, ("seq", "dp"), axis=0, tiled=True),
        lax.all_gather(second_shift, ("seq", "dp"), axis=0, tiled=True),
    )
    token_rows = tokens.reshape(GROUP, D)
    key_total = GROUP * lax.axis_size("seq")
    group_index = lax.axis_index("seq")
    doc_ends = jnp.cumsum(doc_lengths[0])
    positions = lax.iota(jnp.int32, key_total)
    key_docs = jnp.sum((positions[:, None] >= doc_ends[None, :]).astype(jnp.int32), axis=1)
    query_docs = lax.dynamic_slice_in_dim(key_docs, group_index * GROUP, GROUP)
    allowed = query_docs[:, None] == key_docs[None, :]
    factor = HEAD ** (-0.5)
    pair_count = HEADS // 2
    bias_row = jnp.concatenate(
        [query_add.astype(jnp.float32), jnp.zeros((D,), jnp.float32), value_add.astype(jnp.float32)]
    )
    projected = jnp.dot(token_rows, attend_mat, preferred_element_type=jnp.float32) + bias_row
    queries = projected[:, :D].astype(jnp.bfloat16)
    keys_mine = projected[:, D : 2 * D].astype(jnp.bfloat16)
    values_mine = projected[:, 2 * D :].astype(jnp.bfloat16)
    keys_all, values_all = (
        lax.all_gather(keys_mine, "seq", axis=0, tiled=True),
        lax.all_gather(values_mine, "seq", axis=0, tiled=True),
    )

    def forward_pair(pair_index, state_tuple):
        mixed_heads, logsum = state_tuple
        column_start = pair_index * 2 * HEAD
        query_pair = column_pair(queries, column_start, GROUP)
        key_pair = column_pair(keys_all, column_start, key_total)
        value_pair = column_pair(values_all, column_start, key_total)
        scores = pair_scores(query_pair, key_pair, allowed, factor)
        row_peak = jnp.max(scores, axis=-1, keepdims=True)
        expo_terms = jnp.exp(scores - row_peak)
        row_total = jnp.sum(expo_terms, axis=-1, keepdims=True)
        weights = (expo_terms / row_total).astype(jnp.bfloat16)
        result = jnp.einsum(
            "hqk,khd->qhd", weights, value_pair, preferred_element_type=jnp.float32
        ).reshape(GROUP, 2 * HEAD)
        mixed_heads = lax.dynamic_update_slice_in_dim(mixed_heads, result, column_start, 1)
        logsum = lax.dynamic_update_slice_in_dim(
            logsum, row_peak + jnp.log(row_total), pair_index * 2, 0
        )
        return (mixed_heads, logsum)

    mixed_heads, logsum = lax.fori_loop(
        0,
        pair_count,
        forward_pair,
        (jnp.zeros((GROUP, D), jnp.float32), jnp.zeros((HEADS, GROUP, 1), jnp.float32)),
    )
    attended = mixed_heads.astype(jnp.bfloat16)
    branch = jnp.dot(attended, output_mat, preferred_element_type=jnp.float32) + output_add.astype(
        jnp.float32
    )
    first_out, first_normed, first_inverse = norm_forward(
        token_rows.astype(jnp.float32) + branch,
        first_scale.astype(jnp.float32),
        first_offset.astype(jnp.float32),
    )
    first_low = first_out.astype(jnp.bfloat16)
    pre_act = jnp.dot(first_low, inner_mat, preferred_element_type=jnp.float32) + inner_add.astype(
        jnp.float32
    )
    activated = exact_gelu(pre_act).astype(jnp.bfloat16)
    mlp_out = jnp.dot(activated, outer_mat, preferred_element_type=jnp.float32) + outer_add.astype(
        jnp.float32
    )
    second_out, second_normed, second_inverse = norm_forward(
        first_out + mlp_out, second_scale.astype(jnp.float32), second_offset.astype(jnp.float32)
    )
    layer_output = second_out.astype(jnp.bfloat16).reshape(1, GROUP, D)
    (
        attend_mat,
        query_add,
        value_add,
        output_mat,
        output_add,
        first_scale,
        first_offset,
        inner_mat,
        inner_add,
        outer_mat,
        outer_add,
        second_scale,
        second_offset,
    ) = (
        lax.all_gather(attend_weight, ("seq", "dp"), axis=0, tiled=True),
        lax.all_gather(query_bias, ("seq", "dp"), axis=0, tiled=True),
        lax.all_gather(value_bias, ("seq", "dp"), axis=0, tiled=True),
        lax.all_gather(output_weight, ("seq", "dp"), axis=0, tiled=True),
        lax.all_gather(output_bias, ("seq", "dp"), axis=0, tiled=True),
        lax.all_gather(first_gain, ("seq", "dp"), axis=0, tiled=True),
        lax.all_gather(first_shift, ("seq", "dp"), axis=0, tiled=True),
        lax.all_gather(inner_weight, ("seq", "dp"), axis=0, tiled=True),
        lax.all_gather(inner_bias, ("seq", "dp"), axis=0, tiled=True),
        lax.all_gather(outer_weight, ("seq", "dp"), axis=0, tiled=True),
        lax.all_gather(outer_bias, ("seq", "dp"), axis=0, tiled=True),
        lax.all_gather(second_gain, ("seq", "dp"), axis=0, tiled=True),
        lax.all_gather(second_shift, ("seq", "dp"), axis=0, tiled=True),
    )
    upstream = cotangent.reshape(GROUP, D).astype(jnp.float32)
    grad_second_scale = jnp.sum(upstream * second_normed, axis=0)
    grad_second_offset = jnp.sum(upstream, axis=0)
    grad_two = norm_backward(
        upstream, second_normed, second_inverse, second_scale.astype(jnp.float32)
    )
    grad_mlp = grad_two.astype(jnp.bfloat16)
    grad_outer_add = jnp.sum(grad_mlp.astype(jnp.float32), axis=0)
    grad_outer_mat = jnp.einsum(
        "tf,td->fd", activated, grad_mlp, preferred_element_type=jnp.float32
    )
    grad_act = jnp.einsum("td,fd->tf", grad_mlp, outer_mat, preferred_element_type=jnp.float32)
    unused_value, gelu_pull = jax.vjp(exact_gelu, pre_act)
    grad_pre = gelu_pull(grad_act)[0].astype(jnp.bfloat16)
    grad_inner_add = jnp.sum(grad_pre.astype(jnp.float32), axis=0)
    grad_inner_mat = jnp.einsum(
        "td,tf->df", first_low, grad_pre, preferred_element_type=jnp.float32
    )
    grad_first = (
        jnp.einsum("tf,df->td", grad_pre, inner_mat, preferred_element_type=jnp.float32) + grad_two
    )
    grad_first_scale = jnp.sum(grad_first * first_normed, axis=0)
    grad_first_offset = jnp.sum(grad_first, axis=0)
    grad_hidden = norm_backward(
        grad_first, first_normed, first_inverse, first_scale.astype(jnp.float32)
    )
    grad_branch = grad_hidden.astype(jnp.bfloat16)
    grad_output_add = jnp.sum(grad_branch.astype(jnp.float32), axis=0)
    grad_output_mat = jnp.einsum(
        "td,te->de", attended, grad_branch, preferred_element_type=jnp.float32
    )
    grad_attended = jnp.einsum(
        "te,de->td", grad_branch, output_mat, preferred_element_type=jnp.float32
    ).astype(jnp.bfloat16)

    def backward_pair(pair_index, state_tuple):
        grad_queries, grad_keys, grad_values = state_tuple
        column_start = pair_index * 2 * HEAD
        query_pair = column_pair(queries, column_start, GROUP)
        key_pair = column_pair(keys_all, column_start, key_total)
        value_pair = column_pair(values_all, column_start, key_total)
        upstream_pair = column_pair(grad_attended, column_start, GROUP)
        scores = pair_scores(query_pair, key_pair, allowed, factor)
        pair_logsum = lax.dynamic_slice_in_dim(logsum, pair_index * 2, 2, 0)
        pair_probs = jnp.exp(scores - pair_logsum)
        weights = pair_probs.astype(jnp.bfloat16)
        grad_weights = jnp.einsum(
            "qhd,khd->hqk", upstream_pair, value_pair, preferred_element_type=jnp.float32
        )
        row_dot = jnp.sum(grad_weights * pair_probs, axis=-1, keepdims=True)
        grad_scores = (pair_probs * (grad_weights - row_dot)).astype(jnp.bfloat16)
        query_part = (
            jnp.einsum("hqk,khd->qhd", grad_scores, key_pair, preferred_element_type=jnp.float32)
            * factor
        )
        key_part = (
            jnp.einsum("hqk,qhd->khd", grad_scores, query_pair, preferred_element_type=jnp.float32)
            * factor
        )
        value_part = jnp.einsum(
            "hqk,qhd->khd", weights, upstream_pair, preferred_element_type=jnp.float32
        )
        grad_queries = lax.dynamic_update_slice_in_dim(
            grad_queries, query_part.reshape(GROUP, 2 * HEAD), column_start, 1
        )
        grad_keys = lax.dynamic_update_slice_in_dim(
            grad_keys, key_part.reshape(key_total, 2 * HEAD), column_start, 1
        )
        grad_values = lax.dynamic_update_slice_in_dim(
            grad_values, value_part.reshape(key_total, 2 * HEAD), column_start, 1
        )
        return (grad_queries, grad_keys, grad_values)

    grad_queries, grad_keys, grad_values = lax.fori_loop(
        0,
        pair_count,
        backward_pair,
        (
            jnp.zeros((GROUP, D), jnp.float32),
            jnp.zeros((key_total, D), jnp.float32),
            jnp.zeros((key_total, D), jnp.float32),
        ),
    )
    key_share, value_share = (
        lax.psum_scatter(
            grad_keys.astype(jnp.bfloat16), "seq", scatter_dimension=0, tiled=True
        ).astype(jnp.float32),
        lax.psum_scatter(
            grad_values.astype(jnp.bfloat16), "seq", scatter_dimension=0, tiled=True
        ).astype(jnp.float32),
    )
    grad_projected = jnp.concatenate(
        [
            grad_queries.astype(jnp.bfloat16),
            key_share.astype(jnp.bfloat16),
            value_share.astype(jnp.bfloat16),
        ],
        axis=1,
    )
    grad_query_add = jnp.sum(grad_projected[:, :D].astype(jnp.float32), axis=0)
    grad_value_add = jnp.sum(grad_projected[:, 2 * D :].astype(jnp.float32), axis=0)
    grad_attend_mat = jnp.einsum(
        "td,te->de", token_rows, grad_projected, preferred_element_type=jnp.float32
    )
    input_grad = grad_hidden + jnp.einsum(
        "te,de->td", grad_projected, attend_mat, preferred_element_type=jnp.float32
    )
    (
        sum_attend_mat,
        sum_query_add,
        sum_value_add,
        sum_output_mat,
        sum_output_add,
        sum_first_scale,
        sum_first_offset,
        sum_inner_mat,
        sum_inner_add,
        sum_outer_mat,
        sum_outer_add,
        sum_second_scale,
        sum_second_offset,
    ) = (
        lax.psum_scatter(grad_attend_mat, ("seq", "dp"), scatter_dimension=0, tiled=True),
        lax.psum_scatter(grad_query_add, ("seq", "dp"), scatter_dimension=0, tiled=True),
        lax.psum_scatter(grad_value_add, ("seq", "dp"), scatter_dimension=0, tiled=True),
        lax.psum_scatter(grad_output_mat, ("seq", "dp"), scatter_dimension=0, tiled=True),
        lax.psum_scatter(grad_output_add, ("seq", "dp"), scatter_dimension=0, tiled=True),
        lax.psum_scatter(grad_first_scale, ("seq", "dp"), scatter_dimension=0, tiled=True),
        lax.psum_scatter(grad_first_offset, ("seq", "dp"), scatter_dimension=0, tiled=True),
        lax.psum_scatter(grad_inner_mat, ("seq", "dp"), scatter_dimension=0, tiled=True),
        lax.psum_scatter(grad_inner_add, ("seq", "dp"), scatter_dimension=0, tiled=True),
        lax.psum_scatter(grad_outer_mat, ("seq", "dp"), scatter_dimension=0, tiled=True),
        lax.psum_scatter(grad_outer_add, ("seq", "dp"), scatter_dimension=0, tiled=True),
        lax.psum_scatter(grad_second_scale, ("seq", "dp"), scatter_dimension=0, tiled=True),
        lax.psum_scatter(grad_second_offset, ("seq", "dp"), scatter_dimension=0, tiled=True),
    )
    return (
        layer_output,
        input_grad.reshape(1, GROUP, D),
        sum_attend_mat,
        sum_query_add,
        sum_value_add,
        sum_output_mat,
        sum_output_add,
        sum_first_scale,
        sum_first_offset,
        sum_inner_mat,
        sum_inner_add,
        sum_outer_mat,
        sum_outer_add,
        sum_second_scale,
        sum_second_offset,
    )


AXES = ("seq", "dp")
DEVICES = 32
WIDE = ((3, 4, 2, 1), (3, 1, 4, 2))
NARROW = ((3, 2, 1, 4), (3, 2, 1, 4))
HINT = pl.CostEstimate(flops=1, bytes_accessed=1, transcendentals=0)
REMOTE = GROUP - 64
ROWS = GROUP + REMOTE


def swap(value, masks):
    pairs = [(i, i ^ masks[i & 1]) for i in range(DEVICES)]
    return lax.ppermute(value, AXES, pairs)


def sync(movers, *values):
    state, values = lax.optimization_barrier(([mover.data for mover in movers], values))
    for mover, data in zip(movers, state):
        mover.data = data
    return values


def stage_masks(order, stage):
    return (1 << order[0][stage], 1 << order[1][stage])


def chip_mask(bits, place):
    return sum(1 << b for t, b in enumerate(bits) if place >> t & 1)


def join_body(cut, *refs):
    sems = refs[-1]
    ins, outs = refs[: len(refs) - 3], refs[len(refs) - 3 : -1]
    copies = []
    for number, out_ref in enumerate(outs):
        width = out_ref.shape[2]
        for side in range(2):
            source = ins[side] if cut else ins[2 * number + side]
            count = source.shape[0]
            if cut:
                source = source.at[:, :, pl.ds(number * cut, width)]
            target = out_ref.at[pl.ds(side * count, count)]
            copies.append(pltpu.make_async_copy(source, target, sems.at[2 * number + side]))
    for copy in copies:
        copy.start()
    for copy in copies:
        copy.wait()


def join(pieces, cut=0):
    count, rows, columns = pieces[0].shape
    widths = (cut, columns - cut) if cut else (columns, pieces[2].shape[2])
    return pl.pallas_call(
        functools.partial(join_body, cut),
        out_shape=[
            jax.ShapeDtypeStruct((2 * count, rows, width), jnp.bfloat16) for width in widths
        ],
        in_specs=[pl.BlockSpec(memory_space=pl.ANY)] * len(pieces),
        out_specs=[pl.BlockSpec(memory_space=pltpu.VMEM)] * 2,
        scratch_shapes=[pltpu.SemaphoreType.DMA((4,))],
        compiler_params=pltpu.CompilerParams(vmem_limit_bytes=16 * 2**20),
        cost_estimate=HINT,
    )(*pieces)


class Gather:
    def __init__(self, me, weights, cut, extra=()):
        self.me, self.cut, self.data = me, cut, {}
        core = me & 1
        both = []
        for side in (core, 1 - core):
            parts = []
            for weight in weights:
                half = weight.shape[1] // 2
                parts.append(lax.dynamic_slice(weight, (0, side * half), (weight.shape[0], half)))
            parts.extend(extra)
            both.append(parts[0] if len(parts) == 1 else jnp.concatenate(parts, axis=1))
        self.data["mine"] = both[0]
        self.data["arrived"] = swap(both[1], (1, 1))

    def depth(self):
        mine, other = self.data["mine"], self.data["arrived"]
        first = (self.me & 1) == 0
        both = jnp.concatenate([jnp.where(first, mine, other), jnp.where(first, other, mine)])
        both = both[None]
        self.data = {"held": both, "arrived": swap(both, stage_masks(WIDE, 0))}

    def step(self, stage):
        held, arrived = self.data["held"], self.data["arrived"]
        if stage == 1:
            held = join([held, arrived], self.cut)
        else:
            held = join([piece for pair in zip(held, arrived) for piece in pair])
        arrived = [
            swap(piece, stage_masks(order, stage)) for piece, order in zip(held, (WIDE, NARROW))
        ]
        self.data = {"held": held, "arrived": arrived}

    def share(self, name):
        self.data[name + " core"] = [swap(piece, (1, 1)) for piece in self.data[name]]

    def pieces(self):
        names = ("held", "arrived", "held core", "arrived core")
        return [piece for name in names for piece in self.data[name]]


def gather_matmul_body(routes, count, tile, me_ref, left_ref, *refs):
    piece_refs = refs[:8]
    out_refs, product_ref = refs[8 : 8 + count], refs[8 + count]
    mats, in_sems, out_sems = refs[9 + count : 9 + 2 * count], refs[-2], refs[-1]
    me = me_ref[0]
    rows = piece_refs[0].shape[1]
    copies = []
    for number, piece in enumerate(piece_refs):
        chunk, arrived, side = number % 2, number // 2 % 2, number // 4
        order = (WIDE, NARROW)[chunk]
        base = me ^ side
        core = base & 1
        for sub in range(8):
            place = 8 * arrived + sub
            mask = jnp.where(core == 0, chip_mask(order[0], place), chip_mask(order[1], place))
            chip = (base ^ mask) >> 1
            for start, width, mat, begin in routes(chunk, mats):
                half = mat.shape[1] // 2
                target = mat.at[
                    pl.ds(pl.multiple_of(chip * rows, rows), rows),
                    pl.ds(pl.multiple_of(core * half + begin, 128), width),
                ]
                source = piece.at[sub, :, pl.ds(start, width)]
                copies.append(pltpu.make_async_copy(source, target, in_sems.at[len(copies)]))
    for copy in copies:
        copy.start()
    kept = []
    per_side = len(copies) // 2
    for side in range(2):
        core = (me ^ side) & 1
        for copy in copies[side * per_side : (side + 1) * per_side]:
            copy.wait()
        for number, (mat, out_ref) in enumerate(zip(mats, out_refs)):
            half = mat.shape[1] // 2
            columns = pl.ds(pl.multiple_of(core * half, half), half)
            kept.append(
                pltpu.make_async_copy(
                    mat.at[:, columns], out_ref.at[:, columns], out_sems.at[2 * number + side]
                )
            )
            kept[-1].start()
        half = product_ref.shape[1] // 2

        def step(i, carry):
            columns = pl.ds(pl.multiple_of(core * half + i * tile, tile), tile)
            product_ref[:, columns] = jnp.dot(
                left_ref[...], mats[0][:, columns], preferred_element_type=jnp.float32
            )
            return carry

        lax.fori_loop(0, half // tile, step, 0)
    for copy in kept:
        copy.wait()


def gather_matmul(gather, routes, widths, left):
    pieces = gather.pieces()
    depth = pieces[0].shape[1] * DEVICES // 2
    mats = [(depth, width) for width in widths]
    return pl.pallas_call(
        functools.partial(gather_matmul_body, routes, len(widths), 512),
        out_shape=[jax.ShapeDtypeStruct(mat, jnp.bfloat16) for mat in mats]
        + [jax.ShapeDtypeStruct((left.shape[0], widths[0]), jnp.float32)],
        in_specs=[
            pl.BlockSpec(memory_space=pltpu.SMEM),
            pl.BlockSpec(memory_space=pltpu.VMEM),
        ]
        + [pl.BlockSpec(memory_space=pl.ANY)] * 8,
        out_specs=[pl.BlockSpec(memory_space=pl.ANY)] * len(widths)
        + [pl.BlockSpec(memory_space=pltpu.VMEM)],
        scratch_shapes=[pltpu.VMEM(mat, jnp.bfloat16) for mat in mats]
        + [pltpu.SemaphoreType.DMA((96,)), pltpu.SemaphoreType.DMA((2 * len(widths),))],
        compiler_params=pltpu.CompilerParams(vmem_limit_bytes=40 * 2**20),
        cost_estimate=HINT,
    )(gather.me.reshape(1), left, *pieces)


def whole_routes(cut, chunk, outs):
    half = outs[0].shape[1] // 2
    return ((0, (cut, half - cut)[chunk], outs[0], chunk * cut),)


def first_routes(chunk, outs):
    if chunk == 0:
        return ((0, outs[0].shape[1] // 2, outs[0], 0),)
    half = outs[1].shape[1] // 2
    return ((0, half, outs[1], 0), (half, outs[2].shape[1] // 2, outs[2], 0))


def place_of(bits, shard):
    place = shard & 1
    for t, b in enumerate(bits):
        place = place | ((shard >> b) & 1) << (t + 1)
    return place


def weight_grad_body(chunks, tile, me_ref, left_ref, right_ref, *refs):
    extra_refs = refs[: -2 * len(chunks)]
    outs = refs[-2 * len(chunks) :]
    me = me_ref[0]
    rows = outs[0].shape[1]
    half = right_ref.shape[1] // 2
    per_tile = tile // rows

    def step(i, carry):
        left = left_ref[:, pl.ds(pl.multiple_of(i * tile, tile), tile)]
        for side in (1, 0):
            base = me ^ side
            core = base & 1
            right = right_ref[:, pl.ds(pl.multiple_of(core * half, half), half)]
            product = lax.dot_general(
                left, right, (((0,), (0,)), ((), ())), preferred_element_type=jnp.float32
            ).astype(jnp.bfloat16)
            for sub in range(per_tile):
                number = i * per_tile + sub
                shard = number ^ base
                for which, (order, begin, width) in enumerate(chunks):
                    place = jnp.where(
                        core == 0, place_of(order[0], shard), place_of(order[1], shard)
                    )
                    out_ref = outs[2 * which + side]
                    out_ref[place, :, :width] = product[
                        sub * rows : (sub + 1) * rows, begin : begin + width
                    ]
                    for extra_ref in extra_refs:
                        out_ref[place, :, width:] = extra_ref[number]
        return carry

    lax.fori_loop(0, left_ref.shape[1] // tile, step, 0)


def weight_grad(left, right, me, chunks, extra=()):
    depth = left.shape[1]
    rows = depth // DEVICES
    more = sum(e.shape[2] for e in extra)
    shapes = [
        jax.ShapeDtypeStruct((DEVICES, rows, width + more), jnp.bfloat16)
        for _, _, width in chunks
        for _ in range(2)
    ]
    outs = pl.pallas_call(
        functools.partial(weight_grad_body, chunks, 256),
        out_shape=shapes,
        in_specs=[pl.BlockSpec(memory_space=pltpu.SMEM)]
        + [pl.BlockSpec(memory_space=pltpu.VMEM)] * (2 + len(extra)),
        out_specs=[pl.BlockSpec(memory_space=pltpu.VMEM)] * len(shapes),
        compiler_params=pltpu.CompilerParams(vmem_limit_bytes=24 * 2**20),
        cost_estimate=HINT,
    )(me.reshape(1), left, right, *extra)
    return [tuple(outs[i : i + 2]) for i in range(0, len(outs), 2)]


def add_low(one, two):
    return (one.astype(jnp.float32) + two.astype(jnp.float32)).astype(jnp.bfloat16)


def halve_body(held_low, held_high, low, high, keep_ref, send_ref):
    send_ref[...] = add_low(held_high[...], high[...])
    keep_ref[...] = add_low(held_low[...], low[...])


def halve(held, arrived):
    count, rows, columns = held.shape
    half = count // 2
    block = max(half // 4, 1)
    steps = half // block
    low = pl.BlockSpec((block, rows, columns), lambda i: (i, 0, 0))
    high = pl.BlockSpec((block, rows, columns), lambda i: (steps + i, 0, 0))
    shape = jax.ShapeDtypeStruct((half, rows, columns), jnp.bfloat16)
    keep, send = pl.pallas_call(
        halve_body,
        grid=(steps,),
        in_specs=[low, high, low, high],
        out_specs=[low, low],
        out_shape=[shape, shape],
        compiler_params=pltpu.CompilerParams(vmem_limit_bytes=16 * 2**20),
        cost_estimate=HINT,
    )(held, held, arrived, arrived)
    return keep, send


def first_norm_body(
    rows_ref, mixed_ref, matrix_ref, add_ref, gain_ref, shift_ref, low_ref, out_ref, normed_ref, inverse_ref
):
    branch = jnp.dot(mixed_ref[...], matrix_ref[...], preferred_element_type=jnp.float32)
    out, normed, inverse = norm_forward(
        rows_ref[...].astype(jnp.float32) + (branch + add_ref[...]), gain_ref[...], shift_ref[...]
    )
    low_ref[...] = out.astype(jnp.bfloat16)
    out_ref[...] = out
    normed_ref[...] = normed
    inverse_ref[...] = inverse


def first_norm(rows, mixed, matrix, add, gain, shift):
    block = 128
    tall = pl.BlockSpec((block, D), lambda i: (i, 0))
    whole = pl.BlockSpec((1, D), lambda i: (0, 0))
    return pl.pallas_call(
        first_norm_body,
        grid=(GROUP // block,),
        in_specs=[tall, tall, pl.BlockSpec((D, D), lambda i: (0, 0)), whole, whole, whole],
        out_specs=[tall, tall, tall, pl.BlockSpec((block, 1), lambda i: (i, 0))],
        out_shape=[
            jax.ShapeDtypeStruct((GROUP, D), jnp.bfloat16),
            jax.ShapeDtypeStruct((GROUP, D), jnp.float32),
            jax.ShapeDtypeStruct((GROUP, D), jnp.float32),
            jax.ShapeDtypeStruct((GROUP, 1), jnp.float32),
        ],
        compiler_params=pltpu.CompilerParams(vmem_limit_bytes=20 * 2**20),
        cost_estimate=HINT,
    )(rows, mixed, matrix, add, gain, shift)


def rows_back_body(grad_ref, matrix_ref, near_ref, far_ref):
    product = lax.dot_general(
        grad_ref[...],
        matrix_ref[...],
        (((1,), (1,)), ((), ())),
        preferred_element_type=jnp.float32,
    )
    near_ref[...] = product[:GROUP]
    far_ref[...] = product[GROUP:].astype(jnp.bfloat16)


def rows_back(grad, matrix):
    return pl.pallas_call(
        rows_back_body,
        grid=(4,),
        in_specs=[
            pl.BlockSpec((ROWS, 3 * D), lambda i: (0, 0)),
            pl.BlockSpec((D // 4, 3 * D), lambda i: (i, 0)),
        ],
        out_specs=[
            pl.BlockSpec((GROUP, D // 4), lambda i: (0, i)),
            pl.BlockSpec((REMOTE, D // 4), lambda i: (0, i)),
        ],
        out_shape=[
            jax.ShapeDtypeStruct((GROUP, D), jnp.float32),
            jax.ShapeDtypeStruct((REMOTE, D), jnp.bfloat16),
        ],
        compiler_params=pltpu.CompilerParams(vmem_limit_bytes=16 * 2**20),
        cost_estimate=HINT,
    )(grad, matrix)


def cut_grads(me, left, right, cut):
    half = right.shape[1] // 2
    return weight_grad(left, right, me, ((WIDE, 0, cut), (NARROW, cut, half - cut)))


class Scatter:
    def __init__(self, me, grads):
        self.me, self.stage = me, 4
        self.data = {"held": [keep for keep, _ in grads], "send": [send for _, send in grads]}

    def begin(self):
        self.data["arrived"] = [swap(piece, (1, 1)) for piece in self.data.pop("send")]

    def step(self):
        self.stage -= 1
        sums = [halve(*pair) for pair in zip(self.data["held"], self.data["arrived"])]
        held, send = [keep for keep, _ in sums], [other for _, other in sums]
        if self.stage == 0:
            held, send = jnp.concatenate(held, axis=2), jnp.concatenate(send, axis=2)
            arrived = swap(send, stage_masks(WIDE, 0))
        else:
            arrived = [
                swap(piece, stage_masks(order, self.stage))
                for piece, order in zip(send, (WIDE, NARROW))
            ]
        self.data = {"held": held, "arrived": arrived}

    def near(self):
        held, arrived = self.data["held"], self.data["arrived"]
        send = add_low(held[1], arrived[1])
        held = held[0].astype(jnp.float32) + arrived[0].astype(jnp.float32)
        self.data = {"held": held, "arrived": swap(send, (1, 1))}

    def result(self):
        held, arrived = self.data["held"], self.data["arrived"].astype(jnp.float32)
        first = (self.me & 1) == 0
        return jnp.where(first, held, arrived), jnp.where(first, arrived, held)


def attend_forward_body(query_docs, key_docs, query_ref, key_ref, value_ref, mixed_ref, log_ref):
    allowed = query_docs[...] == key_docs[...]
    queries, keys, values = query_ref[...], key_ref[...], value_ref[...]
    lanes = lax.broadcasted_iota(jnp.int32, queries.shape, 1)
    results, logs = [], []
    for head in range(2):
        chosen = (lanes < HEAD) if head == 0 else (lanes >= HEAD)
        raw = lax.dot_general(
            jnp.where(chosen, queries, jnp.zeros_like(queries)),
            keys,
            (((1,), (1,)), ((), ())),
            preferred_element_type=jnp.float32,
        )
        scores = jnp.where(allowed, raw * HEAD**-0.5, masked_score)
        peak = jnp.max(scores, axis=-1, keepdims=True)
        terms = jnp.exp(scores - peak)
        total = jnp.sum(terms, axis=-1, keepdims=True)
        weights = (terms * (1.0 / total)).astype(jnp.bfloat16)
        results.append(jnp.dot(weights, values, preferred_element_type=jnp.float32))
        logs.append(peak + jnp.log(total))
    mixed_ref[...] = jnp.where(lanes < HEAD, results[0], results[1]).astype(jnp.bfloat16)
    log_ref[0] = jnp.where(lanes < HEAD, logs[0], logs[1])


def attend_forward(query_docs, key_docs, projected):
    pairs = HEADS // 2
    return pl.pallas_call(
        attend_forward_body,
        grid=(pairs,),
        in_specs=[
            pl.BlockSpec((GROUP, 1), lambda i: (0, 0)),
            pl.BlockSpec((1, ROWS), lambda i: (0, 0)),
            pl.BlockSpec((GROUP, 128), lambda i: (0, i)),
            pl.BlockSpec((ROWS, 128), lambda i: (0, pairs + i)),
            pl.BlockSpec((ROWS, 128), lambda i: (0, 2 * pairs + i)),
        ],
        out_specs=[
            pl.BlockSpec((GROUP, 128), lambda i: (0, i)),
            pl.BlockSpec((1, GROUP, 128), lambda i: (i, 0, 0)),
        ],
        out_shape=[
            jax.ShapeDtypeStruct((GROUP, D), jnp.bfloat16),
            jax.ShapeDtypeStruct((pairs, GROUP, 128), jnp.float32),
        ],
        compiler_params=pltpu.CompilerParams(vmem_limit_bytes=16 * 2**20),
        cost_estimate=HINT,
    )(query_docs, key_docs, projected, projected, projected)


def attend_backward_body(
    query_docs, key_docs, query_ref, key_ref, value_ref, upstream_ref, log_ref, grad_ref, sum_ref
):
    pair = pl.program_id(0)
    allowed = query_docs[...] == key_docs[...]
    queries, keys, values = query_ref[...], key_ref[...], value_ref[...]
    upstream = upstream_ref[...]
    lanes = lax.broadcasted_iota(jnp.int32, queries.shape, 1)
    zeros = jnp.zeros_like(queries)
    across = (((1,), (1,)), ((), ()))
    down = (((0,), (0,)), ((), ()))
    query_parts, key_parts, value_parts = [], [], []
    for head in range(2):
        chosen = (lanes < HEAD) if head == 0 else (lanes >= HEAD)
        raw = lax.dot_general(
            jnp.where(chosen, queries, zeros), keys, across, preferred_element_type=jnp.float32
        )
        scores = jnp.where(allowed, raw * HEAD**-0.5, masked_score)
        probs = jnp.exp(scores - log_ref[0, :, head * HEAD : head * HEAD + 1])
        grad_weights = lax.dot_general(
            jnp.where(chosen, upstream, zeros), values, across, preferred_element_type=jnp.float32
        )
        row_dot = jnp.sum(grad_weights * probs, axis=-1, keepdims=True)
        grad_scores = (probs * (grad_weights - row_dot)).astype(jnp.bfloat16)
        weights = probs.astype(jnp.bfloat16)
        query_parts.append(jnp.dot(grad_scores, keys, preferred_element_type=jnp.float32))
        key_parts.append(
            lax.dot_general(grad_scores, queries, down, preferred_element_type=jnp.float32)
        )
        value_parts.append(
            lax.dot_general(weights, upstream, down, preferred_element_type=jnp.float32)
        )
    wide = lax.broadcasted_iota(jnp.int32, keys.shape, 1) < HEAD
    grad_queries = jnp.where(lanes < HEAD, query_parts[0], query_parts[1]) * HEAD**-0.5
    grad_keys = jnp.where(wide, key_parts[0], key_parts[1]) * HEAD**-0.5
    grad_values = jnp.where(wide, value_parts[0], value_parts[1])
    column = pl.multiple_of(pair * 128, 128)
    grad_ref[:GROUP, pl.ds(column, 128)] = grad_queries.astype(jnp.bfloat16)
    grad_ref[GROUP:, pl.ds(column, 128)] = jnp.zeros((REMOTE, 128), jnp.bfloat16)
    grad_ref[:, pl.ds(pl.multiple_of(D + pair * 128, 128), 128)] = grad_keys.astype(jnp.bfloat16)
    grad_values = grad_values.astype(jnp.bfloat16)
    grad_ref[:, pl.ds(pl.multiple_of(2 * D + pair * 128, 128), 128)] = grad_values
    low = grad_queries.astype(jnp.bfloat16).astype(jnp.float32)
    sum_ref[0, :, pl.ds(column, 128)] = jnp.sum(low, axis=0, keepdims=True)
    low = grad_values.astype(jnp.float32)
    sum_ref[1, :, pl.ds(column, 128)] = jnp.sum(low, axis=0, keepdims=True)


def attend_backward(query_docs, key_docs, projected, upstream, logs):
    pairs = HEADS // 2
    return pl.pallas_call(
        attend_backward_body,
        grid=(pairs,),
        in_specs=[
            pl.BlockSpec((GROUP, 1), lambda i: (0, 0)),
            pl.BlockSpec((1, ROWS), lambda i: (0, 0)),
            pl.BlockSpec((GROUP, 128), lambda i: (0, i)),
            pl.BlockSpec((ROWS, 128), lambda i: (0, pairs + i)),
            pl.BlockSpec((ROWS, 128), lambda i: (0, 2 * pairs + i)),
            pl.BlockSpec((GROUP, 128), lambda i: (0, i)),
            pl.BlockSpec((1, GROUP, 128), lambda i: (i, 0, 0)),
        ],
        out_specs=[
            pl.BlockSpec((ROWS, 3 * D), lambda i: (0, 0)),
            pl.BlockSpec((2, 1, D), lambda i: (0, 0, 0)),
        ],
        out_shape=[
            jax.ShapeDtypeStruct((ROWS, 3 * D), jnp.bfloat16),
            jax.ShapeDtypeStruct((2, 1, D), jnp.float32),
        ],
        compiler_params=pltpu.CompilerParams(vmem_limit_bytes=16 * 2**20),
        cost_estimate=HINT,
    )(query_docs, key_docs, projected, projected, projected, upstream, logs)


def pack_shard(vectors):
    rows = jnp.concatenate([vector.reshape(-1, 32) for vector in vectors])
    return jnp.pad(rows, ((0, 32 - rows.shape[0]), (0, 96)))


def unpack_shards(packed):
    rows = packed.reshape(DEVICES, 32, 256)[:, :12, :32].astype(jnp.float32)
    short = rows[:, :8].transpose(1, 0, 2).reshape(8, 1, D)
    return [short[i] for i in range(8)] + [rows[:, 8:].reshape(1, 4 * D)]


def pack_grads(short, long):
    rows = jnp.concatenate([vector.reshape(1, 8, 128) for vector in short])
    rows = jnp.repeat(rows.transpose(1, 0, 2), 4, axis=0)
    rows = jnp.concatenate([rows, long.reshape(DEVICES, 1, 128)], axis=1)
    return jnp.pad(rows, ((0, 0), (0, 23), (0, 0))).astype(jnp.bfloat16)


def fast_local(
    tokens,
    cotangent,
    doc_lengths,
    attend_weight,
    query_bias,
    value_bias,
    output_weight,
    output_bias,
    first_gain,
    first_shift,
    inner_weight,
    inner_bias,
    outer_weight,
    outer_bias,
    second_gain,
    second_shift,
):
    me = lax.axis_index(AXES)
    group_index = me >> 4
    small_shard = pack_shard(
        [
            query_bias,
            value_bias,
            output_bias,
            first_gain,
            first_shift,
            outer_bias,
            second_gain,
            second_shift,
            inner_bias,
        ]
    )
    attend_cut, inner_cut, outer_cut = 3 * D // 2, 1408, 384
    one = Gather(me, (attend_weight, output_weight), attend_cut, (small_shard,))
    two = Gather(me, (inner_weight,), inner_cut)
    three = Gather(me, (outer_weight,), outer_cut)
    movers = (one, two, three)
    near = tokens.reshape(GROUP, D)
    far = lax.dynamic_slice(near, (64 * (1 - group_index), 0), (REMOTE, D))
    sync((one,))

    one.depth()
    far = lax.ppermute(far, "seq", [(0, 1), (1, 0)])
    doc_ends = jnp.cumsum(doc_lengths[0])
    near_at = group_index * GROUP + lax.iota(jnp.int32, GROUP)
    far_at = jnp.where(group_index == 0, GROUP, 64) + lax.iota(jnp.int32, REMOTE)
    row_at = jnp.concatenate([near_at, far_at])
    row_docs = jnp.sum((row_at[:, None] >= doc_ends[None, :]).astype(jnp.int32), axis=1)
    query_docs, key_docs = row_docs[:GROUP, None], row_docs[None, :]
    query_docs, key_docs, far = sync(movers, query_docs, key_docs, far)

    one.step(1)
    two.depth()
    token_rows = jnp.concatenate([near, far])
    (token_rows,) = sync((one, two), token_rows)

    one.step(2)
    three.depth()
    sync(movers)

    one.step(3)
    two.step(1)
    sync((one, two))

    one.share("held")
    one.share("arrived")
    sync((one,))

    two.step(2)
    three.step(1)
    attend_mat, output_mat, small_all, projected = gather_matmul(
        one, first_routes, (3 * D, D, 256), token_rows
    )
    (
        query_add,
        value_add,
        output_add,
        first_scale,
        first_offset,
        outer_add,
        second_scale,
        second_offset,
        inner_add,
    ) = unpack_shards(small_all)
    bias_row = jnp.concatenate([query_add, jnp.zeros((1, D), jnp.float32), value_add], axis=1)
    projected = (projected + bias_row).astype(jnp.bfloat16)
    (projected,) = sync((two, three), projected)

    two.step(3)
    three.step(2)
    attended, logs = attend_forward(query_docs, key_docs, projected)
    first_low, first_out, first_normed, first_inverse = first_norm(
        near, attended, output_mat, output_add, first_scale, first_offset
    )
    first_out, first_normed, first_inverse, first_low = sync(
        (two, three), first_out, first_normed, first_inverse, first_low
    )

    two.share("held")
    two.share("arrived")
    sync((two,))

    three.step(3)
    inner_mat, pre_act = gather_matmul(
        two, functools.partial(whole_routes, inner_cut), (4 * D,), first_low
    )
    pre_act = pre_act + inner_add
    cdf = 0.5 * (1.0 + lax.erf(pre_act * 0.5**0.5))
    gelu_slope = cdf + pre_act * jnp.exp(-0.5 * pre_act * pre_act) * 0.3989422804014327
    activated = (pre_act * cdf).astype(jnp.bfloat16)
    activated, gelu_slope = sync((three,), activated, gelu_slope)

    three.share("held")
    three.share("arrived")
    outer_mat, mlp_out = gather_matmul(
        three, functools.partial(whole_routes, outer_cut), (D,), activated
    )
    mlp_out = mlp_out + outer_add
    second_out, second_normed, second_inverse = norm_forward(
        first_out + mlp_out, second_scale, second_offset
    )
    layer_output = second_out.astype(jnp.bfloat16).reshape(1, GROUP, D)
    upstream = cotangent.reshape(GROUP, D).astype(jnp.float32)
    grad_two = norm_backward(upstream, second_normed, second_inverse, second_scale)
    grad_mlp = grad_two.astype(jnp.bfloat16)
    outer = Scatter(me, cut_grads(me, activated, grad_mlp, outer_cut))
    grad_mlp, grad_two, second_normed = sync((outer,), grad_mlp, grad_two, second_normed)

    outer.begin()
    grad_act = jnp.einsum("td,fd->tf", grad_mlp, outer_mat, preferred_element_type=jnp.float32)
    grad_pre = (grad_act * gelu_slope).astype(jnp.bfloat16)
    inner_sum = jnp.sum(grad_pre.astype(jnp.float32), axis=0)
    grad_pre, inner_sum = sync((outer,), grad_pre, inner_sum)

    outer.step()
    inner = Scatter(me, cut_grads(me, first_low, grad_pre, inner_cut))
    second_sums = (
        jnp.sum(grad_mlp.astype(jnp.float32), axis=0),
        jnp.sum(upstream * second_normed, axis=0),
        jnp.sum(upstream, axis=0),
    )
    grad_first = (
        jnp.einsum("tf,df->td", grad_pre, inner_mat, preferred_element_type=jnp.float32) + grad_two
    )
    grad_hidden = norm_backward(grad_first, first_normed, first_inverse, first_scale)
    grad_branch = grad_hidden.astype(jnp.bfloat16)
    first_sums = (
        jnp.sum(grad_branch.astype(jnp.float32), axis=0),
        jnp.sum(grad_first * first_normed, axis=0),
        jnp.sum(grad_first, axis=0),
    )
    grad_attended = jnp.einsum(
        "te,de->td", grad_branch, output_mat, preferred_element_type=jnp.float32
    ).astype(jnp.bfloat16)
    first_sums, second_sums, grad_hidden, grad_branch, grad_attended = sync(
        (outer, inner), first_sums, second_sums, grad_hidden, grad_branch, grad_attended
    )

    inner.begin()
    outer.step()
    grad_projected, row_sums = attend_backward(
        query_docs, key_docs, projected, grad_attended, logs
    )
    grad_projected, row_sums = sync((outer, inner), grad_projected, row_sums)

    inner.step()
    outer.step()
    small = pack_grads([row_sums[0, 0], row_sums[1, 0], *first_sums, *second_sums], inner_sum)
    first = Scatter(
        me,
        weight_grad(token_rows, grad_projected, me, ((WIDE, 0, attend_cut),))
        + weight_grad(attended, grad_branch, me, ((NARROW, 0, D // 2),), (small,)),
    )
    movers = (outer, inner, first)
    sync(movers)

    first.begin()
    inner.step()
    outer.step()
    sync(movers)

    first.step()
    inner.step()
    outer.near()
    sync(movers)

    first.step()
    inner.step()
    sum_outer_mat = jnp.concatenate(outer.result(), axis=1)
    row_grad, far_grad = rows_back(grad_projected, attend_mat)
    sum_outer_mat, row_grad, far_grad = sync((inner, first), sum_outer_mat, row_grad, far_grad)

    first.step()
    inner.near()
    far_grad = lax.ppermute(far_grad, "seq", [(0, 1), (1, 0)])
    (far_grad,) = sync((inner, first), far_grad)

    first.step()
    sum_inner_mat = jnp.concatenate(inner.result(), axis=1)
    (sum_inner_mat,) = sync((first,), sum_inner_mat)

    first.near()
    filler = jnp.zeros((64, D), jnp.float32)
    far_grad = far_grad.astype(jnp.float32)
    far_grad = jnp.where(
        group_index == 0,
        jnp.concatenate([filler, far_grad]),
        jnp.concatenate([far_grad, filler]),
    )
    input_grad = grad_hidden + row_grad + far_grad
    halves = first.result()
    output_end = attend_cut + D // 2
    sum_attend_mat = jnp.concatenate([half[:, :attend_cut] for half in halves], axis=1)
    sum_output_mat = jnp.concatenate([half[:, attend_cut:output_end] for half in halves], axis=1)
    small_rows = halves[0][:, output_end:]
    own = lax.dynamic_slice(small_rows, (0, 32 * (me & 3)), (8, 32))
    (
        sum_query_add,
        sum_value_add,
        sum_output_add,
        sum_first_scale,
        sum_first_offset,
        sum_outer_add,
        sum_second_scale,
        sum_second_offset,
    ) = (own[i] for i in range(8))
    sum_inner_add = small_rows[8]
    return (
        layer_output,
        input_grad.reshape(1, GROUP, D),
        sum_attend_mat,
        sum_query_add,
        sum_value_add,
        sum_output_mat,
        sum_output_add,
        sum_first_scale,
        sum_first_offset,
        sum_inner_mat,
        sum_inner_add,
        sum_outer_mat,
        sum_outer_add,
        sum_second_scale,
        sum_second_offset,
    )


def solution(mesh):
    sizes = (mesh.shape["seq"], mesh.shape["dp"])
    return jax.shard_map(
        fast_local if sizes == (2, 16) else general_local,
        mesh=mesh,
        in_specs=(
            P("dp", "seq", None),
            P("dp", "seq", None),
            P("dp", None),
            P(("seq", "dp"), None),
            P(("seq", "dp")),
            P(("seq", "dp")),
            P(("seq", "dp"), None),
            P(("seq", "dp")),
            P(("seq", "dp")),
            P(("seq", "dp")),
            P(("seq", "dp"), None),
            P(("seq", "dp")),
            P(("seq", "dp"), None),
            P(("seq", "dp")),
            P(("seq", "dp")),
            P(("seq", "dp")),
        ),
        out_specs=(
            P("dp", "seq", None),
            P("dp", "seq", None),
            P(("seq", "dp"), None),
            P(("seq", "dp")),
            P(("seq", "dp")),
            P(("seq", "dp"), None),
            P(("seq", "dp")),
            P(("seq", "dp")),
            P(("seq", "dp")),
            P(("seq", "dp"), None),
            P(("seq", "dp")),
            P(("seq", "dp"), None),
            P(("seq", "dp")),
            P(("seq", "dp")),
            P(("seq", "dp")),
        ),
        check_vma=False,
    )
```

```python
import functools

import jax
import jax.numpy as jnp
from jax import lax
from jax.experimental import pallas as pl
from jax.experimental.pallas import tpu as pltpu
from jax.sharding import PartitionSpec as P

D = 1024
HEADS = 16
HEAD = 64
GROUP = 256


epsilon = 1e-12
masked_score = -1e30


def norm_forward(value, gain, shift):
    mean_value = jnp.mean(value, axis=-1, keepdims=True)
    center = value - mean_value
    inverse = lax.rsqrt(jnp.mean(center * center, axis=-1, keepdims=True) + epsilon)
    normed = center * inverse
    return (normed * gain + shift, normed, inverse)


def norm_backward(upstream, normed, inverse, gain):
    scaled = upstream * gain
    first_mean = jnp.mean(scaled, axis=-1, keepdims=True)
    second_mean = jnp.mean(scaled * normed, axis=-1, keepdims=True)
    return inverse * (scaled - first_mean - normed * second_mean)


def exact_gelu(value):
    return jax.nn.gelu(value, approximate=False)


def pair_scores(query_pair, key_pair, allowed, factor):
    raw = (
        jnp.einsum("qhd,khd->hqk", query_pair, key_pair, preferred_element_type=jnp.float32)
        * factor
    )
    return jnp.where(allowed[None], raw, masked_score)


def column_pair(matrix, column_start, row_count):
    return lax.dynamic_slice_in_dim(matrix, column_start, 2 * HEAD, 1).reshape(row_count, 2, HEAD)


def general_local(
    tokens,
    cotangent,
    doc_lengths,
    attend_weight,
    query_bias,
    value_bias,
    output_weight,
    output_bias,
    first_gain,
    first_shift,
    inner_weight,
    inner_bias,
    outer_weight,
    outer_bias,
    second_gain,
    second_shift,
):
    (
        attend_mat,
        query_add,
        value_add,
        output_mat,
        output_add,
        first_scale,
        first_offset,
        inner_mat,
        inner_add,
        outer_mat,
        outer_add,
        second_scale,
        second_offset,
    ) = (
        lax.all_gather(attend_weight, ("seq", "dp"), axis=0, tiled=True),
        lax.all_gather(query_bias, ("seq", "dp"), axis=0, tiled=True),
        lax.all_gather(value_bias, ("seq", "dp"), axis=0, tiled=True),
        lax.all_gather(output_weight, ("seq", "dp"), axis=0, tiled=True),
        lax.all_gather(output_bias, ("seq", "dp"), axis=0, tiled=True),
        lax.all_gather(first_gain, ("seq", "dp"), axis=0, tiled=True),
        lax.all_gather(first_shift, ("seq", "dp"), axis=0, tiled=True),
        lax.all_gather(inner_weight, ("seq", "dp"), axis=0, tiled=True),
        lax.all_gather(inner_bias, ("seq", "dp"), axis=0, tiled=True),
        lax.all_gather(outer_weight, ("seq", "dp"), axis=0, tiled=True),
        lax.all_gather(outer_bias, ("seq", "dp"), axis=0, tiled=True),
        lax.all_gather(second_gain, ("seq", "dp"), axis=0, tiled=True),
        lax.all_gather(second_shift, ("seq", "dp"), axis=0, tiled=True),
    )
    token_rows = tokens.reshape(GROUP, D)
    key_total = GROUP * lax.axis_size("seq")
    group_index = lax.axis_index("seq")
    doc_ends = jnp.cumsum(doc_lengths[0])
    positions = lax.iota(jnp.int32, key_total)
    key_docs = jnp.sum((positions[:, None] >= doc_ends[None, :]).astype(jnp.int32), axis=1)
    query_docs = lax.dynamic_slice_in_dim(key_docs, group_index * GROUP, GROUP)
    allowed = query_docs[:, None] == key_docs[None, :]
    factor = HEAD ** (-0.5)
    pair_count = HEADS // 2
    bias_row = jnp.concatenate(
        [query_add.astype(jnp.float32), jnp.zeros((D,), jnp.float32), value_add.astype(jnp.float32)]
    )
    projected = jnp.dot(token_rows, attend_mat, preferred_element_type=jnp.float32) + bias_row
    queries = projected[:, :D].astype(jnp.bfloat16)
    keys_mine = projected[:, D : 2 * D].astype(jnp.bfloat16)
    values_mine = projected[:, 2 * D :].astype(jnp.bfloat16)
    keys_all, values_all = (
        lax.all_gather(keys_mine, "seq", axis=0, tiled=True),
        lax.all_gather(values_mine, "seq", axis=0, tiled=True),
    )

    def forward_pair(pair_index, state_tuple):
        mixed_heads, logsum = state_tuple
        column_start = pair_index * 2 * HEAD
        query_pair = column_pair(queries, column_start, GROUP)
        key_pair = column_pair(keys_all, column_start, key_total)
        value_pair = column_pair(values_all, column_start, key_total)
        scores = pair_scores(query_pair, key_pair, allowed, factor)
        row_peak = jnp.max(scores, axis=-1, keepdims=True)
        expo_terms = jnp.exp(scores - row_peak)
        row_total = jnp.sum(expo_terms, axis=-1, keepdims=True)
        weights = (expo_terms / row_total).astype(jnp.bfloat16)
        result = jnp.einsum(
            "hqk,khd->qhd", weights, value_pair, preferred_element_type=jnp.float32
        ).reshape(GROUP, 2 * HEAD)
        mixed_heads = lax.dynamic_update_slice_in_dim(mixed_heads, result, column_start, 1)
        logsum = lax.dynamic_update_slice_in_dim(
            logsum, row_peak + jnp.log(row_total), pair_index * 2, 0
        )
        return (mixed_heads, logsum)

    mixed_heads, logsum = lax.fori_loop(
        0,
        pair_count,
        forward_pair,
        (jnp.zeros((GROUP, D), jnp.float32), jnp.zeros((HEADS, GROUP, 1), jnp.float32)),
    )
    attended = mixed_heads.astype(jnp.bfloat16)
    branch = jnp.dot(attended, output_mat, preferred_element_type=jnp.float32) + output_add.astype(
        jnp.float32
    )
    first_out, first_normed, first_inverse = norm_forward(
        token_rows.astype(jnp.float32) + branch,
        first_scale.astype(jnp.float32),
        first_offset.astype(jnp.float32),
    )
    first_low = first_out.astype(jnp.bfloat16)
    pre_act = jnp.dot(first_low, inner_mat, preferred_element_type=jnp.float32) + inner_add.astype(
        jnp.float32
    )
    activated = exact_gelu(pre_act).astype(jnp.bfloat16)
    mlp_out = jnp.dot(activated, outer_mat, preferred_element_type=jnp.float32) + outer_add.astype(
        jnp.float32
    )
    second_out, second_normed, second_inverse = norm_forward(
        first_out + mlp_out, second_scale.astype(jnp.float32), second_offset.astype(jnp.float32)
    )
    layer_output = second_out.astype(jnp.bfloat16).reshape(1, GROUP, D)
    (
        attend_mat,
        query_add,
        value_add,
        output_mat,
        output_add,
        first_scale,
        first_offset,
        inner_mat,
        inner_add,
        outer_mat,
        outer_add,
        second_scale,
        second_offset,
    ) = (
        lax.all_gather(attend_weight, ("seq", "dp"), axis=0, tiled=True),
        lax.all_gather(query_bias, ("seq", "dp"), axis=0, tiled=True),
        lax.all_gather(value_bias, ("seq", "dp"), axis=0, tiled=True),
        lax.all_gather(output_weight, ("seq", "dp"), axis=0, tiled=True),
        lax.all_gather(output_bias, ("seq", "dp"), axis=0, tiled=True),
        lax.all_gather(first_gain, ("seq", "dp"), axis=0, tiled=True),
        lax.all_gather(first_shift, ("seq", "dp"), axis=0, tiled=True),
        lax.all_gather(inner_weight, ("seq", "dp"), axis=0, tiled=True),
        lax.all_gather(inner_bias, ("seq", "dp"), axis=0, tiled=True),
        lax.all_gather(outer_weight, ("seq", "dp"), axis=0, tiled=True),
        lax.all_gather(outer_bias, ("seq", "dp"), axis=0, tiled=True),
        lax.all_gather(second_gain, ("seq", "dp"), axis=0, tiled=True),
        lax.all_gather(second_shift, ("seq", "dp"), axis=0, tiled=True),
    )
    upstream = cotangent.reshape(GROUP, D).astype(jnp.float32)
    grad_second_scale = jnp.sum(upstream * second_normed, axis=0)
    grad_second_offset = jnp.sum(upstream, axis=0)
    grad_two = norm_backward(
        upstream, second_normed, second_inverse, second_scale.astype(jnp.float32)
    )
    grad_mlp = grad_two.astype(jnp.bfloat16)
    grad_outer_add = jnp.sum(grad_mlp.astype(jnp.float32), axis=0)
    grad_outer_mat = jnp.einsum(
        "tf,td->fd", activated, grad_mlp, preferred_element_type=jnp.float32
    )
    grad_act = jnp.einsum("td,fd->tf", grad_mlp, outer_mat, preferred_element_type=jnp.float32)
    unused_value, gelu_pull = jax.vjp(exact_gelu, pre_act)
    grad_pre = gelu_pull(grad_act)[0].astype(jnp.bfloat16)
    grad_inner_add = jnp.sum(grad_pre.astype(jnp.float32), axis=0)
    grad_inner_mat = jnp.einsum(
        "td,tf->df", first_low, grad_pre, preferred_element_type=jnp.float32
    )
    grad_first = (
        jnp.einsum("tf,df->td", grad_pre, inner_mat, preferred_element_type=jnp.float32) + grad_two
    )
    grad_first_scale = jnp.sum(grad_first * first_normed, axis=0)
    grad_first_offset = jnp.sum(grad_first, axis=0)
    grad_hidden = norm_backward(
        grad_first, first_normed, first_inverse, first_scale.astype(jnp.float32)
    )
    grad_branch = grad_hidden.astype(jnp.bfloat16)
    grad_output_add = jnp.sum(grad_branch.astype(jnp.float32), axis=0)
    grad_output_mat = jnp.einsum(
        "td,te->de", attended, grad_branch, preferred_element_type=jnp.float32
    )
    grad_attended = jnp.einsum(
        "te,de->td", grad_branch, output_mat, preferred_element_type=jnp.float32
    ).astype(jnp.bfloat16)

    def backward_pair(pair_index, state_tuple):
        grad_queries, grad_keys, grad_values = state_tuple
        column_start = pair_index * 2 * HEAD
        query_pair = column_pair(queries, column_start, GROUP)
        key_pair = column_pair(keys_all, column_start, key_total)
        value_pair = column_pair(values_all, column_start, key_total)
        upstream_pair = column_pair(grad_attended, column_start, GROUP)
        scores = pair_scores(query_pair, key_pair, allowed, factor)
        pair_logsum = lax.dynamic_slice_in_dim(logsum, pair_index * 2, 2, 0)
        pair_probs = jnp.exp(scores - pair_logsum)
        weights = pair_probs.astype(jnp.bfloat16)
        grad_weights = jnp.einsum(
            "qhd,khd->hqk", upstream_pair, value_pair, preferred_element_type=jnp.float32
        )
        row_dot = jnp.sum(grad_weights * pair_probs, axis=-1, keepdims=True)
        grad_scores = (pair_probs * (grad_weights - row_dot)).astype(jnp.bfloat16)
        query_part = (
            jnp.einsum("hqk,khd->qhd", grad_scores, key_pair, preferred_element_type=jnp.float32)
            * factor
        )
        key_part = (
            jnp.einsum("hqk,qhd->khd", grad_scores, query_pair, preferred_element_type=jnp.float32)
            * factor
        )
        value_part = jnp.einsum(
            "hqk,qhd->khd", weights, upstream_pair, preferred_element_type=jnp.float32
        )
        grad_queries = lax.dynamic_update_slice_in_dim(
            grad_queries, query_part.reshape(GROUP, 2 * HEAD), column_start, 1
        )
        grad_keys = lax.dynamic_update_slice_in_dim(
            grad_keys, key_part.reshape(key_total, 2 * HEAD), column_start, 1
        )
        grad_values = lax.dynamic_update_slice_in_dim(
            grad_values, value_part.reshape(key_total, 2 * HEAD), column_start, 1
        )
        return (grad_queries, grad_keys, grad_values)

    grad_queries, grad_keys, grad_values = lax.fori_loop(
        0,
        pair_count,
        backward_pair,
        (
            jnp.zeros((GROUP, D), jnp.float32),
            jnp.zeros((key_total, D), jnp.float32),
            jnp.zeros((key_total, D), jnp.float32),
        ),
    )
    key_share, value_share = (
        lax.psum_scatter(
            grad_keys.astype(jnp.bfloat16), "seq", scatter_dimension=0, tiled=True
        ).astype(jnp.float32),
        lax.psum_scatter(
            grad_values.astype(jnp.bfloat16), "seq", scatter_dimension=0, tiled=True
        ).astype(jnp.float32),
    )
    grad_projected = jnp.concatenate(
        [
            grad_queries.astype(jnp.bfloat16),
            key_share.astype(jnp.bfloat16),
            value_share.astype(jnp.bfloat16),
        ],
        axis=1,
    )
    grad_query_add = jnp.sum(grad_projected[:, :D].astype(jnp.float32), axis=0)
    grad_value_add = jnp.sum(grad_projected[:, 2 * D :].astype(jnp.float32), axis=0)
    grad_attend_mat = jnp.einsum(
        "td,te->de", token_rows, grad_projected, preferred_element_type=jnp.float32
    )
    input_grad = grad_hidden + jnp.einsum(
        "te,de->td", grad_projected, attend_mat, preferred_element_type=jnp.float32
    )
    (
        sum_attend_mat,
        sum_query_add,
        sum_value_add,
        sum_output_mat,
        sum_output_add,
        sum_first_scale,
        sum_first_offset,
        sum_inner_mat,
        sum_inner_add,
        sum_outer_mat,
        sum_outer_add,
        sum_second_scale,
        sum_second_offset,
    ) = (
        lax.psum_scatter(grad_attend_mat, ("seq", "dp"), scatter_dimension=0, tiled=True),
        lax.psum_scatter(grad_query_add, ("seq", "dp"), scatter_dimension=0, tiled=True),
        lax.psum_scatter(grad_value_add, ("seq", "dp"), scatter_dimension=0, tiled=True),
        lax.psum_scatter(grad_output_mat, ("seq", "dp"), scatter_dimension=0, tiled=True),
        lax.psum_scatter(grad_output_add, ("seq", "dp"), scatter_dimension=0, tiled=True),
        lax.psum_scatter(grad_first_scale, ("seq", "dp"), scatter_dimension=0, tiled=True),
        lax.psum_scatter(grad_first_offset, ("seq", "dp"), scatter_dimension=0, tiled=True),
        lax.psum_scatter(grad_inner_mat, ("seq", "dp"), scatter_dimension=0, tiled=True),
        lax.psum_scatter(grad_inner_add, ("seq", "dp"), scatter_dimension=0, tiled=True),
        lax.psum_scatter(grad_outer_mat, ("seq", "dp"), scatter_dimension=0, tiled=True),
        lax.psum_scatter(grad_outer_add, ("seq", "dp"), scatter_dimension=0, tiled=True),
        lax.psum_scatter(grad_second_scale, ("seq", "dp"), scatter_dimension=0, tiled=True),
        lax.psum_scatter(grad_second_offset, ("seq", "dp"), scatter_dimension=0, tiled=True),
    )
    return (
        layer_output,
        input_grad.reshape(1, GROUP, D),
        sum_attend_mat,
        sum_query_add,
        sum_value_add,
        sum_output_mat,
        sum_output_add,
        sum_first_scale,
        sum_first_offset,
        sum_inner_mat,
        sum_inner_add,
        sum_outer_mat,
        sum_outer_add,
        sum_second_scale,
        sum_second_offset,
    )


AXES = ("seq", "dp")
DEVICES = 32
WIDE = ((3, 4, 2, 1), (3, 1, 4, 2))
NARROW = ((3, 2, 1, 4), (3, 2, 1, 4))
HINT = pl.CostEstimate(flops=1, bytes_accessed=1, transcendentals=0)
REMOTE = GROUP - 64
ROWS = GROUP + REMOTE


def swap(value, masks):
    pairs = [(i, i ^ masks[i & 1]) for i in range(DEVICES)]
    return lax.ppermute(value, AXES, pairs)


def sync(movers, *values):
    state, values = lax.optimization_barrier(([mover.data for mover in movers], values))
    for mover, data in zip(movers, state):
        mover.data = data
    return values


def stage_masks(order, stage):
    return (1 << order[0][stage], 1 << order[1][stage])


def chip_mask(bits, place):
    return sum(1 << b for t, b in enumerate(bits) if place >> t & 1)


def join_body(cut, *refs):
    sems = refs[-1]
    ins, outs = refs[: len(refs) - 3], refs[len(refs) - 3 : -1]
    copies = []
    for number, out_ref in enumerate(outs):
        width = out_ref.shape[2]
        for side in range(2):
            source = ins[side] if cut else ins[2 * number + side]
            count = source.shape[0]
            if cut:
                source = source.at[:, :, pl.ds(number * cut, width)]
            target = out_ref.at[pl.ds(side * count, count)]
            copies.append(pltpu.make_async_copy(source, target, sems.at[2 * number + side]))
    for copy in copies:
        copy.start()
    for copy in copies:
        copy.wait()


def join(pieces, cut=0):
    count, rows, columns = pieces[0].shape
    widths = (cut, columns - cut) if cut else (columns, pieces[2].shape[2])
    return pl.pallas_call(
        functools.partial(join_body, cut),
        out_shape=[
            jax.ShapeDtypeStruct((2 * count, rows, width), jnp.bfloat16) for width in widths
        ],
        in_specs=[pl.BlockSpec(memory_space=pl.ANY)] * len(pieces),
        out_specs=[pl.BlockSpec(memory_space=pltpu.VMEM)] * 2,
        scratch_shapes=[pltpu.SemaphoreType.DMA((4,))],
        compiler_params=pltpu.CompilerParams(vmem_limit_bytes=16 * 2**20),
        cost_estimate=HINT,
    )(*pieces)


class Gather:
    def __init__(self, me, weights, cut, extra=()):
        self.me, self.cut, self.data = me, cut, {}
        core = me & 1
        both = []
        for side in (core, 1 - core):
            parts = []
            for weight in weights:
                half = weight.shape[1] // 2
                parts.append(lax.dynamic_slice(weight, (0, side * half), (weight.shape[0], half)))
            parts.extend(extra)
            both.append(parts[0] if len(parts) == 1 else jnp.concatenate(parts, axis=1))
        self.data["mine"] = both[0]
        self.data["arrived"] = swap(both[1], (1, 1))

    def depth(self):
        mine, other = self.data["mine"], self.data["arrived"]
        first = (self.me & 1) == 0
        both = jnp.concatenate([jnp.where(first, mine, other), jnp.where(first, other, mine)])
        both = both[None]
        self.data = {"held": both, "arrived": swap(both, stage_masks(WIDE, 0))}

    def step(self, stage):
        held, arrived = self.data["held"], self.data["arrived"]
        if stage == 1:
            held = join([held, arrived], self.cut)
        else:
            held = join([piece for pair in zip(held, arrived) for piece in pair])
        arrived = [
            swap(piece, stage_masks(order, stage)) for piece, order in zip(held, (WIDE, NARROW))
        ]
        self.data = {"held": held, "arrived": arrived}

    def share(self, name):
        self.data[name + " core"] = [swap(piece, (1, 1)) for piece in self.data[name]]

    def pieces(self):
        names = ("held", "arrived", "held core", "arrived core")
        return [piece for name in names for piece in self.data[name]]


def gather_matmul_body(routes, count, tile, me_ref, left_ref, *refs):
    piece_refs = refs[:8]
    out_refs, product_ref = refs[8 : 8 + count], refs[8 + count]
    mats, in_sems, out_sems = refs[9 + count : 9 + 2 * count], refs[-2], refs[-1]
    me = me_ref[0]
    rows = piece_refs[0].shape[1]
    copies = []
    for number, piece in enumerate(piece_refs):
        chunk, arrived, side = number % 2, number // 2 % 2, number // 4
        order = (WIDE, NARROW)[chunk]
        base = me ^ side
        core = base & 1
        for sub in range(8):
            place = 8 * arrived + sub
            mask = jnp.where(core == 0, chip_mask(order[0], place), chip_mask(order[1], place))
            chip = (base ^ mask) >> 1
            for start, width, mat, begin in routes(chunk, mats):
                half = mat.shape[1] // 2
                target = mat.at[
                    pl.ds(pl.multiple_of(chip * rows, rows), rows),
                    pl.ds(pl.multiple_of(core * half + begin, 128), width),
                ]
                source = piece.at[sub, :, pl.ds(start, width)]
                copies.append(pltpu.make_async_copy(source, target, in_sems.at[len(copies)]))
    for copy in copies:
        copy.start()
    kept = []
    per_side = len(copies) // 2
    for side in range(2):
        core = (me ^ side) & 1
        for copy in copies[side * per_side : (side + 1) * per_side]:
            copy.wait()
        for number, (mat, out_ref) in enumerate(zip(mats, out_refs)):
            half = mat.shape[1] // 2
            columns = pl.ds(pl.multiple_of(core * half, half), half)
            kept.append(
                pltpu.make_async_copy(
                    mat.at[:, columns], out_ref.at[:, columns], out_sems.at[2 * number + side]
                )
            )
            kept[-1].start()
        half = product_ref.shape[1] // 2

        def step(i, carry):
            columns = pl.ds(pl.multiple_of(core * half + i * tile, tile), tile)
            product_ref[:, columns] = jnp.dot(
                left_ref[...], mats[0][:, columns], preferred_element_type=jnp.float32
            )
            return carry

        lax.fori_loop(0, half // tile, step, 0)
    for copy in kept:
        copy.wait()


def gather_matmul(gather, routes, widths, left):
    pieces = gather.pieces()
    depth = pieces[0].shape[1] * DEVICES // 2
    mats = [(depth, width) for width in widths]
    return pl.pallas_call(
        functools.partial(gather_matmul_body, routes, len(widths), 512),
        out_shape=[jax.ShapeDtypeStruct(mat, jnp.bfloat16) for mat in mats]
        + [jax.ShapeDtypeStruct((left.shape[0], widths[0]), jnp.float32)],
        in_specs=[
            pl.BlockSpec(memory_space=pltpu.SMEM),
            pl.BlockSpec(memory_space=pltpu.VMEM),
        ]
        + [pl.BlockSpec(memory_space=pl.ANY)] * 8,
        out_specs=[pl.BlockSpec(memory_space=pl.ANY)] * len(widths)
        + [pl.BlockSpec(memory_space=pltpu.VMEM)],
        scratch_shapes=[pltpu.VMEM(mat, jnp.bfloat16) for mat in mats]
        + [pltpu.SemaphoreType.DMA((96,)), pltpu.SemaphoreType.DMA((2 * len(widths),))],
        compiler_params=pltpu.CompilerParams(vmem_limit_bytes=40 * 2**20),
        cost_estimate=HINT,
    )(gather.me.reshape(1), left, *pieces)


def whole_routes(cut, chunk, outs):
    half = outs[0].shape[1] // 2
    return ((0, (cut, half - cut)[chunk], outs[0], chunk * cut),)


def first_routes(chunk, outs):
    if chunk == 0:
        return ((0, outs[0].shape[1] // 2, outs[0], 0),)
    half = outs[1].shape[1] // 2
    return ((0, half, outs[1], 0), (half, outs[2].shape[1] // 2, outs[2], 0))


def place_of(bits, shard):
    place = shard & 1
    for t, b in enumerate(bits):
        place = place | ((shard >> b) & 1) << (t + 1)
    return place


def weight_grad_body(chunks, tile, me_ref, left_ref, right_ref, *refs):
    extra_refs = refs[: -2 * len(chunks)]
    outs = refs[-2 * len(chunks) :]
    me = me_ref[0]
    rows = outs[0].shape[1]
    half = right_ref.shape[1] // 2
    per_tile = tile // rows

    def step(i, carry):
        left = left_ref[:, pl.ds(pl.multiple_of(i * tile, tile), tile)].T
        for side in (1, 0):
            base = me ^ side
            core = base & 1
            right = right_ref[:, pl.ds(pl.multiple_of(core * half, half), half)]
            product = jnp.dot(left, right, preferred_element_type=jnp.float32).astype(
                jnp.bfloat16
            )
            for sub in range(per_tile):
                number = i * per_tile + sub
                shard = number ^ base
                for which, (order, begin, width) in enumerate(chunks):
                    place = jnp.where(
                        core == 0, place_of(order[0], shard), place_of(order[1], shard)
                    )
                    out_ref = outs[2 * which + side]
                    out_ref[place, :, :width] = product[
                        sub * rows : (sub + 1) * rows, begin : begin + width
                    ]
                    for extra_ref in extra_refs:
                        out_ref[place, :, width:] = extra_ref[number]
        return carry

    lax.fori_loop(0, left_ref.shape[1] // tile, step, 0)


def weight_grad(left, right, me, chunks, extra=()):
    depth = left.shape[1]
    rows = depth // DEVICES
    more = sum(e.shape[2] for e in extra)
    shapes = [
        jax.ShapeDtypeStruct((DEVICES, rows, width + more), jnp.bfloat16)
        for _, _, width in chunks
        for _ in range(2)
    ]
    outs = pl.pallas_call(
        functools.partial(weight_grad_body, chunks, 256),
        out_shape=shapes,
        in_specs=[pl.BlockSpec(memory_space=pltpu.SMEM)]
        + [pl.BlockSpec(memory_space=pltpu.VMEM)] * (2 + len(extra)),
        out_specs=[pl.BlockSpec(memory_space=pltpu.VMEM)] * len(shapes),
        compiler_params=pltpu.CompilerParams(vmem_limit_bytes=24 * 2**20),
        cost_estimate=HINT,
    )(me.reshape(1), left, right, *extra)
    return [tuple(outs[i : i + 2]) for i in range(0, len(outs), 2)]


def add_low(one, two):
    return (one.astype(jnp.float32) + two.astype(jnp.float32)).astype(jnp.bfloat16)


def halve_body(*refs):
    count = len(refs) // 6
    for which in range(count):
        held_low, held_high, low, high = refs[4 * which : 4 * which + 4]
        keep_ref, send_ref = refs[4 * count + 2 * which : 4 * count + 2 * which + 2]
        send_ref[...] = add_low(held_high[...], high[...])
        keep_ref[...] = add_low(held_low[...], low[...])


def halve(pairs):
    half = pairs[0][0].shape[0] // 2
    block = max(half // 4, 1)
    steps = half // block
    specs, outs, shapes, values = [], [], [], []
    for held, arrived in pairs:
        _, rows, columns = held.shape
        low = pl.BlockSpec((block, rows, columns), lambda i: (i, 0, 0))
        high = pl.BlockSpec((block, rows, columns), lambda i: (steps + i, 0, 0))
        specs += [low, high, low, high]
        outs += [low, low]
        shapes += [jax.ShapeDtypeStruct((half, rows, columns), jnp.bfloat16)] * 2
        values += [held, held, arrived, arrived]
    results = pl.pallas_call(
        halve_body,
        grid=(steps,),
        in_specs=specs,
        out_specs=outs,
        out_shape=shapes,
        compiler_params=pltpu.CompilerParams(vmem_limit_bytes=16 * 2**20),
        cost_estimate=HINT,
    )(*values)
    return results[0::2], results[1::2]


def first_norm_body(
    rows_ref, mixed_ref, matrix_ref, add_ref, gain_ref, shift_ref, low_ref, out_ref, normed_ref, inverse_ref
):
    branch = jnp.dot(mixed_ref[...], matrix_ref[...], preferred_element_type=jnp.float32)
    out, normed, inverse = norm_forward(
        rows_ref[...].astype(jnp.float32) + (branch + add_ref[...]), gain_ref[...], shift_ref[...]
    )
    low_ref[...] = out.astype(jnp.bfloat16)
    out_ref[...] = out
    normed_ref[...] = normed
    inverse_ref[...] = inverse


def first_norm(rows, mixed, matrix, add, gain, shift):
    block = 128
    tall = pl.BlockSpec((block, D), lambda i: (i, 0))
    whole = pl.BlockSpec((1, D), lambda i: (0, 0))
    return pl.pallas_call(
        first_norm_body,
        grid=(GROUP // block,),
        in_specs=[tall, tall, pl.BlockSpec((D, D), lambda i: (0, 0)), whole, whole, whole],
        out_specs=[tall, tall, tall, pl.BlockSpec((block, 1), lambda i: (i, 0))],
        out_shape=[
            jax.ShapeDtypeStruct((GROUP, D), jnp.bfloat16),
            jax.ShapeDtypeStruct((GROUP, D), jnp.float32),
            jax.ShapeDtypeStruct((GROUP, D), jnp.float32),
            jax.ShapeDtypeStruct((GROUP, 1), jnp.float32),
        ],
        compiler_params=pltpu.CompilerParams(vmem_limit_bytes=20 * 2**20),
        cost_estimate=HINT,
    )(rows, mixed, matrix, add, gain, shift)


def rows_back_body(grad_ref, matrix_ref, near_ref, far_ref):
    product = lax.dot_general(
        grad_ref[...],
        matrix_ref[...],
        (((1,), (1,)), ((), ())),
        preferred_element_type=jnp.float32,
    )
    near_ref[...] = product[:GROUP]
    far_ref[...] = product[GROUP:].astype(jnp.bfloat16)


def rows_back(grad, matrix):
    return pl.pallas_call(
        rows_back_body,
        grid=(4,),
        in_specs=[
            pl.BlockSpec((ROWS, 3 * D), lambda i: (0, 0)),
            pl.BlockSpec((D // 4, 3 * D), lambda i: (i, 0)),
        ],
        out_specs=[
            pl.BlockSpec((GROUP, D // 4), lambda i: (0, i)),
            pl.BlockSpec((REMOTE, D // 4), lambda i: (0, i)),
        ],
        out_shape=[
            jax.ShapeDtypeStruct((GROUP, D), jnp.float32),
            jax.ShapeDtypeStruct((REMOTE, D), jnp.bfloat16),
        ],
        compiler_params=pltpu.CompilerParams(vmem_limit_bytes=16 * 2**20),
        cost_estimate=HINT,
    )(grad, matrix)


def cut_grads(me, left, right, cut):
    half = right.shape[1] // 2
    return weight_grad(left, right, me, ((WIDE, 0, cut), (NARROW, cut, half - cut)))


class Scatter:
    def __init__(self, me, grads):
        self.me, self.stage = me, 4
        self.data = {"held": [keep for keep, _ in grads], "send": [send for _, send in grads]}

    def begin(self):
        self.data["arrived"] = [swap(piece, (1, 1)) for piece in self.data.pop("send")]

    def step(self):
        self.stage -= 1
        held, send = halve(list(zip(self.data["held"], self.data["arrived"])))
        if self.stage == 0:
            held, send = jnp.concatenate(held, axis=2), jnp.concatenate(send, axis=2)
            arrived = swap(send, stage_masks(WIDE, 0))
        else:
            arrived = [
                swap(piece, stage_masks(order, self.stage))
                for piece, order in zip(send, (WIDE, NARROW))
            ]
        self.data = {"held": held, "arrived": arrived}

    def near(self):
        held, arrived = self.data["held"], self.data["arrived"]
        send = add_low(held[1], arrived[1])
        held = held[0].astype(jnp.float32) + arrived[0].astype(jnp.float32)
        self.data = {"held": held, "arrived": swap(send, (1, 1))}

    def result(self):
        held, arrived = self.data["held"], self.data["arrived"].astype(jnp.float32)
        first = (self.me & 1) == 0
        return jnp.where(first, held, arrived), jnp.where(first, arrived, held)


def attend_forward_body(query_docs, key_docs, query_ref, key_ref, value_ref, mixed_ref, log_ref):
    allowed = key_docs[...] == query_docs[...]
    queries, keys = query_ref[...], key_ref[...]
    value_rows = value_ref[...].T
    lanes = lax.broadcasted_iota(jnp.int32, keys.shape, 1)
    results = []
    for head in range(2):
        chosen = (lanes < HEAD) if head == 0 else (lanes >= HEAD)
        raw = lax.dot_general(
            jnp.where(chosen, keys, jnp.zeros_like(keys)),
            queries,
            (((1,), (1,)), ((), ())),
            preferred_element_type=jnp.float32,
        )
        scores = jnp.where(allowed, raw * HEAD**-0.5, masked_score)
        peak = jnp.max(scores, axis=0, keepdims=True)
        terms = jnp.exp(scores - peak)
        total = jnp.sum(terms, axis=0, keepdims=True)
        weights = (terms * (1.0 / total)).astype(jnp.bfloat16)
        results.append(
            jnp.dot(
                value_rows[head * HEAD : (head + 1) * HEAD],
                weights,
                preferred_element_type=jnp.float32,
            )
        )
        log_ref[0, head : head + 1] = peak + jnp.log(total)
    mixed_ref[...] = jnp.concatenate(results).T.astype(jnp.bfloat16)


def attend_forward(query_docs, key_docs, projected):
    pairs = HEADS // 2
    return pl.pallas_call(
        attend_forward_body,
        grid=(pairs,),
        in_specs=[
            pl.BlockSpec((1, GROUP), lambda i: (0, 0)),
            pl.BlockSpec((ROWS, 1), lambda i: (0, 0)),
            pl.BlockSpec((GROUP, 128), lambda i: (0, i)),
            pl.BlockSpec((ROWS, 128), lambda i: (0, pairs + i)),
            pl.BlockSpec((ROWS, 128), lambda i: (0, 2 * pairs + i)),
        ],
        out_specs=[
            pl.BlockSpec((GROUP, 128), lambda i: (0, i)),
            pl.BlockSpec((1, 2, GROUP), lambda i: (i, 0, 0)),
        ],
        out_shape=[
            jax.ShapeDtypeStruct((GROUP, D), jnp.bfloat16),
            jax.ShapeDtypeStruct((pairs, 2, GROUP), jnp.float32),
        ],
        compiler_params=pltpu.CompilerParams(vmem_limit_bytes=16 * 2**20),
        cost_estimate=HINT,
    )(query_docs, key_docs, projected, projected, projected)


def attend_backward_body(
    query_docs, key_docs, query_ref, key_ref, value_ref, upstream_ref, log_ref, grad_ref, sum_ref
):
    pair = pl.program_id(0)
    allowed = key_docs[...] == query_docs[...]
    queries, keys, values = query_ref[...], key_ref[...], value_ref[...]
    upstream = upstream_ref[...]
    key_rows = keys.T
    wide = lax.broadcasted_iota(jnp.int32, keys.shape, 1) < HEAD
    zeros = jnp.zeros_like(keys)
    across = (((1,), (1,)), ((), ()))
    query_parts, key_parts, value_parts = [], [], []
    for head in range(2):
        chosen = wide if head == 0 else jnp.logical_not(wide)
        raw = lax.dot_general(
            jnp.where(chosen, keys, zeros), queries, across, preferred_element_type=jnp.float32
        )
        scores = jnp.where(allowed, raw * HEAD**-0.5, masked_score)
        probs = jnp.exp(scores - log_ref[0, head : head + 1])
        grad_weights = lax.dot_general(
            jnp.where(chosen, values, zeros), upstream, across, preferred_element_type=jnp.float32
        )
        row_dot = jnp.sum(grad_weights * probs, axis=0, keepdims=True)
        grad_scores = (probs * (grad_weights - row_dot)).astype(jnp.bfloat16)
        weights = probs.astype(jnp.bfloat16)
        query_parts.append(
            jnp.dot(
                key_rows[head * HEAD : (head + 1) * HEAD],
                grad_scores,
                preferred_element_type=jnp.float32,
            )
        )
        key_parts.append(jnp.dot(grad_scores, queries, preferred_element_type=jnp.float32))
        value_parts.append(jnp.dot(weights, upstream, preferred_element_type=jnp.float32))
    grad_queries = (jnp.concatenate(query_parts).T * HEAD**-0.5).astype(jnp.bfloat16)
    grad_keys = jnp.where(wide, key_parts[0], key_parts[1]) * HEAD**-0.5
    grad_values = jnp.where(wide, value_parts[0], value_parts[1]).astype(jnp.bfloat16)
    column = pl.multiple_of(pair * 128, 128)
    grad_ref[:GROUP, pl.ds(column, 128)] = grad_queries
    grad_ref[GROUP:, pl.ds(column, 128)] = jnp.zeros((REMOTE, 128), jnp.bfloat16)
    grad_ref[:, pl.ds(pl.multiple_of(D + pair * 128, 128), 128)] = grad_keys.astype(jnp.bfloat16)
    grad_ref[:, pl.ds(pl.multiple_of(2 * D + pair * 128, 128), 128)] = grad_values
    low = grad_queries.astype(jnp.float32)
    sum_ref[0, :, pl.ds(column, 128)] = jnp.sum(low, axis=0, keepdims=True)
    low = grad_values.astype(jnp.float32)
    sum_ref[1, :, pl.ds(column, 128)] = jnp.sum(low, axis=0, keepdims=True)


def attend_backward(query_docs, key_docs, projected, upstream, logs):
    pairs = HEADS // 2
    return pl.pallas_call(
        attend_backward_body,
        grid=(pairs,),
        in_specs=[
            pl.BlockSpec((1, GROUP), lambda i: (0, 0)),
            pl.BlockSpec((ROWS, 1), lambda i: (0, 0)),
            pl.BlockSpec((GROUP, 128), lambda i: (0, i)),
            pl.BlockSpec((ROWS, 128), lambda i: (0, pairs + i)),
            pl.BlockSpec((ROWS, 128), lambda i: (0, 2 * pairs + i)),
            pl.BlockSpec((GROUP, 128), lambda i: (0, i)),
            pl.BlockSpec((1, 2, GROUP), lambda i: (i, 0, 0)),
        ],
        out_specs=[
            pl.BlockSpec((ROWS, 3 * D), lambda i: (0, 0)),
            pl.BlockSpec((2, 1, D), lambda i: (0, 0, 0)),
        ],
        out_shape=[
            jax.ShapeDtypeStruct((ROWS, 3 * D), jnp.bfloat16),
            jax.ShapeDtypeStruct((2, 1, D), jnp.float32),
        ],
        compiler_params=pltpu.CompilerParams(vmem_limit_bytes=16 * 2**20),
        cost_estimate=HINT,
    )(query_docs, key_docs, projected, projected, projected, upstream, logs)


def pack_shard(vectors):
    rows = jnp.concatenate([vector.reshape(-1, 32) for vector in vectors])
    return jnp.pad(rows, ((0, 32 - rows.shape[0]), (0, 96)))


def unpack_shards(packed):
    rows = packed.reshape(DEVICES, 32, 256)[:, :12, :32].astype(jnp.float32)
    short = rows[:, :8].transpose(1, 0, 2).reshape(8, 1, D)
    return [short[i] for i in range(8)] + [rows[:, 8:].reshape(1, 4 * D)]


def pack_grads(short, long):
    rows = jnp.concatenate([vector.reshape(1, 8, 128) for vector in short])
    rows = jnp.repeat(rows.transpose(1, 0, 2), 4, axis=0)
    rows = jnp.concatenate([rows, long.reshape(DEVICES, 1, 128)], axis=1)
    return jnp.pad(rows, ((0, 0), (0, 23), (0, 0))).astype(jnp.bfloat16)


def fast_local(
    tokens,
    cotangent,
    doc_lengths,
    attend_weight,
    query_bias,
    value_bias,
    output_weight,
    output_bias,
    first_gain,
    first_shift,
    inner_weight,
    inner_bias,
    outer_weight,
    outer_bias,
    second_gain,
    second_shift,
):
    me = lax.axis_index(AXES)
    group_index = me >> 4
    small_shard = pack_shard(
        [
            query_bias,
            value_bias,
            output_bias,
            first_gain,
            first_shift,
            outer_bias,
            second_gain,
            second_shift,
            inner_bias,
        ]
    )
    attend_cut, inner_cut, outer_cut = 3 * D // 2, 1408, 384
    one = Gather(me, (attend_weight, output_weight), attend_cut, (small_shard,))
    sync((one,))

    one.depth()
    two = Gather(me, (inner_weight,), inner_cut)
    three = Gather(me, (outer_weight,), outer_cut)
    movers = (one, two, three)
    doc_ends = jnp.cumsum(doc_lengths[0])
    near_at = group_index * GROUP + lax.iota(jnp.int32, GROUP)
    far_at = jnp.where(group_index == 0, GROUP, 64) + lax.iota(jnp.int32, REMOTE)
    row_at = jnp.concatenate([near_at, far_at])
    row_docs = jnp.sum((row_at[:, None] >= doc_ends[None, :]).astype(jnp.int32), axis=1)
    query_docs, key_docs = row_docs[None, :GROUP], row_docs[:, None]
    near = tokens.reshape(GROUP, D)
    query_docs, key_docs, near = sync(movers, query_docs, key_docs, near)

    one.step(1)
    two.depth()
    far = lax.dynamic_slice(near, (64 * (1 - group_index), 0), (REMOTE, D))
    far = lax.ppermute(far, "seq", [(0, 1), (1, 0)])
    (far,) = sync((one, two), far)

    one.step(2)
    three.depth()
    token_rows = jnp.concatenate([near, far])
    (token_rows,) = sync(movers, token_rows)

    one.step(3)
    two.step(1)
    sync((one, two))

    one.share("held")
    one.share("arrived")
    sync((one,))

    two.step(2)
    three.step(1)
    attend_mat, output_mat, small_all, projected = gather_matmul(
        one, first_routes, (3 * D, D, 256), token_rows
    )
    (
        query_add,
        value_add,
        output_add,
        first_scale,
        first_offset,
        outer_add,
        second_scale,
        second_offset,
        inner_add,
    ) = unpack_shards(small_all)
    bias_row = jnp.concatenate([query_add, jnp.zeros((1, D), jnp.float32), value_add], axis=1)
    projected = (projected + bias_row).astype(jnp.bfloat16)
    (projected,) = sync((two, three), projected)

    two.step(3)
    three.step(2)
    attended, logs = attend_forward(query_docs, key_docs, projected)
    first_low, first_out, first_normed, first_inverse = first_norm(
        near, attended, output_mat, output_add, first_scale, first_offset
    )
    first_out, first_normed, first_inverse, first_low = sync(
        (two, three), first_out, first_normed, first_inverse, first_low
    )

    two.share("held")
    two.share("arrived")
    sync((two,))

    three.step(3)
    three.share("held")
    inner_mat, pre_act = gather_matmul(
        two, functools.partial(whole_routes, inner_cut), (4 * D,), first_low
    )
    pre_act = pre_act + inner_add
    cdf = 0.5 * (1.0 + lax.erf(pre_act * 0.5**0.5))
    gelu_slope = cdf + pre_act * jnp.exp(-0.5 * pre_act * pre_act) * 0.3989422804014327
    activated = (pre_act * cdf).astype(jnp.bfloat16)
    activated, gelu_slope = sync((three,), activated, gelu_slope)

    three.share("arrived")
    outer_mat, mlp_out = gather_matmul(
        three, functools.partial(whole_routes, outer_cut), (D,), activated
    )
    mlp_out = mlp_out + outer_add
    second_out, second_normed, second_inverse = norm_forward(
        first_out + mlp_out, second_scale, second_offset
    )
    layer_output = second_out.astype(jnp.bfloat16).reshape(1, GROUP, D)
    upstream = cotangent.reshape(GROUP, D).astype(jnp.float32)
    grad_two = norm_backward(upstream, second_normed, second_inverse, second_scale)
    grad_mlp = grad_two.astype(jnp.bfloat16)
    outer = Scatter(me, cut_grads(me, activated, grad_mlp, outer_cut))
    grad_mlp, grad_two, second_normed = sync((outer,), grad_mlp, grad_two, second_normed)

    outer.begin()
    grad_act = jnp.einsum("td,fd->tf", grad_mlp, outer_mat, preferred_element_type=jnp.float32)
    grad_pre = (grad_act * gelu_slope).astype(jnp.bfloat16)
    inner_sum = jnp.sum(grad_pre.astype(jnp.float32), axis=0)
    grad_pre, inner_sum, grad_mlp, second_normed = sync(
        (outer,), grad_pre, inner_sum, grad_mlp, second_normed
    )

    outer.step()
    inner = Scatter(me, cut_grads(me, first_low, grad_pre, inner_cut))
    second_sums = (
        jnp.sum(grad_mlp.astype(jnp.float32), axis=0),
        jnp.sum(upstream * second_normed, axis=0),
        jnp.sum(upstream, axis=0),
    )
    grad_first = (
        jnp.einsum("tf,df->td", grad_pre, inner_mat, preferred_element_type=jnp.float32) + grad_two
    )
    grad_hidden = norm_backward(grad_first, first_normed, first_inverse, first_scale)
    grad_branch = grad_hidden.astype(jnp.bfloat16)
    first_sums = (
        jnp.sum(grad_branch.astype(jnp.float32), axis=0),
        jnp.sum(grad_first * first_normed, axis=0),
        jnp.sum(grad_first, axis=0),
    )
    grad_attended = jnp.einsum(
        "te,de->td", grad_branch, output_mat, preferred_element_type=jnp.float32
    ).astype(jnp.bfloat16)
    first_sums, second_sums, grad_hidden, grad_branch, grad_attended = sync(
        (outer, inner), first_sums, second_sums, grad_hidden, grad_branch, grad_attended
    )

    inner.begin()
    outer.step()
    grad_projected, row_sums = attend_backward(
        query_docs, key_docs, projected, grad_attended, logs
    )
    grad_projected, row_sums = sync((outer, inner), grad_projected, row_sums)

    inner.step()
    outer.step()
    small = pack_grads([row_sums[0, 0], row_sums[1, 0], *first_sums, *second_sums], inner_sum)
    first = Scatter(
        me,
        weight_grad(token_rows, grad_projected, me, ((WIDE, 0, attend_cut),))
        + weight_grad(attended, grad_branch, me, ((NARROW, 0, D // 2),), (small,)),
    )
    movers = (outer, inner, first)
    sync(movers)

    first.begin()
    inner.step()
    outer.step()
    row_grad, far_grad = rows_back(grad_projected, attend_mat)
    row_grad, far_grad = sync(movers, row_grad, far_grad)

    first.step()
    inner.step()
    outer.near()
    sync(movers)

    first.step()
    inner.step()
    sum_outer_mat = jnp.concatenate(outer.result(), axis=1)
    (sum_outer_mat,) = sync((inner, first), sum_outer_mat)

    first.step()
    inner.near()
    (far_grad,) = sync((inner, first), far_grad)

    first.step()
    far_grad = lax.ppermute(far_grad, "seq", [(0, 1), (1, 0)])
    sum_inner_mat = jnp.concatenate(inner.result(), axis=1)
    sum_inner_mat, far_grad = sync((first,), sum_inner_mat, far_grad)

    first.near()
    filler = jnp.zeros((64, D), jnp.float32)
    far_grad = far_grad.astype(jnp.float32)
    far_grad = jnp.where(
        group_index == 0,
        jnp.concatenate([filler, far_grad]),
        jnp.concatenate([far_grad, filler]),
    )
    input_grad = grad_hidden + row_grad + far_grad
    halves = first.result()
    output_end = attend_cut + D // 2
    sum_attend_mat = jnp.concatenate([half[:, :attend_cut] for half in halves], axis=1)
    sum_output_mat = jnp.concatenate([half[:, attend_cut:output_end] for half in halves], axis=1)
    small_rows = halves[0][:, output_end:]
    own = lax.dynamic_slice(small_rows, (0, 32 * (me & 3)), (8, 32))
    (
        sum_query_add,
        sum_value_add,
        sum_output_add,
        sum_first_scale,
        sum_first_offset,
        sum_outer_add,
        sum_second_scale,
        sum_second_offset,
    ) = (own[i] for i in range(8))
    sum_inner_add = small_rows[8]
    return (
        layer_output,
        input_grad.reshape(1, GROUP, D),
        sum_attend_mat,
        sum_query_add,
        sum_value_add,
        sum_output_mat,
        sum_output_add,
        sum_first_scale,
        sum_first_offset,
        sum_inner_mat,
        sum_inner_add,
        sum_outer_mat,
        sum_outer_add,
        sum_second_scale,
        sum_second_offset,
    )


def solution(mesh):
    sizes = (mesh.shape["seq"], mesh.shape["dp"])
    return jax.shard_map(
        fast_local if sizes == (2, 16) else general_local,
        mesh=mesh,
        in_specs=(
            P("dp", "seq", None),
            P("dp", "seq", None),
            P("dp", None),
            P(("seq", "dp"), None),
            P(("seq", "dp")),
            P(("seq", "dp")),
            P(("seq", "dp"), None),
            P(("seq", "dp")),
            P(("seq", "dp")),
            P(("seq", "dp")),
            P(("seq", "dp"), None),
            P(("seq", "dp")),
            P(("seq", "dp"), None),
            P(("seq", "dp")),
            P(("seq", "dp")),
            P(("seq", "dp")),
        ),
        out_specs=(
            P("dp", "seq", None),
            P("dp", "seq", None),
            P(("seq", "dp"), None),
            P(("seq", "dp")),
            P(("seq", "dp")),
            P(("seq", "dp"), None),
            P(("seq", "dp")),
            P(("seq", "dp")),
            P(("seq", "dp")),
            P(("seq", "dp"), None),
            P(("seq", "dp")),
            P(("seq", "dp"), None),
            P(("seq", "dp")),
            P(("seq", "dp")),
            P(("seq", "dp")),
        ),
        check_vma=False,
    )
```

```python
import functools

import jax
import jax.numpy as jnp
from jax import lax
from jax.experimental import pallas as pl
from jax.experimental.pallas import tpu as pltpu
from jax.sharding import PartitionSpec as P

D = 1024
HEADS = 16
HEAD = 64
GROUP = 256


epsilon = 1e-12
masked_score = -1e30


def norm_forward(value, gain, shift):
    mean_value = jnp.mean(value, axis=-1, keepdims=True)
    center = value - mean_value
    inverse = lax.rsqrt(jnp.mean(center * center, axis=-1, keepdims=True) + epsilon)
    normed = center * inverse
    return (normed * gain + shift, normed, inverse)


def norm_backward(upstream, normed, inverse, gain):
    scaled = upstream * gain
    first_mean = jnp.mean(scaled, axis=-1, keepdims=True)
    second_mean = jnp.mean(scaled * normed, axis=-1, keepdims=True)
    return inverse * (scaled - first_mean - normed * second_mean)


def exact_gelu(value):
    return jax.nn.gelu(value, approximate=False)


def pair_scores(query_pair, key_pair, allowed, factor):
    raw = (
        jnp.einsum("qhd,khd->hqk", query_pair, key_pair, preferred_element_type=jnp.float32)
        * factor
    )
    return jnp.where(allowed[None], raw, masked_score)


def column_pair(matrix, column_start, row_count):
    return lax.dynamic_slice_in_dim(matrix, column_start, 2 * HEAD, 1).reshape(row_count, 2, HEAD)


def general_local(
    tokens,
    cotangent,
    doc_lengths,
    attend_weight,
    query_bias,
    value_bias,
    output_weight,
    output_bias,
    first_gain,
    first_shift,
    inner_weight,
    inner_bias,
    outer_weight,
    outer_bias,
    second_gain,
    second_shift,
):
    (
        attend_mat,
        query_add,
        value_add,
        output_mat,
        output_add,
        first_scale,
        first_offset,
        inner_mat,
        inner_add,
        outer_mat,
        outer_add,
        second_scale,
        second_offset,
    ) = (
        lax.all_gather(attend_weight, ("seq", "dp"), axis=0, tiled=True),
        lax.all_gather(query_bias, ("seq", "dp"), axis=0, tiled=True),
        lax.all_gather(value_bias, ("seq", "dp"), axis=0, tiled=True),
        lax.all_gather(output_weight, ("seq", "dp"), axis=0, tiled=True),
        lax.all_gather(output_bias, ("seq", "dp"), axis=0, tiled=True),
        lax.all_gather(first_gain, ("seq", "dp"), axis=0, tiled=True),
        lax.all_gather(first_shift, ("seq", "dp"), axis=0, tiled=True),
        lax.all_gather(inner_weight, ("seq", "dp"), axis=0, tiled=True),
        lax.all_gather(inner_bias, ("seq", "dp"), axis=0, tiled=True),
        lax.all_gather(outer_weight, ("seq", "dp"), axis=0, tiled=True),
        lax.all_gather(outer_bias, ("seq", "dp"), axis=0, tiled=True),
        lax.all_gather(second_gain, ("seq", "dp"), axis=0, tiled=True),
        lax.all_gather(second_shift, ("seq", "dp"), axis=0, tiled=True),
    )
    token_rows = tokens.reshape(GROUP, D)
    key_total = GROUP * lax.axis_size("seq")
    group_index = lax.axis_index("seq")
    doc_ends = jnp.cumsum(doc_lengths[0])
    positions = lax.iota(jnp.int32, key_total)
    key_docs = jnp.sum((positions[:, None] >= doc_ends[None, :]).astype(jnp.int32), axis=1)
    query_docs = lax.dynamic_slice_in_dim(key_docs, group_index * GROUP, GROUP)
    allowed = query_docs[:, None] == key_docs[None, :]
    factor = HEAD ** (-0.5)
    pair_count = HEADS // 2
    bias_row = jnp.concatenate(
        [query_add.astype(jnp.float32), jnp.zeros((D,), jnp.float32), value_add.astype(jnp.float32)]
    )
    projected = jnp.dot(token_rows, attend_mat, preferred_element_type=jnp.float32) + bias_row
    queries = projected[:, :D].astype(jnp.bfloat16)
    keys_mine = projected[:, D : 2 * D].astype(jnp.bfloat16)
    values_mine = projected[:, 2 * D :].astype(jnp.bfloat16)
    keys_all, values_all = (
        lax.all_gather(keys_mine, "seq", axis=0, tiled=True),
        lax.all_gather(values_mine, "seq", axis=0, tiled=True),
    )

    def forward_pair(pair_index, state_tuple):
        mixed_heads, logsum = state_tuple
        column_start = pair_index * 2 * HEAD
        query_pair = column_pair(queries, column_start, GROUP)
        key_pair = column_pair(keys_all, column_start, key_total)
        value_pair = column_pair(values_all, column_start, key_total)
        scores = pair_scores(query_pair, key_pair, allowed, factor)
        row_peak = jnp.max(scores, axis=-1, keepdims=True)
        expo_terms = jnp.exp(scores - row_peak)
        row_total = jnp.sum(expo_terms, axis=-1, keepdims=True)
        weights = (expo_terms / row_total).astype(jnp.bfloat16)
        result = jnp.einsum(
            "hqk,khd->qhd", weights, value_pair, preferred_element_type=jnp.float32
        ).reshape(GROUP, 2 * HEAD)
        mixed_heads = lax.dynamic_update_slice_in_dim(mixed_heads, result, column_start, 1)
        logsum = lax.dynamic_update_slice_in_dim(
            logsum, row_peak + jnp.log(row_total), pair_index * 2, 0
        )
        return (mixed_heads, logsum)

    mixed_heads, logsum = lax.fori_loop(
        0,
        pair_count,
        forward_pair,
        (jnp.zeros((GROUP, D), jnp.float32), jnp.zeros((HEADS, GROUP, 1), jnp.float32)),
    )
    attended = mixed_heads.astype(jnp.bfloat16)
    branch = jnp.dot(attended, output_mat, preferred_element_type=jnp.float32) + output_add.astype(
        jnp.float32
    )
    first_out, first_normed, first_inverse = norm_forward(
        token_rows.astype(jnp.float32) + branch,
        first_scale.astype(jnp.float32),
        first_offset.astype(jnp.float32),
    )
    first_low = first_out.astype(jnp.bfloat16)
    pre_act = jnp.dot(first_low, inner_mat, preferred_element_type=jnp.float32) + inner_add.astype(
        jnp.float32
    )
    activated = exact_gelu(pre_act).astype(jnp.bfloat16)
    mlp_out = jnp.dot(activated, outer_mat, preferred_element_type=jnp.float32) + outer_add.astype(
        jnp.float32
    )
    second_out, second_normed, second_inverse = norm_forward(
        first_out + mlp_out, second_scale.astype(jnp.float32), second_offset.astype(jnp.float32)
    )
    layer_output = second_out.astype(jnp.bfloat16).reshape(1, GROUP, D)
    (
        attend_mat,
        query_add,
        value_add,
        output_mat,
        output_add,
        first_scale,
        first_offset,
        inner_mat,
        inner_add,
        outer_mat,
        outer_add,
        second_scale,
        second_offset,
    ) = (
        lax.all_gather(attend_weight, ("seq", "dp"), axis=0, tiled=True),
        lax.all_gather(query_bias, ("seq", "dp"), axis=0, tiled=True),
        lax.all_gather(value_bias, ("seq", "dp"), axis=0, tiled=True),
        lax.all_gather(output_weight, ("seq", "dp"), axis=0, tiled=True),
        lax.all_gather(output_bias, ("seq", "dp"), axis=0, tiled=True),
        lax.all_gather(first_gain, ("seq", "dp"), axis=0, tiled=True),
        lax.all_gather(first_shift, ("seq", "dp"), axis=0, tiled=True),
        lax.all_gather(inner_weight, ("seq", "dp"), axis=0, tiled=True),
        lax.all_gather(inner_bias, ("seq", "dp"), axis=0, tiled=True),
        lax.all_gather(outer_weight, ("seq", "dp"), axis=0, tiled=True),
        lax.all_gather(outer_bias, ("seq", "dp"), axis=0, tiled=True),
        lax.all_gather(second_gain, ("seq", "dp"), axis=0, tiled=True),
        lax.all_gather(second_shift, ("seq", "dp"), axis=0, tiled=True),
    )
    upstream = cotangent.reshape(GROUP, D).astype(jnp.float32)
    grad_second_scale = jnp.sum(upstream * second_normed, axis=0)
    grad_second_offset = jnp.sum(upstream, axis=0)
    grad_two = norm_backward(
        upstream, second_normed, second_inverse, second_scale.astype(jnp.float32)
    )
    grad_mlp = grad_two.astype(jnp.bfloat16)
    grad_outer_add = jnp.sum(grad_mlp.astype(jnp.float32), axis=0)
    grad_outer_mat = jnp.einsum(
        "tf,td->fd", activated, grad_mlp, preferred_element_type=jnp.float32
    )
    grad_act = jnp.einsum("td,fd->tf", grad_mlp, outer_mat, preferred_element_type=jnp.float32)
    unused_value, gelu_pull = jax.vjp(exact_gelu, pre_act)
    grad_pre = gelu_pull(grad_act)[0].astype(jnp.bfloat16)
    grad_inner_add = jnp.sum(grad_pre.astype(jnp.float32), axis=0)
    grad_inner_mat = jnp.einsum(
        "td,tf->df", first_low, grad_pre, preferred_element_type=jnp.float32
    )
    grad_first = (
        jnp.einsum("tf,df->td", grad_pre, inner_mat, preferred_element_type=jnp.float32) + grad_two
    )
    grad_first_scale = jnp.sum(grad_first * first_normed, axis=0)
    grad_first_offset = jnp.sum(grad_first, axis=0)
    grad_hidden = norm_backward(
        grad_first, first_normed, first_inverse, first_scale.astype(jnp.float32)
    )
    grad_branch = grad_hidden.astype(jnp.bfloat16)
    grad_output_add = jnp.sum(grad_branch.astype(jnp.float32), axis=0)
    grad_output_mat = jnp.einsum(
        "td,te->de", attended, grad_branch, preferred_element_type=jnp.float32
    )
    grad_attended = jnp.einsum(
        "te,de->td", grad_branch, output_mat, preferred_element_type=jnp.float32
    ).astype(jnp.bfloat16)

    def backward_pair(pair_index, state_tuple):
        grad_queries, grad_keys, grad_values = state_tuple
        column_start = pair_index * 2 * HEAD
        query_pair = column_pair(queries, column_start, GROUP)
        key_pair = column_pair(keys_all, column_start, key_total)
        value_pair = column_pair(values_all, column_start, key_total)
        upstream_pair = column_pair(grad_attended, column_start, GROUP)
        scores = pair_scores(query_pair, key_pair, allowed, factor)
        pair_logsum = lax.dynamic_slice_in_dim(logsum, pair_index * 2, 2, 0)
        pair_probs = jnp.exp(scores - pair_logsum)
        weights = pair_probs.astype(jnp.bfloat16)
        grad_weights = jnp.einsum(
            "qhd,khd->hqk", upstream_pair, value_pair, preferred_element_type=jnp.float32
        )
        row_dot = jnp.sum(grad_weights * pair_probs, axis=-1, keepdims=True)
        grad_scores = (pair_probs * (grad_weights - row_dot)).astype(jnp.bfloat16)
        query_part = (
            jnp.einsum("hqk,khd->qhd", grad_scores, key_pair, preferred_element_type=jnp.float32)
            * factor
        )
        key_part = (
            jnp.einsum("hqk,qhd->khd", grad_scores, query_pair, preferred_element_type=jnp.float32)
            * factor
        )
        value_part = jnp.einsum(
            "hqk,qhd->khd", weights, upstream_pair, preferred_element_type=jnp.float32
        )
        grad_queries = lax.dynamic_update_slice_in_dim(
            grad_queries, query_part.reshape(GROUP, 2 * HEAD), column_start, 1
        )
        grad_keys = lax.dynamic_update_slice_in_dim(
            grad_keys, key_part.reshape(key_total, 2 * HEAD), column_start, 1
        )
        grad_values = lax.dynamic_update_slice_in_dim(
            grad_values, value_part.reshape(key_total, 2 * HEAD), column_start, 1
        )
        return (grad_queries, grad_keys, grad_values)

    grad_queries, grad_keys, grad_values = lax.fori_loop(
        0,
        pair_count,
        backward_pair,
        (
            jnp.zeros((GROUP, D), jnp.float32),
            jnp.zeros((key_total, D), jnp.float32),
            jnp.zeros((key_total, D), jnp.float32),
        ),
    )
    key_share, value_share = (
        lax.psum_scatter(
            grad_keys.astype(jnp.bfloat16), "seq", scatter_dimension=0, tiled=True
        ).astype(jnp.float32),
        lax.psum_scatter(
            grad_values.astype(jnp.bfloat16), "seq", scatter_dimension=0, tiled=True
        ).astype(jnp.float32),
    )
    grad_projected = jnp.concatenate(
        [
            grad_queries.astype(jnp.bfloat16),
            key_share.astype(jnp.bfloat16),
            value_share.astype(jnp.bfloat16),
        ],
        axis=1,
    )
    grad_query_add = jnp.sum(grad_projected[:, :D].astype(jnp.float32), axis=0)
    grad_value_add = jnp.sum(grad_projected[:, 2 * D :].astype(jnp.float32), axis=0)
    grad_attend_mat = jnp.einsum(
        "td,te->de", token_rows, grad_projected, preferred_element_type=jnp.float32
    )
    input_grad = grad_hidden + jnp.einsum(
        "te,de->td", grad_projected, attend_mat, preferred_element_type=jnp.float32
    )
    (
        sum_attend_mat,
        sum_query_add,
        sum_value_add,
        sum_output_mat,
        sum_output_add,
        sum_first_scale,
        sum_first_offset,
        sum_inner_mat,
        sum_inner_add,
        sum_outer_mat,
        sum_outer_add,
        sum_second_scale,
        sum_second_offset,
    ) = (
        lax.psum_scatter(grad_attend_mat, ("seq", "dp"), scatter_dimension=0, tiled=True),
        lax.psum_scatter(grad_query_add, ("seq", "dp"), scatter_dimension=0, tiled=True),
        lax.psum_scatter(grad_value_add, ("seq", "dp"), scatter_dimension=0, tiled=True),
        lax.psum_scatter(grad_output_mat, ("seq", "dp"), scatter_dimension=0, tiled=True),
        lax.psum_scatter(grad_output_add, ("seq", "dp"), scatter_dimension=0, tiled=True),
        lax.psum_scatter(grad_first_scale, ("seq", "dp"), scatter_dimension=0, tiled=True),
        lax.psum_scatter(grad_first_offset, ("seq", "dp"), scatter_dimension=0, tiled=True),
        lax.psum_scatter(grad_inner_mat, ("seq", "dp"), scatter_dimension=0, tiled=True),
        lax.psum_scatter(grad_inner_add, ("seq", "dp"), scatter_dimension=0, tiled=True),
        lax.psum_scatter(grad_outer_mat, ("seq", "dp"), scatter_dimension=0, tiled=True),
        lax.psum_scatter(grad_outer_add, ("seq", "dp"), scatter_dimension=0, tiled=True),
        lax.psum_scatter(grad_second_scale, ("seq", "dp"), scatter_dimension=0, tiled=True),
        lax.psum_scatter(grad_second_offset, ("seq", "dp"), scatter_dimension=0, tiled=True),
    )
    return (
        layer_output,
        input_grad.reshape(1, GROUP, D),
        sum_attend_mat,
        sum_query_add,
        sum_value_add,
        sum_output_mat,
        sum_output_add,
        sum_first_scale,
        sum_first_offset,
        sum_inner_mat,
        sum_inner_add,
        sum_outer_mat,
        sum_outer_add,
        sum_second_scale,
        sum_second_offset,
    )


AXES = ("seq", "dp")
DEVICES = 32
WIDE = ((3, 4, 2, 1), (3, 1, 4, 2))
NARROW = ((3, 2, 1, 4), (3, 2, 1, 4))
HINT = pl.CostEstimate(flops=1, bytes_accessed=1, transcendentals=0)
REMOTE = GROUP - 64
ROWS = GROUP + REMOTE


def swap(value, masks):
    pairs = [(i, i ^ masks[i & 1]) for i in range(DEVICES)]
    return lax.ppermute(value, AXES, pairs)


def sync(movers, *values):
    state, values = lax.optimization_barrier(([mover.data for mover in movers], values))
    for mover, data in zip(movers, state):
        mover.data = data
    return values


def stage_masks(order, stage):
    return (1 << order[0][stage], 1 << order[1][stage])


def chip_mask(bits, place):
    return sum(1 << b for t, b in enumerate(bits) if place >> t & 1)


def join_body(cut, *refs):
    sems = refs[-1]
    ins, outs = refs[: len(refs) - 3], refs[len(refs) - 3 : -1]
    copies = []
    for number, out_ref in enumerate(outs):
        width = out_ref.shape[2]
        for side in range(2):
            source = ins[side] if cut else ins[2 * number + side]
            count = source.shape[0]
            if cut:
                source = source.at[:, :, pl.ds(number * cut, width)]
            target = out_ref.at[pl.ds(side * count, count)]
            copies.append(pltpu.make_async_copy(source, target, sems.at[2 * number + side]))
    for copy in copies:
        copy.start()
    for copy in copies:
        copy.wait()


def join(pieces, cut=0):
    count, rows, columns = pieces[0].shape
    widths = (cut, columns - cut) if cut else (columns, pieces[2].shape[2])
    return pl.pallas_call(
        functools.partial(join_body, cut),
        out_shape=[
            jax.ShapeDtypeStruct((2 * count, rows, width), jnp.bfloat16) for width in widths
        ],
        in_specs=[pl.BlockSpec(memory_space=pl.ANY)] * len(pieces),
        out_specs=[pl.BlockSpec(memory_space=pltpu.VMEM)] * 2,
        scratch_shapes=[pltpu.SemaphoreType.DMA((4,))],
        compiler_params=pltpu.CompilerParams(vmem_limit_bytes=16 * 2**20),
        cost_estimate=HINT,
    )(*pieces)


class Gather:
    def __init__(self, me, weights, cut, extra=()):
        self.me, self.cut, self.data = me, cut, {}
        core = me & 1
        both = []
        for side in (core, 1 - core):
            parts = []
            for weight in weights:
                half = weight.shape[1] // 2
                parts.append(lax.dynamic_slice(weight, (0, side * half), (weight.shape[0], half)))
            parts.extend(extra)
            both.append(parts[0] if len(parts) == 1 else jnp.concatenate(parts, axis=1))
        self.data["mine"] = both[0]
        self.data["arrived"] = swap(both[1], (1, 1))

    def depth(self):
        mine, other = self.data["mine"], self.data["arrived"]
        first = (self.me & 1) == 0
        both = jnp.concatenate([jnp.where(first, mine, other), jnp.where(first, other, mine)])
        both = both[None]
        self.data = {"held": both, "arrived": swap(both, stage_masks(WIDE, 0))}

    def step(self, stage):
        held, arrived = self.data["held"], self.data["arrived"]
        if stage == 1:
            held = join([held, arrived], self.cut)
        else:
            held = join([piece for pair in zip(held, arrived) for piece in pair])
        arrived = [
            swap(piece, stage_masks(order, stage)) for piece, order in zip(held, (WIDE, NARROW))
        ]
        self.data = {"held": held, "arrived": arrived}

    def share(self, name, cuts=(0, 1)):
        shared = self.data.setdefault(name + " core", [None, None])
        for cut in cuts:
            shared[cut] = swap(self.data[name][cut], (1, 1))

    def pieces(self):
        names = ("held", "arrived", "held core", "arrived core")
        return [piece for name in names for piece in self.data[name]]


def gather_matmul_body(routes, count, tile, me_ref, left_ref, *refs):
    piece_refs = refs[:8]
    out_refs, product_ref = refs[8 : 8 + count], refs[8 + count]
    mats, in_sems, out_sems = refs[9 + count : 9 + 2 * count], refs[-2], refs[-1]
    me = me_ref[0]
    rows = piece_refs[0].shape[1]
    copies = []
    for number, piece in enumerate(piece_refs):
        chunk, arrived, side = number % 2, number // 2 % 2, number // 4
        order = (WIDE, NARROW)[chunk]
        base = me ^ side
        core = base & 1
        for sub in range(8):
            place = 8 * arrived + sub
            mask = jnp.where(core == 0, chip_mask(order[0], place), chip_mask(order[1], place))
            chip = (base ^ mask) >> 1
            for start, width, mat, begin in routes(chunk, mats):
                half = mat.shape[1] // 2
                target = mat.at[
                    pl.ds(pl.multiple_of(chip * rows, rows), rows),
                    pl.ds(pl.multiple_of(core * half + begin, 128), width),
                ]
                source = piece.at[sub, :, pl.ds(start, width)]
                copies.append(pltpu.make_async_copy(source, target, in_sems.at[len(copies)]))
    for copy in copies:
        copy.start()
    kept = []
    per_side = len(copies) // 2
    for side in range(2):
        core = (me ^ side) & 1
        for copy in copies[side * per_side : (side + 1) * per_side]:
            copy.wait()
        for number, (mat, out_ref) in enumerate(zip(mats, out_refs)):
            half = mat.shape[1] // 2
            columns = pl.ds(pl.multiple_of(core * half, half), half)
            kept.append(
                pltpu.make_async_copy(
                    mat.at[:, columns], out_ref.at[:, columns], out_sems.at[2 * number + side]
                )
            )
            kept[-1].start()
        half = product_ref.shape[1] // 2

        def step(i, carry):
            columns = pl.ds(pl.multiple_of(core * half + i * tile, tile), tile)
            product_ref[:, columns] = jnp.dot(
                left_ref[...], mats[0][:, columns], preferred_element_type=jnp.float32
            )
            return carry

        lax.fori_loop(0, half // tile, step, 0)
    for copy in kept:
        copy.wait()


def gather_matmul(gather, routes, widths, left):
    pieces = gather.pieces()
    depth = pieces[0].shape[1] * DEVICES // 2
    mats = [(depth, width) for width in widths]
    return pl.pallas_call(
        functools.partial(gather_matmul_body, routes, len(widths), 512),
        out_shape=[jax.ShapeDtypeStruct(mat, jnp.bfloat16) for mat in mats]
        + [jax.ShapeDtypeStruct((left.shape[0], widths[0]), jnp.float32)],
        in_specs=[
            pl.BlockSpec(memory_space=pltpu.SMEM),
            pl.BlockSpec(memory_space=pltpu.VMEM),
        ]
        + [pl.BlockSpec(memory_space=pl.ANY)] * 8,
        out_specs=[pl.BlockSpec(memory_space=pl.ANY)] * len(widths)
        + [pl.BlockSpec(memory_space=pltpu.VMEM)],
        scratch_shapes=[pltpu.VMEM(mat, jnp.bfloat16) for mat in mats]
        + [pltpu.SemaphoreType.DMA((96,)), pltpu.SemaphoreType.DMA((2 * len(widths),))],
        compiler_params=pltpu.CompilerParams(vmem_limit_bytes=40 * 2**20),
        cost_estimate=HINT,
    )(gather.me.reshape(1), left, *pieces)


def whole_routes(cut, chunk, outs):
    half = outs[0].shape[1] // 2
    return ((0, (cut, half - cut)[chunk], outs[0], chunk * cut),)


def first_routes(chunk, outs):
    if chunk == 0:
        return ((0, outs[0].shape[1] // 2, outs[0], 0),)
    half = outs[1].shape[1] // 2
    return ((0, half, outs[1], 0), (half, outs[2].shape[1] // 2, outs[2], 0))


def place_of(bits, shard):
    place = shard & 1
    for t, b in enumerate(bits):
        place = place | ((shard >> b) & 1) << (t + 1)
    return place


def weight_grad_body(chunks, tile, me_ref, left_ref, right_ref, *refs):
    extra_refs = refs[: -2 * len(chunks)]
    outs = refs[-2 * len(chunks) :]
    me = me_ref[0]
    rows = outs[0].shape[1]
    half = right_ref.shape[1] // 2
    per_tile = tile // rows

    def step(i, carry):
        left = left_ref[:, pl.ds(pl.multiple_of(i * tile, tile), tile)].T
        for side in (1, 0):
            base = me ^ side
            core = base & 1
            right = right_ref[:, pl.ds(pl.multiple_of(core * half, half), half)]
            product = jnp.dot(left, right, preferred_element_type=jnp.float32).astype(
                jnp.bfloat16
            )
            for sub in range(per_tile):
                number = i * per_tile + sub
                shard = number ^ base
                for which, (order, begin, width) in enumerate(chunks):
                    place = jnp.where(
                        core == 0, place_of(order[0], shard), place_of(order[1], shard)
                    )
                    out_ref = outs[2 * which + side]
                    out_ref[place, :, :width] = product[
                        sub * rows : (sub + 1) * rows, begin : begin + width
                    ]
                    for extra_ref in extra_refs:
                        out_ref[place, :, width:] = extra_ref[number]
        return carry

    lax.fori_loop(0, left_ref.shape[1] // tile, step, 0, unroll=4)


def weight_grad(left, right, me, chunks, extra=()):
    depth = left.shape[1]
    rows = depth // DEVICES
    more = sum(e.shape[2] for e in extra)
    shapes = [
        jax.ShapeDtypeStruct((DEVICES, rows, width + more), jnp.bfloat16)
        for _, _, width in chunks
        for _ in range(2)
    ]
    outs = pl.pallas_call(
        functools.partial(weight_grad_body, chunks, 256),
        out_shape=shapes,
        in_specs=[pl.BlockSpec(memory_space=pltpu.SMEM)]
        + [pl.BlockSpec(memory_space=pltpu.VMEM)] * (2 + len(extra)),
        out_specs=[pl.BlockSpec(memory_space=pltpu.VMEM)] * len(shapes),
        compiler_params=pltpu.CompilerParams(vmem_limit_bytes=24 * 2**20),
        cost_estimate=HINT,
    )(me.reshape(1), left, right, *extra)
    return [tuple(outs[i : i + 2]) for i in range(0, len(outs), 2)]


def add_low(one, two):
    return (one.astype(jnp.float32) + two.astype(jnp.float32)).astype(jnp.bfloat16)


def halve_body(*refs):
    count = len(refs) // 6
    for which in range(count):
        held_low, held_high, low, high = refs[4 * which : 4 * which + 4]
        keep_ref, send_ref = refs[4 * count + 2 * which : 4 * count + 2 * which + 2]
        send_ref[...] = add_low(held_high[...], high[...])
        keep_ref[...] = add_low(held_low[...], low[...])


def halve(pairs):
    half = pairs[0][0].shape[0] // 2
    block = max(half // 4, 1)
    steps = half // block
    specs, outs, shapes, values = [], [], [], []
    for held, arrived in pairs:
        _, rows, columns = held.shape
        low = pl.BlockSpec((block, rows, columns), lambda i: (i, 0, 0))
        high = pl.BlockSpec((block, rows, columns), lambda i: (steps + i, 0, 0))
        specs += [low, high, low, high]
        outs += [low, low]
        shapes += [jax.ShapeDtypeStruct((half, rows, columns), jnp.bfloat16)] * 2
        values += [held, held, arrived, arrived]
    results = pl.pallas_call(
        halve_body,
        grid=(steps,),
        in_specs=specs,
        out_specs=outs,
        out_shape=shapes,
        compiler_params=pltpu.CompilerParams(vmem_limit_bytes=16 * 2**20),
        cost_estimate=HINT,
    )(*values)
    return results[0::2], results[1::2]


def first_norm_body(
    rows_ref, mixed_ref, matrix_ref, add_ref, gain_ref, shift_ref, low_ref, out_ref, normed_ref, inverse_ref
):
    branch = jnp.dot(mixed_ref[...], matrix_ref[...], preferred_element_type=jnp.float32)
    out, normed, inverse = norm_forward(
        rows_ref[...].astype(jnp.float32) + (branch + add_ref[...]), gain_ref[...], shift_ref[...]
    )
    low_ref[...] = out.astype(jnp.bfloat16)
    out_ref[...] = out
    normed_ref[...] = normed
    inverse_ref[...] = inverse


def first_norm(rows, mixed, matrix, add, gain, shift):
    block = 128
    tall = pl.BlockSpec((block, D), lambda i: (i, 0))
    whole = pl.BlockSpec((1, D), lambda i: (0, 0))
    return pl.pallas_call(
        first_norm_body,
        grid=(GROUP // block,),
        in_specs=[tall, tall, pl.BlockSpec((D, D), lambda i: (0, 0)), whole, whole, whole],
        out_specs=[tall, tall, tall, pl.BlockSpec((block, 1), lambda i: (i, 0))],
        out_shape=[
            jax.ShapeDtypeStruct((GROUP, D), jnp.bfloat16),
            jax.ShapeDtypeStruct((GROUP, D), jnp.float32),
            jax.ShapeDtypeStruct((GROUP, D), jnp.float32),
            jax.ShapeDtypeStruct((GROUP, 1), jnp.float32),
        ],
        compiler_params=pltpu.CompilerParams(vmem_limit_bytes=20 * 2**20),
        cost_estimate=HINT,
    )(rows, mixed, matrix, add, gain, shift)


def rows_back_body(grad_ref, matrix_ref, near_ref, far_ref):
    product = lax.dot_general(
        grad_ref[...],
        matrix_ref[...],
        (((1,), (1,)), ((), ())),
        preferred_element_type=jnp.float32,
    )
    near_ref[...] = product[:GROUP]
    far_ref[...] = product[GROUP:].astype(jnp.bfloat16)


def rows_back(grad, matrix):
    return pl.pallas_call(
        rows_back_body,
        grid=(4,),
        in_specs=[
            pl.BlockSpec((ROWS, 3 * D), lambda i: (0, 0)),
            pl.BlockSpec((D // 4, 3 * D), lambda i: (i, 0)),
        ],
        out_specs=[
            pl.BlockSpec((GROUP, D // 4), lambda i: (0, i)),
            pl.BlockSpec((REMOTE, D // 4), lambda i: (0, i)),
        ],
        out_shape=[
            jax.ShapeDtypeStruct((GROUP, D), jnp.float32),
            jax.ShapeDtypeStruct((REMOTE, D), jnp.bfloat16),
        ],
        compiler_params=pltpu.CompilerParams(vmem_limit_bytes=16 * 2**20),
        cost_estimate=HINT,
    )(grad, matrix)


def cut_grads(me, left, right, cut):
    half = right.shape[1] // 2
    return weight_grad(left, right, me, ((WIDE, 0, cut), (NARROW, cut, half - cut)))


class Scatter:
    def __init__(self, me, grads):
        self.me, self.stage = me, 4
        self.data = {"held": [keep for keep, _ in grads], "send": [send for _, send in grads]}

    def begin(self):
        self.data["arrived"] = [swap(piece, (1, 1)) for piece in self.data.pop("send")]

    def step(self):
        self.stage -= 1
        held, send = halve(list(zip(self.data["held"], self.data["arrived"])))
        if self.stage == 0:
            held, send = jnp.concatenate(held, axis=2), jnp.concatenate(send, axis=2)
            arrived = swap(send, stage_masks(WIDE, 0))
        else:
            arrived = [
                swap(piece, stage_masks(order, self.stage))
                for piece, order in zip(send, (WIDE, NARROW))
            ]
        self.data = {"held": held, "arrived": arrived}

    def near(self):
        held, arrived = self.data["held"], self.data["arrived"]
        send = add_low(held[1], arrived[1])
        held = held[0].astype(jnp.float32) + arrived[0].astype(jnp.float32)
        self.data = {"held": held, "arrived": swap(send, (1, 1))}

    def result(self):
        held, arrived = self.data["held"], self.data["arrived"].astype(jnp.float32)
        first = (self.me & 1) == 0
        return jnp.where(first, held, arrived), jnp.where(first, arrived, held)


def masked_pair(keys):
    first = lax.broadcasted_iota(jnp.int32, keys.shape, 1) < HEAD
    zeros = jnp.zeros_like(keys)
    return jnp.where(first, keys, zeros), jnp.where(first, zeros, keys)


PAIRS = 2
WIDTH = PAIRS * 128
STEPS = D // WIDTH


def attend_forward_body(query_docs, key_docs, query_ref, key_ref, value_ref, mixed_ref, log_ref):
    allowed = key_docs[...] == query_docs[...]
    for pair in range(PAIRS):
        columns = slice(pair * 128, (pair + 1) * 128)
        queries = query_ref[:, columns]
        value_rows = value_ref[:, columns].T
        results = []
        for head, keys in enumerate(masked_pair(key_ref[:, columns])):
            raw = lax.dot_general(
                keys, queries, (((1,), (1,)), ((), ())), preferred_element_type=jnp.float32
            )
            scores = jnp.where(allowed, raw * HEAD**-0.5, masked_score)
            peak = jnp.max(scores, axis=0, keepdims=True)
            terms = jnp.exp(scores - peak)
            total = jnp.sum(terms, axis=0, keepdims=True)
            weights = (terms * (1.0 / total)).astype(jnp.bfloat16)
            results.append(
                jnp.dot(
                    value_rows[head * HEAD : (head + 1) * HEAD],
                    weights,
                    preferred_element_type=jnp.float32,
                )
            )
            log_ref[pair, head : head + 1] = peak + jnp.log(total)
        mixed_ref[:, columns] = jnp.concatenate(results).T.astype(jnp.bfloat16)


def attend_specs():
    return [
        pl.BlockSpec((1, GROUP), lambda i: (0, 0)),
        pl.BlockSpec((ROWS, 1), lambda i: (0, 0)),
        pl.BlockSpec((GROUP, WIDTH), lambda i: (0, i)),
        pl.BlockSpec((ROWS, WIDTH), lambda i: (0, STEPS + i)),
        pl.BlockSpec((ROWS, WIDTH), lambda i: (0, 2 * STEPS + i)),
    ]


def attend_forward(query_docs, key_docs, projected):
    return pl.pallas_call(
        attend_forward_body,
        grid=(STEPS,),
        in_specs=attend_specs(),
        out_specs=[
            pl.BlockSpec((GROUP, WIDTH), lambda i: (0, i)),
            pl.BlockSpec((PAIRS, 2, GROUP), lambda i: (i, 0, 0)),
        ],
        out_shape=[
            jax.ShapeDtypeStruct((GROUP, D), jnp.bfloat16),
            jax.ShapeDtypeStruct((HEADS // 2, 2, GROUP), jnp.float32),
        ],
        compiler_params=pltpu.CompilerParams(vmem_limit_bytes=16 * 2**20),
        cost_estimate=HINT,
    )(query_docs, key_docs, projected, projected, projected)


def attend_backward_body(
    query_docs, key_docs, query_ref, key_ref, value_ref, upstream_ref, log_ref, grad_ref, sum_ref
):
    allowed = key_docs[...] == query_docs[...]
    across = (((1,), (1,)), ((), ()))
    wide = lax.broadcasted_iota(jnp.int32, (ROWS, 128), 1) < HEAD
    for pair in range(PAIRS):
        columns = slice(pair * 128, (pair + 1) * 128)
        queries, upstream = query_ref[:, columns], upstream_ref[:, columns]
        key_rows = key_ref[:, columns].T
        pairs = zip(masked_pair(key_ref[:, columns]), masked_pair(value_ref[:, columns]))
        query_parts, key_parts, value_parts = [], [], []
        for head, (keys, values) in enumerate(pairs):
            raw = lax.dot_general(keys, queries, across, preferred_element_type=jnp.float32)
            scores = jnp.where(allowed, raw * HEAD**-0.5, masked_score)
            probs = jnp.exp(scores - log_ref[pair, head : head + 1])
            grad_weights = lax.dot_general(
                values, upstream, across, preferred_element_type=jnp.float32
            )
            row_dot = jnp.sum(grad_weights * probs, axis=0, keepdims=True)
            grad_scores = (probs * (grad_weights - row_dot)).astype(jnp.bfloat16)
            weights = probs.astype(jnp.bfloat16)
            query_parts.append(
                jnp.dot(
                    key_rows[head * HEAD : (head + 1) * HEAD],
                    grad_scores,
                    preferred_element_type=jnp.float32,
                )
            )
            key_parts.append(jnp.dot(grad_scores, queries, preferred_element_type=jnp.float32))
            value_parts.append(jnp.dot(weights, upstream, preferred_element_type=jnp.float32))
        grad_queries = (jnp.concatenate(query_parts).T * HEAD**-0.5).astype(jnp.bfloat16)
        grad_keys = jnp.where(wide, key_parts[0], key_parts[1]) * HEAD**-0.5
        grad_values = jnp.where(wide, value_parts[0], value_parts[1]).astype(jnp.bfloat16)
        start = pl.program_id(0) * WIDTH + pair * 128
        query_at, key_at, value_at = (
            pl.ds(pl.multiple_of(start + part * D, 128), 128) for part in range(3)
        )
        grad_ref[:GROUP, query_at] = grad_queries
        grad_ref[GROUP:, query_at] = jnp.zeros((REMOTE, 128), jnp.bfloat16)
        grad_ref[:, key_at] = grad_keys.astype(jnp.bfloat16)
        grad_ref[:, value_at] = grad_values
        low = grad_queries.astype(jnp.float32)
        sum_ref[0, :, query_at] = jnp.sum(low, axis=0, keepdims=True)
        low = grad_values.astype(jnp.float32)
        sum_ref[1, :, query_at] = jnp.sum(low, axis=0, keepdims=True)


def attend_backward(query_docs, key_docs, projected, upstream, logs):
    return pl.pallas_call(
        attend_backward_body,
        grid=(STEPS,),
        in_specs=attend_specs()
        + [
            pl.BlockSpec((GROUP, WIDTH), lambda i: (0, i)),
            pl.BlockSpec((PAIRS, 2, GROUP), lambda i: (i, 0, 0)),
        ],
        out_specs=[
            pl.BlockSpec((ROWS, 3 * D), lambda i: (0, 0)),
            pl.BlockSpec((2, 1, D), lambda i: (0, 0, 0)),
        ],
        out_shape=[
            jax.ShapeDtypeStruct((ROWS, 3 * D), jnp.bfloat16),
            jax.ShapeDtypeStruct((2, 1, D), jnp.float32),
        ],
        compiler_params=pltpu.CompilerParams(vmem_limit_bytes=16 * 2**20),
        cost_estimate=HINT,
    )(query_docs, key_docs, projected, projected, projected, upstream, logs)


def pack_shard(vectors):
    rows = jnp.concatenate([vector.reshape(-1, 32) for vector in vectors])
    return jnp.pad(rows, ((0, 32 - rows.shape[0]), (0, 96)))


def unpack_shards(packed):
    rows = packed.reshape(DEVICES, 32, 256)[:, :12, :32].astype(jnp.float32)
    short = rows[:, :8].transpose(1, 0, 2).reshape(8, 1, D)
    return [short[i] for i in range(8)] + [rows[:, 8:].reshape(1, 4 * D)]


def pack_grads(short, long):
    rows = jnp.concatenate([vector.reshape(1, 8, 128) for vector in short])
    rows = jnp.repeat(rows.transpose(1, 0, 2), 4, axis=0)
    rows = jnp.concatenate([rows, long.reshape(DEVICES, 1, 128)], axis=1)
    return jnp.pad(rows, ((0, 0), (0, 23), (0, 0))).astype(jnp.bfloat16)


def fast_local(
    tokens,
    cotangent,
    doc_lengths,
    attend_weight,
    query_bias,
    value_bias,
    output_weight,
    output_bias,
    first_gain,
    first_shift,
    inner_weight,
    inner_bias,
    outer_weight,
    outer_bias,
    second_gain,
    second_shift,
):
    me = lax.axis_index(AXES)
    group_index = me >> 4
    small_shard = pack_shard(
        [
            query_bias,
            value_bias,
            output_bias,
            first_gain,
            first_shift,
            outer_bias,
            second_gain,
            second_shift,
            inner_bias,
        ]
    )
    attend_cut, inner_cut, outer_cut = 3 * D // 2, 1408, 384
    one = Gather(me, (attend_weight, output_weight), attend_cut, (small_shard,))
    sync((one,))

    one.depth()
    two = Gather(me, (inner_weight,), inner_cut)
    three = Gather(me, (outer_weight,), outer_cut)
    movers = (one, two, three)
    doc_ends = jnp.cumsum(doc_lengths[0])
    near_at = group_index * GROUP + lax.iota(jnp.int32, GROUP)
    far_at = jnp.where(group_index == 0, GROUP, 64) + lax.iota(jnp.int32, REMOTE)
    row_at = jnp.concatenate([near_at, far_at])
    row_docs = jnp.sum((row_at[:, None] >= doc_ends[None, :]).astype(jnp.int32), axis=1)
    query_docs, key_docs = row_docs[None, :GROUP], row_docs[:, None]
    near = tokens.reshape(GROUP, D)
    query_docs, key_docs, near = sync(movers, query_docs, key_docs, near)

    one.step(1)
    two.depth()
    far = lax.dynamic_slice(near, (64 * (1 - group_index), 0), (REMOTE, D))
    far = lax.ppermute(far, "seq", [(0, 1), (1, 0)])
    (far,) = sync((one, two), far)

    one.step(2)
    token_rows = jnp.concatenate([near, far])
    (token_rows,) = sync((one, two), token_rows)

    one.step(3)
    two.step(1)
    three.depth()
    sync(movers)

    one.share("held")
    one.share("arrived")
    sync((one,))

    two.step(2)
    three.step(1)
    attend_mat, output_mat, small_all, projected = gather_matmul(
        one, first_routes, (3 * D, D, 256), token_rows
    )
    (
        query_add,
        value_add,
        output_add,
        first_scale,
        first_offset,
        outer_add,
        second_scale,
        second_offset,
        inner_add,
    ) = unpack_shards(small_all)
    bias_row = jnp.concatenate([query_add, jnp.zeros((1, D), jnp.float32), value_add], axis=1)
    projected = (projected + bias_row).astype(jnp.bfloat16)
    (projected,) = sync((two, three), projected)

    two.step(3)
    two.share("held", (0,))
    three.step(2)
    attended, logs = attend_forward(query_docs, key_docs, projected)
    first_low, first_out, first_normed, first_inverse = first_norm(
        near, attended, output_mat, output_add, first_scale, first_offset
    )
    first_out, first_normed, first_inverse, first_low = sync(
        (two, three), first_out, first_normed, first_inverse, first_low
    )

    two.share("held", (1,))
    two.share("arrived")
    sync((two,))

    three.step(3)
    three.share("held")
    inner_mat, pre_act = gather_matmul(
        two, functools.partial(whole_routes, inner_cut), (4 * D,), first_low
    )
    pre_act = pre_act + inner_add
    cdf = 0.5 * (1.0 + lax.erf(pre_act * 0.5**0.5))
    gelu_slope = cdf + pre_act * jnp.exp(-0.5 * pre_act * pre_act) * 0.3989422804014327
    activated = (pre_act * cdf).astype(jnp.bfloat16)
    activated, gelu_slope = sync((three,), activated, gelu_slope)

    three.share("arrived")
    outer_mat, mlp_out = gather_matmul(
        three, functools.partial(whole_routes, outer_cut), (D,), activated
    )
    mlp_out = mlp_out + outer_add
    second_out, second_normed, second_inverse = norm_forward(
        first_out + mlp_out, second_scale, second_offset
    )
    layer_output = second_out.astype(jnp.bfloat16).reshape(1, GROUP, D)
    upstream = cotangent.reshape(GROUP, D).astype(jnp.float32)
    grad_two = norm_backward(upstream, second_normed, second_inverse, second_scale)
    grad_mlp = grad_two.astype(jnp.bfloat16)
    outer = Scatter(me, cut_grads(me, activated, grad_mlp, outer_cut))
    grad_mlp, grad_two, second_normed = sync((outer,), grad_mlp, grad_two, second_normed)

    outer.begin()
    grad_act = jnp.einsum("td,fd->tf", grad_mlp, outer_mat, preferred_element_type=jnp.float32)
    grad_pre = (grad_act * gelu_slope).astype(jnp.bfloat16)
    inner_sum = jnp.sum(grad_pre.astype(jnp.float32), axis=0)
    grad_pre, inner_sum, grad_mlp, second_normed = sync(
        (outer,), grad_pre, inner_sum, grad_mlp, second_normed
    )

    outer.step()
    inner = Scatter(me, cut_grads(me, first_low, grad_pre, inner_cut))
    second_sums = (
        jnp.sum(grad_mlp.astype(jnp.float32), axis=0),
        jnp.sum(upstream * second_normed, axis=0),
        jnp.sum(upstream, axis=0),
    )
    grad_first = (
        jnp.einsum("tf,df->td", grad_pre, inner_mat, preferred_element_type=jnp.float32) + grad_two
    )
    grad_hidden = norm_backward(grad_first, first_normed, first_inverse, first_scale)
    grad_branch = grad_hidden.astype(jnp.bfloat16)
    first_sums = (
        jnp.sum(grad_branch.astype(jnp.float32), axis=0),
        jnp.sum(grad_first * first_normed, axis=0),
        jnp.sum(grad_first, axis=0),
    )
    grad_attended = jnp.einsum(
        "te,de->td", grad_branch, output_mat, preferred_element_type=jnp.float32
    ).astype(jnp.bfloat16)
    first_sums, second_sums, grad_hidden, grad_branch, grad_attended = sync(
        (outer, inner), first_sums, second_sums, grad_hidden, grad_branch, grad_attended
    )

    inner.begin()
    outer.step()
    grad_projected, row_sums = attend_backward(
        query_docs, key_docs, projected, grad_attended, logs
    )
    grad_projected, row_sums = sync((outer, inner), grad_projected, row_sums)

    inner.step()
    outer.step()
    small = pack_grads([row_sums[0, 0], row_sums[1, 0], *first_sums, *second_sums], inner_sum)
    first = Scatter(
        me,
        weight_grad(token_rows, grad_projected, me, ((WIDE, 0, attend_cut),))
        + weight_grad(attended, grad_branch, me, ((NARROW, 0, D // 2),), (small,)),
    )
    movers = (outer, inner, first)
    sync(movers)

    first.begin()
    inner.step()
    outer.step()
    row_grad, far_grad = rows_back(grad_projected, attend_mat)
    row_grad, far_grad = sync(movers, row_grad, far_grad)

    first.step()
    inner.step()
    outer.near()
    sync(movers)

    first.step()
    inner.step()
    sum_outer_mat = jnp.concatenate(outer.result(), axis=1)
    (sum_outer_mat,) = sync((inner, first), sum_outer_mat)

    first.step()
    inner.near()
    (far_grad,) = sync((inner, first), far_grad)

    first.step()
    far_grad = lax.ppermute(far_grad, "seq", [(0, 1), (1, 0)])
    sum_inner_mat = jnp.concatenate(inner.result(), axis=1)
    sum_inner_mat, far_grad = sync((first,), sum_inner_mat, far_grad)

    first.near()
    filler = jnp.zeros((64, D), jnp.float32)
    far_grad = far_grad.astype(jnp.float32)
    far_grad = jnp.where(
        group_index == 0,
        jnp.concatenate([filler, far_grad]),
        jnp.concatenate([far_grad, filler]),
    )
    input_grad = grad_hidden + row_grad + far_grad
    halves = first.result()
    output_end = attend_cut + D // 2
    sum_attend_mat = jnp.concatenate([half[:, :attend_cut] for half in halves], axis=1)
    sum_output_mat = jnp.concatenate([half[:, attend_cut:output_end] for half in halves], axis=1)
    small_rows = halves[0][:, output_end:]
    own = lax.dynamic_slice(small_rows, (0, 32 * (me & 3)), (8, 32))
    (
        sum_query_add,
        sum_value_add,
        sum_output_add,
        sum_first_scale,
        sum_first_offset,
        sum_outer_add,
        sum_second_scale,
        sum_second_offset,
    ) = (own[i] for i in range(8))
    sum_inner_add = small_rows[8]
    return (
        layer_output,
        input_grad.reshape(1, GROUP, D),
        sum_attend_mat,
        sum_query_add,
        sum_value_add,
        sum_output_mat,
        sum_output_add,
        sum_first_scale,
        sum_first_offset,
        sum_inner_mat,
        sum_inner_add,
        sum_outer_mat,
        sum_outer_add,
        sum_second_scale,
        sum_second_offset,
    )


def solution(mesh):
    sizes = (mesh.shape["seq"], mesh.shape["dp"])
    return jax.shard_map(
        fast_local if sizes == (2, 16) else general_local,
        mesh=mesh,
        in_specs=(
            P("dp", "seq", None),
            P("dp", "seq", None),
            P("dp", None),
            P(("seq", "dp"), None),
            P(("seq", "dp")),
            P(("seq", "dp")),
            P(("seq", "dp"), None),
            P(("seq", "dp")),
            P(("seq", "dp")),
            P(("seq", "dp")),
            P(("seq", "dp"), None),
            P(("seq", "dp")),
            P(("seq", "dp"), None),
            P(("seq", "dp")),
            P(("seq", "dp")),
            P(("seq", "dp")),
        ),
        out_specs=(
            P("dp", "seq", None),
            P("dp", "seq", None),
            P(("seq", "dp"), None),
            P(("seq", "dp")),
            P(("seq", "dp")),
            P(("seq", "dp"), None),
            P(("seq", "dp")),
            P(("seq", "dp")),
            P(("seq", "dp")),
            P(("seq", "dp"), None),
            P(("seq", "dp")),
            P(("seq", "dp"), None),
            P(("seq", "dp")),
            P(("seq", "dp")),
            P(("seq", "dp")),
        ),
        check_vma=False,
    )
```

```python
import functools

import jax
import jax.numpy as jnp
from jax import lax
from jax.experimental import pallas as pl
from jax.experimental.pallas import tpu as pltpu
from jax.sharding import PartitionSpec as P

D = 1024
HEADS = 16
HEAD = 64
GROUP = 256


epsilon = 1e-12
masked_score = -1e30


def norm_forward(value, gain, shift):
    mean_value = jnp.mean(value, axis=-1, keepdims=True)
    center = value - mean_value
    inverse = lax.rsqrt(jnp.mean(center * center, axis=-1, keepdims=True) + epsilon)
    normed = center * inverse
    return (normed * gain + shift, normed, inverse)


def norm_backward(upstream, normed, inverse, gain):
    scaled = upstream * gain
    first_mean = jnp.mean(scaled, axis=-1, keepdims=True)
    second_mean = jnp.mean(scaled * normed, axis=-1, keepdims=True)
    return inverse * (scaled - first_mean - normed * second_mean)


def exact_gelu(value):
    return jax.nn.gelu(value, approximate=False)


def pair_scores(query_pair, key_pair, allowed, factor):
    raw = (
        jnp.einsum("qhd,khd->hqk", query_pair, key_pair, preferred_element_type=jnp.float32)
        * factor
    )
    return jnp.where(allowed[None], raw, masked_score)


def column_pair(matrix, column_start, row_count):
    return lax.dynamic_slice_in_dim(matrix, column_start, 2 * HEAD, 1).reshape(row_count, 2, HEAD)


def general_local(
    tokens,
    cotangent,
    doc_lengths,
    attend_weight,
    query_bias,
    value_bias,
    output_weight,
    output_bias,
    first_gain,
    first_shift,
    inner_weight,
    inner_bias,
    outer_weight,
    outer_bias,
    second_gain,
    second_shift,
):
    (
        attend_mat,
        query_add,
        value_add,
        output_mat,
        output_add,
        first_scale,
        first_offset,
        inner_mat,
        inner_add,
        outer_mat,
        outer_add,
        second_scale,
        second_offset,
    ) = (
        lax.all_gather(attend_weight, ("seq", "dp"), axis=0, tiled=True),
        lax.all_gather(query_bias, ("seq", "dp"), axis=0, tiled=True),
        lax.all_gather(value_bias, ("seq", "dp"), axis=0, tiled=True),
        lax.all_gather(output_weight, ("seq", "dp"), axis=0, tiled=True),
        lax.all_gather(output_bias, ("seq", "dp"), axis=0, tiled=True),
        lax.all_gather(first_gain, ("seq", "dp"), axis=0, tiled=True),
        lax.all_gather(first_shift, ("seq", "dp"), axis=0, tiled=True),
        lax.all_gather(inner_weight, ("seq", "dp"), axis=0, tiled=True),
        lax.all_gather(inner_bias, ("seq", "dp"), axis=0, tiled=True),
        lax.all_gather(outer_weight, ("seq", "dp"), axis=0, tiled=True),
        lax.all_gather(outer_bias, ("seq", "dp"), axis=0, tiled=True),
        lax.all_gather(second_gain, ("seq", "dp"), axis=0, tiled=True),
        lax.all_gather(second_shift, ("seq", "dp"), axis=0, tiled=True),
    )
    token_rows = tokens.reshape(GROUP, D)
    key_total = GROUP * lax.axis_size("seq")
    group_index = lax.axis_index("seq")
    doc_ends = jnp.cumsum(doc_lengths[0])
    positions = lax.iota(jnp.int32, key_total)
    key_docs = jnp.sum((positions[:, None] >= doc_ends[None, :]).astype(jnp.int32), axis=1)
    query_docs = lax.dynamic_slice_in_dim(key_docs, group_index * GROUP, GROUP)
    allowed = query_docs[:, None] == key_docs[None, :]
    factor = HEAD ** (-0.5)
    pair_count = HEADS // 2
    bias_row = jnp.concatenate(
        [query_add.astype(jnp.float32), jnp.zeros((D,), jnp.float32), value_add.astype(jnp.float32)]
    )
    projected = jnp.dot(token_rows, attend_mat, preferred_element_type=jnp.float32) + bias_row
    queries = projected[:, :D].astype(jnp.bfloat16)
    keys_mine = projected[:, D : 2 * D].astype(jnp.bfloat16)
    values_mine = projected[:, 2 * D :].astype(jnp.bfloat16)
    keys_all, values_all = (
        lax.all_gather(keys_mine, "seq", axis=0, tiled=True),
        lax.all_gather(values_mine, "seq", axis=0, tiled=True),
    )

    def forward_pair(pair_index, state_tuple):
        mixed_heads, logsum = state_tuple
        column_start = pair_index * 2 * HEAD
        query_pair = column_pair(queries, column_start, GROUP)
        key_pair = column_pair(keys_all, column_start, key_total)
        value_pair = column_pair(values_all, column_start, key_total)
        scores = pair_scores(query_pair, key_pair, allowed, factor)
        row_peak = jnp.max(scores, axis=-1, keepdims=True)
        expo_terms = jnp.exp(scores - row_peak)
        row_total = jnp.sum(expo_terms, axis=-1, keepdims=True)
        weights = (expo_terms / row_total).astype(jnp.bfloat16)
        result = jnp.einsum(
            "hqk,khd->qhd", weights, value_pair, preferred_element_type=jnp.float32
        ).reshape(GROUP, 2 * HEAD)
        mixed_heads = lax.dynamic_update_slice_in_dim(mixed_heads, result, column_start, 1)
        logsum = lax.dynamic_update_slice_in_dim(
            logsum, row_peak + jnp.log(row_total), pair_index * 2, 0
        )
        return (mixed_heads, logsum)

    mixed_heads, logsum = lax.fori_loop(
        0,
        pair_count,
        forward_pair,
        (jnp.zeros((GROUP, D), jnp.float32), jnp.zeros((HEADS, GROUP, 1), jnp.float32)),
    )
    attended = mixed_heads.astype(jnp.bfloat16)
    branch = jnp.dot(attended, output_mat, preferred_element_type=jnp.float32) + output_add.astype(
        jnp.float32
    )
    first_out, first_normed, first_inverse = norm_forward(
        token_rows.astype(jnp.float32) + branch,
        first_scale.astype(jnp.float32),
        first_offset.astype(jnp.float32),
    )
    first_low = first_out.astype(jnp.bfloat16)
    pre_act = jnp.dot(first_low, inner_mat, preferred_element_type=jnp.float32) + inner_add.astype(
        jnp.float32
    )
    activated = exact_gelu(pre_act).astype(jnp.bfloat16)
    mlp_out = jnp.dot(activated, outer_mat, preferred_element_type=jnp.float32) + outer_add.astype(
        jnp.float32
    )
    second_out, second_normed, second_inverse = norm_forward(
        first_out + mlp_out, second_scale.astype(jnp.float32), second_offset.astype(jnp.float32)
    )
    layer_output = second_out.astype(jnp.bfloat16).reshape(1, GROUP, D)
    (
        attend_mat,
        query_add,
        value_add,
        output_mat,
        output_add,
        first_scale,
        first_offset,
        inner_mat,
        inner_add,
        outer_mat,
        outer_add,
        second_scale,
        second_offset,
    ) = (
        lax.all_gather(attend_weight, ("seq", "dp"), axis=0, tiled=True),
        lax.all_gather(query_bias, ("seq", "dp"), axis=0, tiled=True),
        lax.all_gather(value_bias, ("seq", "dp"), axis=0, tiled=True),
        lax.all_gather(output_weight, ("seq", "dp"), axis=0, tiled=True),
        lax.all_gather(output_bias, ("seq", "dp"), axis=0, tiled=True),
        lax.all_gather(first_gain, ("seq", "dp"), axis=0, tiled=True),
        lax.all_gather(first_shift, ("seq", "dp"), axis=0, tiled=True),
        lax.all_gather(inner_weight, ("seq", "dp"), axis=0, tiled=True),
        lax.all_gather(inner_bias, ("seq", "dp"), axis=0, tiled=True),
        lax.all_gather(outer_weight, ("seq", "dp"), axis=0, tiled=True),
        lax.all_gather(outer_bias, ("seq", "dp"), axis=0, tiled=True),
        lax.all_gather(second_gain, ("seq", "dp"), axis=0, tiled=True),
        lax.all_gather(second_shift, ("seq", "dp"), axis=0, tiled=True),
    )
    upstream = cotangent.reshape(GROUP, D).astype(jnp.float32)
    grad_second_scale = jnp.sum(upstream * second_normed, axis=0)
    grad_second_offset = jnp.sum(upstream, axis=0)
    grad_two = norm_backward(
        upstream, second_normed, second_inverse, second_scale.astype(jnp.float32)
    )
    grad_mlp = grad_two.astype(jnp.bfloat16)
    grad_outer_add = jnp.sum(grad_mlp.astype(jnp.float32), axis=0)
    grad_outer_mat = jnp.einsum(
        "tf,td->fd", activated, grad_mlp, preferred_element_type=jnp.float32
    )
    grad_act = jnp.einsum("td,fd->tf", grad_mlp, outer_mat, preferred_element_type=jnp.float32)
    unused_value, gelu_pull = jax.vjp(exact_gelu, pre_act)
    grad_pre = gelu_pull(grad_act)[0].astype(jnp.bfloat16)
    grad_inner_add = jnp.sum(grad_pre.astype(jnp.float32), axis=0)
    grad_inner_mat = jnp.einsum(
        "td,tf->df", first_low, grad_pre, preferred_element_type=jnp.float32
    )
    grad_first = (
        jnp.einsum("tf,df->td", grad_pre, inner_mat, preferred_element_type=jnp.float32) + grad_two
    )
    grad_first_scale = jnp.sum(grad_first * first_normed, axis=0)
    grad_first_offset = jnp.sum(grad_first, axis=0)
    grad_hidden = norm_backward(
        grad_first, first_normed, first_inverse, first_scale.astype(jnp.float32)
    )
    grad_branch = grad_hidden.astype(jnp.bfloat16)
    grad_output_add = jnp.sum(grad_branch.astype(jnp.float32), axis=0)
    grad_output_mat = jnp.einsum(
        "td,te->de", attended, grad_branch, preferred_element_type=jnp.float32
    )
    grad_attended = jnp.einsum(
        "te,de->td", grad_branch, output_mat, preferred_element_type=jnp.float32
    ).astype(jnp.bfloat16)

    def backward_pair(pair_index, state_tuple):
        grad_queries, grad_keys, grad_values = state_tuple
        column_start = pair_index * 2 * HEAD
        query_pair = column_pair(queries, column_start, GROUP)
        key_pair = column_pair(keys_all, column_start, key_total)
        value_pair = column_pair(values_all, column_start, key_total)
        upstream_pair = column_pair(grad_attended, column_start, GROUP)
        scores = pair_scores(query_pair, key_pair, allowed, factor)
        pair_logsum = lax.dynamic_slice_in_dim(logsum, pair_index * 2, 2, 0)
        pair_probs = jnp.exp(scores - pair_logsum)
        weights = pair_probs.astype(jnp.bfloat16)
        grad_weights = jnp.einsum(
            "qhd,khd->hqk", upstream_pair, value_pair, preferred_element_type=jnp.float32
        )
        row_dot = jnp.sum(grad_weights * pair_probs, axis=-1, keepdims=True)
        grad_scores = (pair_probs * (grad_weights - row_dot)).astype(jnp.bfloat16)
        query_part = (
            jnp.einsum("hqk,khd->qhd", grad_scores, key_pair, preferred_element_type=jnp.float32)
            * factor
        )
        key_part = (
            jnp.einsum("hqk,qhd->khd", grad_scores, query_pair, preferred_element_type=jnp.float32)
            * factor
        )
        value_part = jnp.einsum(
            "hqk,qhd->khd", weights, upstream_pair, preferred_element_type=jnp.float32
        )
        grad_queries = lax.dynamic_update_slice_in_dim(
            grad_queries, query_part.reshape(GROUP, 2 * HEAD), column_start, 1
        )
        grad_keys = lax.dynamic_update_slice_in_dim(
            grad_keys, key_part.reshape(key_total, 2 * HEAD), column_start, 1
        )
        grad_values = lax.dynamic_update_slice_in_dim(
            grad_values, value_part.reshape(key_total, 2 * HEAD), column_start, 1
        )
        return (grad_queries, grad_keys, grad_values)

    grad_queries, grad_keys, grad_values = lax.fori_loop(
        0,
        pair_count,
        backward_pair,
        (
            jnp.zeros((GROUP, D), jnp.float32),
            jnp.zeros((key_total, D), jnp.float32),
            jnp.zeros((key_total, D), jnp.float32),
        ),
    )
    key_share, value_share = (
        lax.psum_scatter(
            grad_keys.astype(jnp.bfloat16), "seq", scatter_dimension=0, tiled=True
        ).astype(jnp.float32),
        lax.psum_scatter(
            grad_values.astype(jnp.bfloat16), "seq", scatter_dimension=0, tiled=True
        ).astype(jnp.float32),
    )
    grad_projected = jnp.concatenate(
        [
            grad_queries.astype(jnp.bfloat16),
            key_share.astype(jnp.bfloat16),
            value_share.astype(jnp.bfloat16),
        ],
        axis=1,
    )
    grad_query_add = jnp.sum(grad_projected[:, :D].astype(jnp.float32), axis=0)
    grad_value_add = jnp.sum(grad_projected[:, 2 * D :].astype(jnp.float32), axis=0)
    grad_attend_mat = jnp.einsum(
        "td,te->de", token_rows, grad_projected, preferred_element_type=jnp.float32
    )
    input_grad = grad_hidden + jnp.einsum(
        "te,de->td", grad_projected, attend_mat, preferred_element_type=jnp.float32
    )
    (
        sum_attend_mat,
        sum_query_add,
        sum_value_add,
        sum_output_mat,
        sum_output_add,
        sum_first_scale,
        sum_first_offset,
        sum_inner_mat,
        sum_inner_add,
        sum_outer_mat,
        sum_outer_add,
        sum_second_scale,
        sum_second_offset,
    ) = (
        lax.psum_scatter(grad_attend_mat, ("seq", "dp"), scatter_dimension=0, tiled=True),
        lax.psum_scatter(grad_query_add, ("seq", "dp"), scatter_dimension=0, tiled=True),
        lax.psum_scatter(grad_value_add, ("seq", "dp"), scatter_dimension=0, tiled=True),
        lax.psum_scatter(grad_output_mat, ("seq", "dp"), scatter_dimension=0, tiled=True),
        lax.psum_scatter(grad_output_add, ("seq", "dp"), scatter_dimension=0, tiled=True),
        lax.psum_scatter(grad_first_scale, ("seq", "dp"), scatter_dimension=0, tiled=True),
        lax.psum_scatter(grad_first_offset, ("seq", "dp"), scatter_dimension=0, tiled=True),
        lax.psum_scatter(grad_inner_mat, ("seq", "dp"), scatter_dimension=0, tiled=True),
        lax.psum_scatter(grad_inner_add, ("seq", "dp"), scatter_dimension=0, tiled=True),
        lax.psum_scatter(grad_outer_mat, ("seq", "dp"), scatter_dimension=0, tiled=True),
        lax.psum_scatter(grad_outer_add, ("seq", "dp"), scatter_dimension=0, tiled=True),
        lax.psum_scatter(grad_second_scale, ("seq", "dp"), scatter_dimension=0, tiled=True),
        lax.psum_scatter(grad_second_offset, ("seq", "dp"), scatter_dimension=0, tiled=True),
    )
    return (
        layer_output,
        input_grad.reshape(1, GROUP, D),
        sum_attend_mat,
        sum_query_add,
        sum_value_add,
        sum_output_mat,
        sum_output_add,
        sum_first_scale,
        sum_first_offset,
        sum_inner_mat,
        sum_inner_add,
        sum_outer_mat,
        sum_outer_add,
        sum_second_scale,
        sum_second_offset,
    )


AXES = ("seq", "dp")
DEVICES = 32
WIDE = ((3, 4, 2, 1), (3, 1, 4, 2))
NARROW = ((3, 2, 1, 4), (3, 2, 1, 4))
HINT = pl.CostEstimate(flops=1, bytes_accessed=1, transcendentals=0)
REMOTE = GROUP - 64
ROWS = GROUP + REMOTE


def swap(value, masks):
    pairs = [(i, i ^ masks[i & 1]) for i in range(DEVICES)]
    return lax.ppermute(value, AXES, pairs)


def sync(movers, *values):
    state, values = lax.optimization_barrier(([mover.data for mover in movers], values))
    for mover, data in zip(movers, state):
        mover.data = data
    return values


def stage_masks(order, stage):
    return (1 << order[0][stage], 1 << order[1][stage])


def chip_mask(bits, place):
    return sum(1 << b for t, b in enumerate(bits) if place >> t & 1)


def join_body(cut, *refs):
    sems = refs[-1]
    ins, outs = refs[: len(refs) - 3], refs[len(refs) - 3 : -1]
    copies = []
    for number, out_ref in enumerate(outs):
        width = out_ref.shape[2]
        for side in range(2):
            source = ins[side] if cut else ins[2 * number + side]
            count = source.shape[0]
            if cut:
                source = source.at[:, :, pl.ds(number * cut, width)]
            target = out_ref.at[pl.ds(side * count, count)]
            copies.append(pltpu.make_async_copy(source, target, sems.at[2 * number + side]))
    for copy in copies:
        copy.start()
    for copy in copies:
        copy.wait()


def join(pieces, cut=0):
    count, rows, columns = pieces[0].shape
    widths = (cut, columns - cut) if cut else (columns, pieces[2].shape[2])
    return pl.pallas_call(
        functools.partial(join_body, cut),
        out_shape=[
            jax.ShapeDtypeStruct((2 * count, rows, width), jnp.bfloat16) for width in widths
        ],
        in_specs=[pl.BlockSpec(memory_space=pl.ANY)] * len(pieces),
        out_specs=[pl.BlockSpec(memory_space=pltpu.VMEM)] * 2,
        scratch_shapes=[pltpu.SemaphoreType.DMA((4,))],
        compiler_params=pltpu.CompilerParams(vmem_limit_bytes=16 * 2**20),
        cost_estimate=HINT,
    )(*pieces)


class Gather:
    def __init__(self, me, weights, cut, extra=()):
        self.me, self.cut, self.data = me, cut, {}
        core = me & 1
        both = []
        for side in (core, 1 - core):
            parts = []
            for weight in weights:
                half = weight.shape[1] // 2
                parts.append(lax.dynamic_slice(weight, (0, side * half), (weight.shape[0], half)))
            parts.extend(extra)
            both.append(parts[0] if len(parts) == 1 else jnp.concatenate(parts, axis=1))
        self.data["mine"] = both[0]
        self.data["arrived"] = swap(both[1], (1, 1))

    def depth(self):
        mine, other = self.data["mine"], self.data["arrived"]
        first = (self.me & 1) == 0
        both = jnp.concatenate([jnp.where(first, mine, other), jnp.where(first, other, mine)])
        both = both[None]
        self.data = {"held": both, "arrived": swap(both, stage_masks(WIDE, 0))}

    def step(self, stage):
        held, arrived = self.data["held"], self.data["arrived"]
        if stage == 1:
            held = join([held, arrived], self.cut)
        else:
            held = join([piece for pair in zip(held, arrived) for piece in pair])
        arrived = [
            swap(piece, stage_masks(order, stage)) for piece, order in zip(held, (WIDE, NARROW))
        ]
        self.data = {"held": held, "arrived": arrived}

    def share(self, name, cuts=(0, 1)):
        shared = self.data.setdefault(name + " core", [None, None])
        for cut in cuts:
            shared[cut] = swap(self.data[name][cut], (1, 1))

    def pieces(self):
        names = ("held", "arrived", "held core", "arrived core")
        return [piece for name in names for piece in self.data[name]]


def gather_matmul_body(routes, count, tile, me_ref, left_ref, *refs):
    piece_refs = refs[:8]
    out_refs, product_ref = refs[8 : 8 + count], refs[8 + count]
    mats, in_sems, out_sems = refs[9 + count : 9 + 2 * count], refs[-2], refs[-1]
    me = me_ref[0]
    rows = piece_refs[0].shape[1]
    copies = []
    for number, piece in enumerate(piece_refs):
        chunk, arrived, side = number % 2, number // 2 % 2, number // 4
        order = (WIDE, NARROW)[chunk]
        base = me ^ side
        core = base & 1
        for sub in range(8):
            place = 8 * arrived + sub
            mask = jnp.where(core == 0, chip_mask(order[0], place), chip_mask(order[1], place))
            chip = (base ^ mask) >> 1
            for start, width, mat, begin in routes(chunk, mats):
                half = mat.shape[1] // 2
                target = mat.at[
                    pl.ds(pl.multiple_of(chip * rows, rows), rows),
                    pl.ds(pl.multiple_of(core * half + begin, 128), width),
                ]
                source = piece.at[sub, :, pl.ds(start, width)]
                copies.append(pltpu.make_async_copy(source, target, in_sems.at[len(copies)]))
    for copy in copies:
        copy.start()
    kept = []
    per_side = len(copies) // 2
    for side in range(2):
        core = (me ^ side) & 1
        for copy in copies[side * per_side : (side + 1) * per_side]:
            copy.wait()
        for number, (mat, out_ref) in enumerate(zip(mats, out_refs)):
            half = mat.shape[1] // 2
            columns = pl.ds(pl.multiple_of(core * half, half), half)
            kept.append(
                pltpu.make_async_copy(
                    mat.at[:, columns], out_ref.at[:, columns], out_sems.at[2 * number + side]
                )
            )
            kept[-1].start()
        half = product_ref.shape[1] // 2

        def step(i, carry):
            columns = pl.ds(pl.multiple_of(core * half + i * tile, tile), tile)
            product_ref[:, columns] = jnp.dot(
                left_ref[...], mats[0][:, columns], preferred_element_type=jnp.float32
            )
            return carry

        lax.fori_loop(0, half // tile, step, 0)
    for copy in kept:
        copy.wait()


def gather_matmul(gather, routes, widths, left):
    pieces = gather.pieces()
    depth = pieces[0].shape[1] * DEVICES // 2
    mats = [(depth, width) for width in widths]
    return pl.pallas_call(
        functools.partial(gather_matmul_body, routes, len(widths), 512),
        out_shape=[jax.ShapeDtypeStruct(mat, jnp.bfloat16) for mat in mats]
        + [jax.ShapeDtypeStruct((left.shape[0], widths[0]), jnp.float32)],
        in_specs=[
            pl.BlockSpec(memory_space=pltpu.SMEM),
            pl.BlockSpec(memory_space=pltpu.VMEM),
        ]
        + [pl.BlockSpec(memory_space=pl.ANY)] * 8,
        out_specs=[pl.BlockSpec(memory_space=pl.ANY)] * len(widths)
        + [pl.BlockSpec(memory_space=pltpu.VMEM)],
        scratch_shapes=[pltpu.VMEM(mat, jnp.bfloat16) for mat in mats]
        + [pltpu.SemaphoreType.DMA((96,)), pltpu.SemaphoreType.DMA((2 * len(widths),))],
        compiler_params=pltpu.CompilerParams(vmem_limit_bytes=40 * 2**20),
        cost_estimate=HINT,
    )(gather.me.reshape(1), left, *pieces)


def whole_routes(cut, chunk, outs):
    half = outs[0].shape[1] // 2
    return ((0, (cut, half - cut)[chunk], outs[0], chunk * cut),)


def first_routes(chunk, outs):
    if chunk == 0:
        return ((0, outs[0].shape[1] // 2, outs[0], 0),)
    half = outs[1].shape[1] // 2
    return ((0, half, outs[1], 0), (half, outs[2].shape[1] // 2, outs[2], 0))


def place_of(bits, shard):
    place = shard & 1
    for t, b in enumerate(bits):
        place = place | ((shard >> b) & 1) << (t + 1)
    return place


def weight_grad_body(chunks, tile, me_ref, left_ref, right_ref, *refs):
    extra_refs = refs[: -2 * len(chunks)]
    outs = refs[-2 * len(chunks) :]
    me = me_ref[0]
    rows = outs[0].shape[1]
    half = right_ref.shape[1] // 2
    per_tile = tile // rows

    def step(i, carry):
        left = left_ref[:, pl.ds(pl.multiple_of(i * tile, tile), tile)].T
        for side in (1, 0):
            base = me ^ side
            core = base & 1
            right = right_ref[:, pl.ds(pl.multiple_of(core * half, half), half)]
            product = jnp.dot(left, right, preferred_element_type=jnp.float32).astype(
                jnp.bfloat16
            )
            for sub in range(per_tile):
                number = i * per_tile + sub
                shard = number ^ base
                for which, (order, begin, width) in enumerate(chunks):
                    place = jnp.where(
                        core == 0, place_of(order[0], shard), place_of(order[1], shard)
                    )
                    out_ref = outs[2 * which + side]
                    out_ref[place, :, :width] = product[
                        sub * rows : (sub + 1) * rows, begin : begin + width
                    ]
                    for extra_ref in extra_refs:
                        out_ref[place, :, width:] = extra_ref[number]
        return carry

    lax.fori_loop(0, left_ref.shape[1] // tile, step, 0, unroll=2)


def weight_grad(left, right, me, chunks, extra=()):
    depth = left.shape[1]
    rows = depth // DEVICES
    more = sum(e.shape[2] for e in extra)
    shapes = [
        jax.ShapeDtypeStruct((DEVICES, rows, width + more), jnp.bfloat16)
        for _, _, width in chunks
        for _ in range(2)
    ]
    outs = pl.pallas_call(
        functools.partial(weight_grad_body, chunks, 256),
        out_shape=shapes,
        in_specs=[pl.BlockSpec(memory_space=pltpu.SMEM)]
        + [pl.BlockSpec(memory_space=pltpu.VMEM)] * (2 + len(extra)),
        out_specs=[pl.BlockSpec(memory_space=pltpu.VMEM)] * len(shapes),
        compiler_params=pltpu.CompilerParams(vmem_limit_bytes=24 * 2**20),
        cost_estimate=HINT,
    )(me.reshape(1), left, right, *extra)
    return [tuple(outs[i : i + 2]) for i in range(0, len(outs), 2)]


def add_low(one, two):
    return (one.astype(jnp.float32) + two.astype(jnp.float32)).astype(jnp.bfloat16)


def halve_body(*refs):
    count = len(refs) // 6
    for which in range(count):
        held_low, held_high, low, high = refs[4 * which : 4 * which + 4]
        keep_ref, send_ref = refs[4 * count + 2 * which : 4 * count + 2 * which + 2]
        send_ref[...] = add_low(held_high[...], high[...])
        keep_ref[...] = add_low(held_low[...], low[...])


def halve(pairs):
    half = pairs[0][0].shape[0] // 2
    block = max(half // 4, 1)
    steps = half // block
    specs, outs, shapes, values = [], [], [], []
    for held, arrived in pairs:
        _, rows, columns = held.shape
        low = pl.BlockSpec((block, rows, columns), lambda i: (i, 0, 0))
        high = pl.BlockSpec((block, rows, columns), lambda i: (steps + i, 0, 0))
        specs += [low, high, low, high]
        outs += [low, low]
        shapes += [jax.ShapeDtypeStruct((half, rows, columns), jnp.bfloat16)] * 2
        values += [held, held, arrived, arrived]
    results = pl.pallas_call(
        halve_body,
        grid=(steps,),
        in_specs=specs,
        out_specs=outs,
        out_shape=shapes,
        compiler_params=pltpu.CompilerParams(vmem_limit_bytes=16 * 2**20),
        cost_estimate=HINT,
    )(*values)
    return results[0::2], results[1::2]


def first_norm_body(
    rows_ref, mixed_ref, matrix_ref, add_ref, gain_ref, shift_ref, low_ref, out_ref, normed_ref, inverse_ref
):
    branch = jnp.dot(mixed_ref[...], matrix_ref[...], preferred_element_type=jnp.float32)
    out, normed, inverse = norm_forward(
        rows_ref[...].astype(jnp.float32) + (branch + add_ref[...]), gain_ref[...], shift_ref[...]
    )
    low_ref[...] = out.astype(jnp.bfloat16)
    out_ref[...] = out
    normed_ref[...] = normed
    inverse_ref[...] = inverse


def first_norm(rows, mixed, matrix, add, gain, shift):
    block = 128
    tall = pl.BlockSpec((block, D), lambda i: (i, 0))
    whole = pl.BlockSpec((1, D), lambda i: (0, 0))
    return pl.pallas_call(
        first_norm_body,
        grid=(GROUP // block,),
        in_specs=[tall, tall, pl.BlockSpec((D, D), lambda i: (0, 0)), whole, whole, whole],
        out_specs=[tall, tall, tall, pl.BlockSpec((block, 1), lambda i: (i, 0))],
        out_shape=[
            jax.ShapeDtypeStruct((GROUP, D), jnp.bfloat16),
            jax.ShapeDtypeStruct((GROUP, D), jnp.float32),
            jax.ShapeDtypeStruct((GROUP, D), jnp.float32),
            jax.ShapeDtypeStruct((GROUP, 1), jnp.float32),
        ],
        compiler_params=pltpu.CompilerParams(vmem_limit_bytes=20 * 2**20),
        cost_estimate=HINT,
    )(rows, mixed, matrix, add, gain, shift)


def rows_back_body(grad_ref, matrix_ref, near_ref, far_ref):
    product = lax.dot_general(
        grad_ref[...],
        matrix_ref[...],
        (((1,), (1,)), ((), ())),
        preferred_element_type=jnp.float32,
    )
    near_ref[...] = product[:GROUP]
    far_ref[...] = product[GROUP:].astype(jnp.bfloat16)


def rows_back(grad, matrix):
    return pl.pallas_call(
        rows_back_body,
        grid=(4,),
        in_specs=[
            pl.BlockSpec((ROWS, 3 * D), lambda i: (0, 0)),
            pl.BlockSpec((D // 4, 3 * D), lambda i: (i, 0)),
        ],
        out_specs=[
            pl.BlockSpec((GROUP, D // 4), lambda i: (0, i)),
            pl.BlockSpec((REMOTE, D // 4), lambda i: (0, i)),
        ],
        out_shape=[
            jax.ShapeDtypeStruct((GROUP, D), jnp.float32),
            jax.ShapeDtypeStruct((REMOTE, D), jnp.bfloat16),
        ],
        compiler_params=pltpu.CompilerParams(vmem_limit_bytes=16 * 2**20),
        cost_estimate=HINT,
    )(grad, matrix)


def cut_grads(me, left, right, cut):
    half = right.shape[1] // 2
    return weight_grad(left, right, me, ((WIDE, 0, cut), (NARROW, cut, half - cut)))


class Scatter:
    def __init__(self, me, grads):
        self.me, self.stage = me, 4
        self.data = {"held": [keep for keep, _ in grads], "send": [send for _, send in grads]}

    def begin(self):
        self.data["arrived"] = [swap(piece, (1, 1)) for piece in self.data.pop("send")]

    def step(self):
        self.stage -= 1
        held, send = halve(list(zip(self.data["held"], self.data["arrived"])))
        if self.stage == 0:
            held, send = jnp.concatenate(held, axis=2), jnp.concatenate(send, axis=2)
            arrived = swap(send, stage_masks(WIDE, 0))
        else:
            arrived = [
                swap(piece, stage_masks(order, self.stage))
                for piece, order in zip(send, (WIDE, NARROW))
            ]
        self.data = {"held": held, "arrived": arrived}

    def near(self):
        held, arrived = self.data["held"], self.data["arrived"]
        send = add_low(held[1], arrived[1])
        held = held[0].astype(jnp.float32) + arrived[0].astype(jnp.float32)
        self.data = {"held": held, "arrived": swap(send, (1, 1))}

    def result(self):
        held, arrived = self.data["held"], self.data["arrived"].astype(jnp.float32)
        first = (self.me & 1) == 0
        return jnp.where(first, held, arrived), jnp.where(first, arrived, held)


def masked_pair(keys):
    first = lax.broadcasted_iota(jnp.int32, keys.shape, 1) < HEAD
    zeros = jnp.zeros_like(keys)
    return jnp.where(first, keys, zeros), jnp.where(first, zeros, keys)


PAIRS = 2
WIDTH = PAIRS * 128
STEPS = D // WIDTH


def attend_forward_body(query_docs, key_docs, query_ref, key_ref, value_ref, mixed_ref, log_ref):
    allowed = key_docs[...] == query_docs[...]
    for pair in range(PAIRS):
        columns = slice(pair * 128, (pair + 1) * 128)
        queries = query_ref[:, columns]
        value_rows = value_ref[:, columns].T
        results = []
        for head, keys in enumerate(masked_pair(key_ref[:, columns])):
            raw = lax.dot_general(
                keys, queries, (((1,), (1,)), ((), ())), preferred_element_type=jnp.float32
            )
            scores = jnp.where(allowed, raw * HEAD**-0.5, masked_score)
            peak = jnp.max(scores, axis=0, keepdims=True)
            terms = jnp.exp(scores - peak)
            total = jnp.sum(terms, axis=0, keepdims=True)
            weights = (terms * (1.0 / total)).astype(jnp.bfloat16)
            results.append(
                jnp.dot(
                    value_rows[head * HEAD : (head + 1) * HEAD],
                    weights,
                    preferred_element_type=jnp.float32,
                )
            )
            log_ref[pair, head : head + 1] = peak + jnp.log(total)
        mixed_ref[:, columns] = jnp.concatenate(results).T.astype(jnp.bfloat16)


def attend_specs():
    return [
        pl.BlockSpec((1, GROUP), lambda i: (0, 0)),
        pl.BlockSpec((ROWS, 1), lambda i: (0, 0)),
        pl.BlockSpec((GROUP, WIDTH), lambda i: (0, i)),
        pl.BlockSpec((ROWS, WIDTH), lambda i: (0, STEPS + i)),
        pl.BlockSpec((ROWS, WIDTH), lambda i: (0, 2 * STEPS + i)),
    ]


def attend_forward(query_docs, key_docs, projected):
    return pl.pallas_call(
        attend_forward_body,
        grid=(STEPS,),
        in_specs=attend_specs(),
        out_specs=[
            pl.BlockSpec((GROUP, WIDTH), lambda i: (0, i)),
            pl.BlockSpec((PAIRS, 2, GROUP), lambda i: (i, 0, 0)),
        ],
        out_shape=[
            jax.ShapeDtypeStruct((GROUP, D), jnp.bfloat16),
            jax.ShapeDtypeStruct((HEADS // 2, 2, GROUP), jnp.float32),
        ],
        compiler_params=pltpu.CompilerParams(vmem_limit_bytes=16 * 2**20),
        cost_estimate=HINT,
    )(query_docs, key_docs, projected, projected, projected)


def attend_backward_body(
    query_docs, key_docs, query_ref, key_ref, value_ref, upstream_ref, log_ref, grad_ref, sum_ref
):
    allowed = key_docs[...] == query_docs[...]
    across = (((1,), (1,)), ((), ()))
    wide = lax.broadcasted_iota(jnp.int32, (ROWS, 128), 1) < HEAD
    for pair in range(PAIRS):
        columns = slice(pair * 128, (pair + 1) * 128)
        queries, upstream = query_ref[:, columns], upstream_ref[:, columns]
        key_rows = key_ref[:, columns].T
        pairs = zip(masked_pair(key_ref[:, columns]), masked_pair(value_ref[:, columns]))
        query_parts, key_parts, value_parts = [], [], []
        for head, (keys, values) in enumerate(pairs):
            raw = lax.dot_general(keys, queries, across, preferred_element_type=jnp.float32)
            scores = jnp.where(allowed, raw * HEAD**-0.5, masked_score)
            probs = jnp.exp(scores - log_ref[pair, head : head + 1])
            grad_weights = lax.dot_general(
                values, upstream, across, preferred_element_type=jnp.float32
            )
            row_dot = jnp.sum(grad_weights * probs, axis=0, keepdims=True)
            grad_scores = (probs * (grad_weights - row_dot)).astype(jnp.bfloat16)
            weights = probs.astype(jnp.bfloat16)
            query_parts.append(
                jnp.dot(
                    key_rows[head * HEAD : (head + 1) * HEAD],
                    grad_scores,
                    preferred_element_type=jnp.float32,
                )
            )
            key_parts.append(jnp.dot(grad_scores, queries, preferred_element_type=jnp.float32))
            value_parts.append(jnp.dot(weights, upstream, preferred_element_type=jnp.float32))
        grad_queries = (jnp.concatenate(query_parts).T * HEAD**-0.5).astype(jnp.bfloat16)
        grad_keys = jnp.where(wide, key_parts[0], key_parts[1]) * HEAD**-0.5
        grad_values = jnp.where(wide, value_parts[0], value_parts[1]).astype(jnp.bfloat16)
        start = pl.program_id(0) * WIDTH + pair * 128
        query_at, key_at, value_at = (
            pl.ds(pl.multiple_of(start + part * D, 128), 128) for part in range(3)
        )
        grad_ref[:GROUP, query_at] = grad_queries
        grad_ref[GROUP:, query_at] = jnp.zeros((REMOTE, 128), jnp.bfloat16)
        grad_ref[:, key_at] = grad_keys.astype(jnp.bfloat16)
        grad_ref[:, value_at] = grad_values
        low = grad_queries.astype(jnp.float32)
        sum_ref[0, :, query_at] = jnp.sum(low, axis=0, keepdims=True)
        low = grad_values.astype(jnp.float32)
        sum_ref[1, :, query_at] = jnp.sum(low, axis=0, keepdims=True)


def attend_backward(query_docs, key_docs, projected, upstream, logs):
    return pl.pallas_call(
        attend_backward_body,
        grid=(STEPS,),
        in_specs=attend_specs()
        + [
            pl.BlockSpec((GROUP, WIDTH), lambda i: (0, i)),
            pl.BlockSpec((PAIRS, 2, GROUP), lambda i: (i, 0, 0)),
        ],
        out_specs=[
            pl.BlockSpec((ROWS, 3 * D), lambda i: (0, 0)),
            pl.BlockSpec((2, 1, D), lambda i: (0, 0, 0)),
        ],
        out_shape=[
            jax.ShapeDtypeStruct((ROWS, 3 * D), jnp.bfloat16),
            jax.ShapeDtypeStruct((2, 1, D), jnp.float32),
        ],
        compiler_params=pltpu.CompilerParams(vmem_limit_bytes=16 * 2**20),
        cost_estimate=HINT,
    )(query_docs, key_docs, projected, projected, projected, upstream, logs)


def pack_shard(vectors):
    rows = jnp.concatenate([vector.reshape(-1, 32) for vector in vectors])
    return jnp.pad(rows, ((0, 32 - rows.shape[0]), (0, 96)))


def unpack_shards(packed):
    rows = packed.reshape(DEVICES, 32, 256)[:, :12, :32].astype(jnp.float32)
    short = rows[:, :8].transpose(1, 0, 2).reshape(8, 1, D)
    return [short[i] for i in range(8)] + [rows[:, 8:].reshape(1, 4 * D)]


def pack_grads(short, long):
    rows = jnp.concatenate([vector.reshape(1, 8, 128) for vector in short])
    rows = jnp.repeat(rows.transpose(1, 0, 2), 4, axis=0)
    rows = jnp.concatenate([rows, long.reshape(DEVICES, 1, 128)], axis=1)
    return jnp.pad(rows, ((0, 0), (0, 23), (0, 0))).astype(jnp.bfloat16)


def fast_local(
    tokens,
    cotangent,
    doc_lengths,
    attend_weight,
    query_bias,
    value_bias,
    output_weight,
    output_bias,
    first_gain,
    first_shift,
    inner_weight,
    inner_bias,
    outer_weight,
    outer_bias,
    second_gain,
    second_shift,
):
    me = lax.axis_index(AXES)
    group_index = me >> 4
    small_shard = pack_shard(
        [
            query_bias,
            value_bias,
            output_bias,
            first_gain,
            first_shift,
            outer_bias,
            second_gain,
            second_shift,
            inner_bias,
        ]
    )
    attend_cut, inner_cut, outer_cut = 3 * D // 2, 1408, 384
    one = Gather(me, (attend_weight, output_weight), attend_cut, (small_shard,))
    sync((one,))

    one.depth()
    two = Gather(me, (inner_weight,), inner_cut)
    three = Gather(me, (outer_weight,), outer_cut)
    movers = (one, two, three)
    doc_ends = jnp.cumsum(doc_lengths[0])
    near_at = group_index * GROUP + lax.iota(jnp.int32, GROUP)
    far_at = jnp.where(group_index == 0, GROUP, 64) + lax.iota(jnp.int32, REMOTE)
    row_at = jnp.concatenate([near_at, far_at])
    row_docs = jnp.sum((row_at[:, None] >= doc_ends[None, :]).astype(jnp.int32), axis=1)
    query_docs, key_docs = row_docs[None, :GROUP], row_docs[:, None]
    near = tokens.reshape(GROUP, D)
    query_docs, key_docs, near = sync(movers, query_docs, key_docs, near)

    one.step(1)
    two.depth()
    far = lax.dynamic_slice(near, (64 * (1 - group_index), 0), (REMOTE, D))
    far = lax.ppermute(far, "seq", [(0, 1), (1, 0)])
    (far,) = sync((one, two), far)

    one.step(2)
    token_rows = jnp.concatenate([near, far])
    (token_rows,) = sync((one, two), token_rows)

    one.step(3)
    two.step(1)
    three.depth()
    sync(movers)

    one.share("held")
    one.share("arrived")
    sync((one,))

    two.step(2)
    three.step(1)
    attend_mat, output_mat, small_all, projected = gather_matmul(
        one, first_routes, (3 * D, D, 256), token_rows
    )
    (
        query_add,
        value_add,
        output_add,
        first_scale,
        first_offset,
        outer_add,
        second_scale,
        second_offset,
        inner_add,
    ) = unpack_shards(small_all)
    bias_row = jnp.concatenate([query_add, jnp.zeros((1, D), jnp.float32), value_add], axis=1)
    projected = (projected + bias_row).astype(jnp.bfloat16)
    (projected,) = sync((two, three), projected)

    two.step(3)
    two.share("held", (0,))
    three.step(2)
    attended, logs = attend_forward(query_docs, key_docs, projected)
    first_low, first_out, first_normed, first_inverse = first_norm(
        near, attended, output_mat, output_add, first_scale, first_offset
    )
    first_out, first_normed, first_inverse, first_low = sync(
        (two, three), first_out, first_normed, first_inverse, first_low
    )

    two.share("held", (1,))
    two.share("arrived")
    sync((two,))

    three.step(3)
    three.share("held")
    inner_mat, pre_act = gather_matmul(
        two, functools.partial(whole_routes, inner_cut), (4 * D,), first_low
    )
    pre_act = pre_act + inner_add
    cdf = 0.5 * (1.0 + lax.erf(pre_act * 0.5**0.5))
    gelu_slope = cdf + pre_act * jnp.exp(-0.5 * pre_act * pre_act) * 0.3989422804014327
    activated = (pre_act * cdf).astype(jnp.bfloat16)
    activated, gelu_slope = sync((three,), activated, gelu_slope)

    three.share("arrived")
    outer_mat, mlp_out = gather_matmul(
        three, functools.partial(whole_routes, outer_cut), (D,), activated
    )
    mlp_out = mlp_out + outer_add
    second_out, second_normed, second_inverse = norm_forward(
        first_out + mlp_out, second_scale, second_offset
    )
    layer_output = second_out.astype(jnp.bfloat16).reshape(1, GROUP, D)
    upstream = cotangent.reshape(GROUP, D).astype(jnp.float32)
    grad_two = norm_backward(upstream, second_normed, second_inverse, second_scale)
    grad_mlp = grad_two.astype(jnp.bfloat16)
    outer = Scatter(me, cut_grads(me, activated, grad_mlp, outer_cut))
    grad_mlp, grad_two, second_normed = sync((outer,), grad_mlp, grad_two, second_normed)

    outer.begin()
    grad_act = jnp.einsum("td,fd->tf", grad_mlp, outer_mat, preferred_element_type=jnp.float32)
    grad_pre = (grad_act * gelu_slope).astype(jnp.bfloat16)
    inner_sum = jnp.sum(grad_pre.astype(jnp.float32), axis=0)
    grad_pre, inner_sum, grad_mlp, second_normed = sync(
        (outer,), grad_pre, inner_sum, grad_mlp, second_normed
    )

    outer.step()
    inner = Scatter(me, cut_grads(me, first_low, grad_pre, inner_cut))
    second_sums = (
        jnp.sum(grad_mlp.astype(jnp.float32), axis=0),
        jnp.sum(upstream * second_normed, axis=0),
        jnp.sum(upstream, axis=0),
    )
    grad_first = (
        jnp.einsum("tf,df->td", grad_pre, inner_mat, preferred_element_type=jnp.float32) + grad_two
    )
    grad_hidden = norm_backward(grad_first, first_normed, first_inverse, first_scale)
    grad_branch = grad_hidden.astype(jnp.bfloat16)
    first_sums = (
        jnp.sum(grad_branch.astype(jnp.float32), axis=0),
        jnp.sum(grad_first * first_normed, axis=0),
        jnp.sum(grad_first, axis=0),
    )
    grad_attended = jnp.einsum(
        "te,de->td", grad_branch, output_mat, preferred_element_type=jnp.float32
    ).astype(jnp.bfloat16)
    first_sums, second_sums, grad_hidden, grad_branch, grad_attended = sync(
        (outer, inner), first_sums, second_sums, grad_hidden, grad_branch, grad_attended
    )

    inner.begin()
    outer.step()
    grad_projected, row_sums = attend_backward(
        query_docs, key_docs, projected, grad_attended, logs
    )
    grad_projected, row_sums = sync((outer, inner), grad_projected, row_sums)

    inner.step()
    outer.step()
    small = pack_grads([row_sums[0, 0], row_sums[1, 0], *first_sums, *second_sums], inner_sum)
    first = Scatter(
        me,
        weight_grad(token_rows, grad_projected, me, ((WIDE, 0, attend_cut),))
        + weight_grad(attended, grad_branch, me, ((NARROW, 0, D // 2),), (small,)),
    )
    movers = (outer, inner, first)
    sync(movers)

    first.begin()
    inner.step()
    outer.step()
    row_grad, far_grad = rows_back(grad_projected, attend_mat)
    row_grad, far_grad = sync(movers, row_grad, far_grad)

    first.step()
    inner.step()
    outer.near()
    sync(movers)

    first.step()
    inner.step()
    sum_outer_mat = jnp.concatenate(outer.result(), axis=1)
    (sum_outer_mat,) = sync((inner, first), sum_outer_mat)

    first.step()
    inner.near()
    (far_grad,) = sync((inner, first), far_grad)

    first.step()
    far_grad = lax.ppermute(far_grad, "seq", [(0, 1), (1, 0)])
    sum_inner_mat = jnp.concatenate(inner.result(), axis=1)
    sum_inner_mat, far_grad = sync((first,), sum_inner_mat, far_grad)

    first.near()
    filler = jnp.zeros((64, D), jnp.float32)
    far_grad = far_grad.astype(jnp.float32)
    far_grad = jnp.where(
        group_index == 0,
        jnp.concatenate([filler, far_grad]),
        jnp.concatenate([far_grad, filler]),
    )
    input_grad = grad_hidden + row_grad + far_grad
    halves = first.result()
    output_end = attend_cut + D // 2
    sum_attend_mat = jnp.concatenate([half[:, :attend_cut] for half in halves], axis=1)
    sum_output_mat = jnp.concatenate([half[:, attend_cut:output_end] for half in halves], axis=1)
    small_rows = halves[0][:, output_end:]
    own = lax.dynamic_slice(small_rows, (0, 32 * (me & 3)), (8, 32))
    (
        sum_query_add,
        sum_value_add,
        sum_output_add,
        sum_first_scale,
        sum_first_offset,
        sum_outer_add,
        sum_second_scale,
        sum_second_offset,
    ) = (own[i] for i in range(8))
    sum_inner_add = small_rows[8]
    return (
        layer_output,
        input_grad.reshape(1, GROUP, D),
        sum_attend_mat,
        sum_query_add,
        sum_value_add,
        sum_output_mat,
        sum_output_add,
        sum_first_scale,
        sum_first_offset,
        sum_inner_mat,
        sum_inner_add,
        sum_outer_mat,
        sum_outer_add,
        sum_second_scale,
        sum_second_offset,
    )


def solution(mesh):
    sizes = (mesh.shape["seq"], mesh.shape["dp"])
    return jax.shard_map(
        fast_local if sizes == (2, 16) else general_local,
        mesh=mesh,
        in_specs=(
            P("dp", "seq", None),
            P("dp", "seq", None),
            P("dp", None),
            P(("seq", "dp"), None),
            P(("seq", "dp")),
            P(("seq", "dp")),
            P(("seq", "dp"), None),
            P(("seq", "dp")),
            P(("seq", "dp")),
            P(("seq", "dp")),
            P(("seq", "dp"), None),
            P(("seq", "dp")),
            P(("seq", "dp"), None),
            P(("seq", "dp")),
            P(("seq", "dp")),
            P(("seq", "dp")),
        ),
        out_specs=(
            P("dp", "seq", None),
            P("dp", "seq", None),
            P(("seq", "dp"), None),
            P(("seq", "dp")),
            P(("seq", "dp")),
            P(("seq", "dp"), None),
            P(("seq", "dp")),
            P(("seq", "dp")),
            P(("seq", "dp")),
            P(("seq", "dp"), None),
            P(("seq", "dp")),
            P(("seq", "dp"), None),
            P(("seq", "dp")),
            P(("seq", "dp")),
            P(("seq", "dp")),
        ),
        check_vma=False,
    )
```

```python
import functools

import jax
import jax.numpy as jnp
from jax import lax
from jax.experimental import pallas as pl
from jax.experimental.pallas import tpu as pltpu
from jax.sharding import PartitionSpec as P

D = 1024
HEADS = 16
HEAD = 64
GROUP = 256


epsilon = 1e-12
masked_score = -1e30


def norm_forward(value, gain, shift):
    mean_value = jnp.mean(value, axis=-1, keepdims=True)
    center = value - mean_value
    inverse = lax.rsqrt(jnp.mean(center * center, axis=-1, keepdims=True) + epsilon)
    normed = center * inverse
    return (normed * gain + shift, normed, inverse)


def norm_backward(upstream, normed, inverse, gain):
    scaled = upstream * gain
    first_mean = jnp.mean(scaled, axis=-1, keepdims=True)
    second_mean = jnp.mean(scaled * normed, axis=-1, keepdims=True)
    return inverse * (scaled - first_mean - normed * second_mean)


def exact_gelu(value):
    return jax.nn.gelu(value, approximate=False)


def pair_scores(query_pair, key_pair, allowed, factor):
    raw = (
        jnp.einsum("qhd,khd->hqk", query_pair, key_pair, preferred_element_type=jnp.float32)
        * factor
    )
    return jnp.where(allowed[None], raw, masked_score)


def column_pair(matrix, column_start, row_count):
    return lax.dynamic_slice_in_dim(matrix, column_start, 2 * HEAD, 1).reshape(row_count, 2, HEAD)


def general_local(
    tokens,
    cotangent,
    doc_lengths,
    attend_weight,
    query_bias,
    value_bias,
    output_weight,
    output_bias,
    first_gain,
    first_shift,
    inner_weight,
    inner_bias,
    outer_weight,
    outer_bias,
    second_gain,
    second_shift,
):
    (
        attend_mat,
        query_add,
        value_add,
        output_mat,
        output_add,
        first_scale,
        first_offset,
        inner_mat,
        inner_add,
        outer_mat,
        outer_add,
        second_scale,
        second_offset,
    ) = (
        lax.all_gather(attend_weight, ("seq", "dp"), axis=0, tiled=True),
        lax.all_gather(query_bias, ("seq", "dp"), axis=0, tiled=True),
        lax.all_gather(value_bias, ("seq", "dp"), axis=0, tiled=True),
        lax.all_gather(output_weight, ("seq", "dp"), axis=0, tiled=True),
        lax.all_gather(output_bias, ("seq", "dp"), axis=0, tiled=True),
        lax.all_gather(first_gain, ("seq", "dp"), axis=0, tiled=True),
        lax.all_gather(first_shift, ("seq", "dp"), axis=0, tiled=True),
        lax.all_gather(inner_weight, ("seq", "dp"), axis=0, tiled=True),
        lax.all_gather(inner_bias, ("seq", "dp"), axis=0, tiled=True),
        lax.all_gather(outer_weight, ("seq", "dp"), axis=0, tiled=True),
        lax.all_gather(outer_bias, ("seq", "dp"), axis=0, tiled=True),
        lax.all_gather(second_gain, ("seq", "dp"), axis=0, tiled=True),
        lax.all_gather(second_shift, ("seq", "dp"), axis=0, tiled=True),
    )
    token_rows = tokens.reshape(GROUP, D)
    key_total = GROUP * lax.axis_size("seq")
    group_index = lax.axis_index("seq")
    doc_ends = jnp.cumsum(doc_lengths[0])
    positions = lax.iota(jnp.int32, key_total)
    key_docs = jnp.sum((positions[:, None] >= doc_ends[None, :]).astype(jnp.int32), axis=1)
    query_docs = lax.dynamic_slice_in_dim(key_docs, group_index * GROUP, GROUP)
    allowed = query_docs[:, None] == key_docs[None, :]
    factor = HEAD ** (-0.5)
    pair_count = HEADS // 2
    bias_row = jnp.concatenate(
        [query_add.astype(jnp.float32), jnp.zeros((D,), jnp.float32), value_add.astype(jnp.float32)]
    )
    projected = jnp.dot(token_rows, attend_mat, preferred_element_type=jnp.float32) + bias_row
    queries = projected[:, :D].astype(jnp.bfloat16)
    keys_mine = projected[:, D : 2 * D].astype(jnp.bfloat16)
    values_mine = projected[:, 2 * D :].astype(jnp.bfloat16)
    keys_all, values_all = (
        lax.all_gather(keys_mine, "seq", axis=0, tiled=True),
        lax.all_gather(values_mine, "seq", axis=0, tiled=True),
    )

    def forward_pair(pair_index, state_tuple):
        mixed_heads, logsum = state_tuple
        column_start = pair_index * 2 * HEAD
        query_pair = column_pair(queries, column_start, GROUP)
        key_pair = column_pair(keys_all, column_start, key_total)
        value_pair = column_pair(values_all, column_start, key_total)
        scores = pair_scores(query_pair, key_pair, allowed, factor)
        row_peak = jnp.max(scores, axis=-1, keepdims=True)
        expo_terms = jnp.exp(scores - row_peak)
        row_total = jnp.sum(expo_terms, axis=-1, keepdims=True)
        weights = (expo_terms / row_total).astype(jnp.bfloat16)
        result = jnp.einsum(
            "hqk,khd->qhd", weights, value_pair, preferred_element_type=jnp.float32
        ).reshape(GROUP, 2 * HEAD)
        mixed_heads = lax.dynamic_update_slice_in_dim(mixed_heads, result, column_start, 1)
        logsum = lax.dynamic_update_slice_in_dim(
            logsum, row_peak + jnp.log(row_total), pair_index * 2, 0
        )
        return (mixed_heads, logsum)

    mixed_heads, logsum = lax.fori_loop(
        0,
        pair_count,
        forward_pair,
        (jnp.zeros((GROUP, D), jnp.float32), jnp.zeros((HEADS, GROUP, 1), jnp.float32)),
    )
    attended = mixed_heads.astype(jnp.bfloat16)
    branch = jnp.dot(attended, output_mat, preferred_element_type=jnp.float32) + output_add.astype(
        jnp.float32
    )
    first_out, first_normed, first_inverse = norm_forward(
        token_rows.astype(jnp.float32) + branch,
        first_scale.astype(jnp.float32),
        first_offset.astype(jnp.float32),
    )
    first_low = first_out.astype(jnp.bfloat16)
    pre_act = jnp.dot(first_low, inner_mat, preferred_element_type=jnp.float32) + inner_add.astype(
        jnp.float32
    )
    activated = exact_gelu(pre_act).astype(jnp.bfloat16)
    mlp_out = jnp.dot(activated, outer_mat, preferred_element_type=jnp.float32) + outer_add.astype(
        jnp.float32
    )
    second_out, second_normed, second_inverse = norm_forward(
        first_out + mlp_out, second_scale.astype(jnp.float32), second_offset.astype(jnp.float32)
    )
    layer_output = second_out.astype(jnp.bfloat16).reshape(1, GROUP, D)
    (
        attend_mat,
        query_add,
        value_add,
        output_mat,
        output_add,
        first_scale,
        first_offset,
        inner_mat,
        inner_add,
        outer_mat,
        outer_add,
        second_scale,
        second_offset,
    ) = (
        lax.all_gather(attend_weight, ("seq", "dp"), axis=0, tiled=True),
        lax.all_gather(query_bias, ("seq", "dp"), axis=0, tiled=True),
        lax.all_gather(value_bias, ("seq", "dp"), axis=0, tiled=True),
        lax.all_gather(output_weight, ("seq", "dp"), axis=0, tiled=True),
        lax.all_gather(output_bias, ("seq", "dp"), axis=0, tiled=True),
        lax.all_gather(first_gain, ("seq", "dp"), axis=0, tiled=True),
        lax.all_gather(first_shift, ("seq", "dp"), axis=0, tiled=True),
        lax.all_gather(inner_weight, ("seq", "dp"), axis=0, tiled=True),
        lax.all_gather(inner_bias, ("seq", "dp"), axis=0, tiled=True),
        lax.all_gather(outer_weight, ("seq", "dp"), axis=0, tiled=True),
        lax.all_gather(outer_bias, ("seq", "dp"), axis=0, tiled=True),
        lax.all_gather(second_gain, ("seq", "dp"), axis=0, tiled=True),
        lax.all_gather(second_shift, ("seq", "dp"), axis=0, tiled=True),
    )
    upstream = cotangent.reshape(GROUP, D).astype(jnp.float32)
    grad_second_scale = jnp.sum(upstream * second_normed, axis=0)
    grad_second_offset = jnp.sum(upstream, axis=0)
    grad_two = norm_backward(
        upstream, second_normed, second_inverse, second_scale.astype(jnp.float32)
    )
    grad_mlp = grad_two.astype(jnp.bfloat16)
    grad_outer_add = jnp.sum(grad_mlp.astype(jnp.float32), axis=0)
    grad_outer_mat = jnp.einsum(
        "tf,td->fd", activated, grad_mlp, preferred_element_type=jnp.float32
    )
    grad_act = jnp.einsum("td,fd->tf", grad_mlp, outer_mat, preferred_element_type=jnp.float32)
    unused_value, gelu_pull = jax.vjp(exact_gelu, pre_act)
    grad_pre = gelu_pull(grad_act)[0].astype(jnp.bfloat16)
    grad_inner_add = jnp.sum(grad_pre.astype(jnp.float32), axis=0)
    grad_inner_mat = jnp.einsum(
        "td,tf->df", first_low, grad_pre, preferred_element_type=jnp.float32
    )
    grad_first = (
        jnp.einsum("tf,df->td", grad_pre, inner_mat, preferred_element_type=jnp.float32) + grad_two
    )
    grad_first_scale = jnp.sum(grad_first * first_normed, axis=0)
    grad_first_offset = jnp.sum(grad_first, axis=0)
    grad_hidden = norm_backward(
        grad_first, first_normed, first_inverse, first_scale.astype(jnp.float32)
    )
    grad_branch = grad_hidden.astype(jnp.bfloat16)
    grad_output_add = jnp.sum(grad_branch.astype(jnp.float32), axis=0)
    grad_output_mat = jnp.einsum(
        "td,te->de", attended, grad_branch, preferred_element_type=jnp.float32
    )
    grad_attended = jnp.einsum(
        "te,de->td", grad_branch, output_mat, preferred_element_type=jnp.float32
    ).astype(jnp.bfloat16)

    def backward_pair(pair_index, state_tuple):
        grad_queries, grad_keys, grad_values = state_tuple
        column_start = pair_index * 2 * HEAD
        query_pair = column_pair(queries, column_start, GROUP)
        key_pair = column_pair(keys_all, column_start, key_total)
        value_pair = column_pair(values_all, column_start, key_total)
        upstream_pair = column_pair(grad_attended, column_start, GROUP)
        scores = pair_scores(query_pair, key_pair, allowed, factor)
        pair_logsum = lax.dynamic_slice_in_dim(logsum, pair_index * 2, 2, 0)
        pair_probs = jnp.exp(scores - pair_logsum)
        weights = pair_probs.astype(jnp.bfloat16)
        grad_weights = jnp.einsum(
            "qhd,khd->hqk", upstream_pair, value_pair, preferred_element_type=jnp.float32
        )
        row_dot = jnp.sum(grad_weights * pair_probs, axis=-1, keepdims=True)
        grad_scores = (pair_probs * (grad_weights - row_dot)).astype(jnp.bfloat16)
        query_part = (
            jnp.einsum("hqk,khd->qhd", grad_scores, key_pair, preferred_element_type=jnp.float32)
            * factor
        )
        key_part = (
            jnp.einsum("hqk,qhd->khd", grad_scores, query_pair, preferred_element_type=jnp.float32)
            * factor
        )
        value_part = jnp.einsum(
            "hqk,qhd->khd", weights, upstream_pair, preferred_element_type=jnp.float32
        )
        grad_queries = lax.dynamic_update_slice_in_dim(
            grad_queries, query_part.reshape(GROUP, 2 * HEAD), column_start, 1
        )
        grad_keys = lax.dynamic_update_slice_in_dim(
            grad_keys, key_part.reshape(key_total, 2 * HEAD), column_start, 1
        )
        grad_values = lax.dynamic_update_slice_in_dim(
            grad_values, value_part.reshape(key_total, 2 * HEAD), column_start, 1
        )
        return (grad_queries, grad_keys, grad_values)

    grad_queries, grad_keys, grad_values = lax.fori_loop(
        0,
        pair_count,
        backward_pair,
        (
            jnp.zeros((GROUP, D), jnp.float32),
            jnp.zeros((key_total, D), jnp.float32),
            jnp.zeros((key_total, D), jnp.float32),
        ),
    )
    key_share, value_share = (
        lax.psum_scatter(
            grad_keys.astype(jnp.bfloat16), "seq", scatter_dimension=0, tiled=True
        ).astype(jnp.float32),
        lax.psum_scatter(
            grad_values.astype(jnp.bfloat16), "seq", scatter_dimension=0, tiled=True
        ).astype(jnp.float32),
    )
    grad_projected = jnp.concatenate(
        [
            grad_queries.astype(jnp.bfloat16),
            key_share.astype(jnp.bfloat16),
            value_share.astype(jnp.bfloat16),
        ],
        axis=1,
    )
    grad_query_add = jnp.sum(grad_projected[:, :D].astype(jnp.float32), axis=0)
    grad_value_add = jnp.sum(grad_projected[:, 2 * D :].astype(jnp.float32), axis=0)
    grad_attend_mat = jnp.einsum(
        "td,te->de", token_rows, grad_projected, preferred_element_type=jnp.float32
    )
    input_grad = grad_hidden + jnp.einsum(
        "te,de->td", grad_projected, attend_mat, preferred_element_type=jnp.float32
    )
    (
        sum_attend_mat,
        sum_query_add,
        sum_value_add,
        sum_output_mat,
        sum_output_add,
        sum_first_scale,
        sum_first_offset,
        sum_inner_mat,
        sum_inner_add,
        sum_outer_mat,
        sum_outer_add,
        sum_second_scale,
        sum_second_offset,
    ) = (
        lax.psum_scatter(grad_attend_mat, ("seq", "dp"), scatter_dimension=0, tiled=True),
        lax.psum_scatter(grad_query_add, ("seq", "dp"), scatter_dimension=0, tiled=True),
        lax.psum_scatter(grad_value_add, ("seq", "dp"), scatter_dimension=0, tiled=True),
        lax.psum_scatter(grad_output_mat, ("seq", "dp"), scatter_dimension=0, tiled=True),
        lax.psum_scatter(grad_output_add, ("seq", "dp"), scatter_dimension=0, tiled=True),
        lax.psum_scatter(grad_first_scale, ("seq", "dp"), scatter_dimension=0, tiled=True),
        lax.psum_scatter(grad_first_offset, ("seq", "dp"), scatter_dimension=0, tiled=True),
        lax.psum_scatter(grad_inner_mat, ("seq", "dp"), scatter_dimension=0, tiled=True),
        lax.psum_scatter(grad_inner_add, ("seq", "dp"), scatter_dimension=0, tiled=True),
        lax.psum_scatter(grad_outer_mat, ("seq", "dp"), scatter_dimension=0, tiled=True),
        lax.psum_scatter(grad_outer_add, ("seq", "dp"), scatter_dimension=0, tiled=True),
        lax.psum_scatter(grad_second_scale, ("seq", "dp"), scatter_dimension=0, tiled=True),
        lax.psum_scatter(grad_second_offset, ("seq", "dp"), scatter_dimension=0, tiled=True),
    )
    return (
        layer_output,
        input_grad.reshape(1, GROUP, D),
        sum_attend_mat,
        sum_query_add,
        sum_value_add,
        sum_output_mat,
        sum_output_add,
        sum_first_scale,
        sum_first_offset,
        sum_inner_mat,
        sum_inner_add,
        sum_outer_mat,
        sum_outer_add,
        sum_second_scale,
        sum_second_offset,
    )


AXES = ("seq", "dp")
DEVICES = 32
WIDE = ((3, 4, 2, 1), (3, 1, 4, 2))
NARROW = ((3, 2, 1, 4), (3, 2, 1, 4))
HINT = pl.CostEstimate(flops=1, bytes_accessed=1, transcendentals=0)
REMOTE = GROUP - 64
ROWS = GROUP + REMOTE


def swap(value, masks):
    pairs = [(i, i ^ masks[i & 1]) for i in range(DEVICES)]
    return lax.ppermute(value, AXES, pairs)


def sync(movers, *values):
    state, values = lax.optimization_barrier(([mover.data for mover in movers], values))
    for mover, data in zip(movers, state):
        mover.data = data
    return values


def stage_masks(order, stage):
    return (1 << order[0][stage], 1 << order[1][stage])


def chip_mask(bits, place):
    return sum(1 << b for t, b in enumerate(bits) if place >> t & 1)


def join_body(cut, *refs):
    sems = refs[-1]
    ins, outs = refs[: len(refs) - 3], refs[len(refs) - 3 : -1]
    copies = []
    for number, out_ref in enumerate(outs):
        width = out_ref.shape[2]
        for side in range(2):
            source = ins[side] if cut else ins[2 * number + side]
            count = source.shape[0]
            if cut:
                source = source.at[:, :, pl.ds(number * cut, width)]
            target = out_ref.at[pl.ds(side * count, count)]
            copies.append(pltpu.make_async_copy(source, target, sems.at[2 * number + side]))
    for copy in copies:
        copy.start()
    for copy in copies:
        copy.wait()


def join(pieces, cut=0):
    count, rows, columns = pieces[0].shape
    widths = (cut, columns - cut) if cut else (columns, pieces[2].shape[2])
    return pl.pallas_call(
        functools.partial(join_body, cut),
        out_shape=[
            jax.ShapeDtypeStruct((2 * count, rows, width), jnp.bfloat16) for width in widths
        ],
        in_specs=[pl.BlockSpec(memory_space=pl.ANY)] * len(pieces),
        out_specs=[pl.BlockSpec(memory_space=pltpu.VMEM)] * 2,
        scratch_shapes=[pltpu.SemaphoreType.DMA((4,))],
        compiler_params=pltpu.CompilerParams(vmem_limit_bytes=16 * 2**20),
        cost_estimate=HINT,
    )(*pieces)


class Gather:
    def __init__(self, me, weights, cut, extra=()):
        self.me, self.cut, self.data = me, cut, {}
        core = me & 1
        both = []
        for side in (core, 1 - core):
            parts = []
            for weight in weights:
                half = weight.shape[1] // 2
                parts.append(lax.dynamic_slice(weight, (0, side * half), (weight.shape[0], half)))
            parts.extend(extra)
            both.append(parts[0] if len(parts) == 1 else jnp.concatenate(parts, axis=1))
        self.data["mine"] = both[0]
        self.data["arrived"] = swap(both[1], (1, 1))

    def depth(self):
        mine, other = self.data["mine"], self.data["arrived"]
        first = (self.me & 1) == 0
        both = jnp.concatenate([jnp.where(first, mine, other), jnp.where(first, other, mine)])
        both = both[None]
        self.data = {"held": both, "arrived": swap(both, stage_masks(WIDE, 0))}

    def step(self, stage):
        held, arrived = self.data["held"], self.data["arrived"]
        if stage == 1:
            held = join([held, arrived], self.cut)
        else:
            held = join([piece for pair in zip(held, arrived) for piece in pair])
        arrived = [
            swap(piece, stage_masks(order, stage)) for piece, order in zip(held, (WIDE, NARROW))
        ]
        self.data = {"held": held, "arrived": arrived}

    def share(self, name, cuts=(0, 1)):
        shared = self.data.setdefault(name + " core", [None, None])
        for cut in cuts:
            shared[cut] = swap(self.data[name][cut], (1, 1))

    def pieces(self):
        names = ("held", "arrived", "held core", "arrived core")
        return [piece for name in names for piece in self.data[name]]


def gather_matmul_body(routes, count, tile, me_ref, left_ref, *refs):
    piece_refs = refs[:8]
    out_refs, product_ref = refs[8 : 8 + count], refs[8 + count]
    mats, in_sems, out_sems = refs[9 + count : 9 + 2 * count], refs[-2], refs[-1]
    me = me_ref[0]
    rows = piece_refs[0].shape[1]
    copies = []
    for number, piece in enumerate(piece_refs):
        chunk, arrived, side = number % 2, number // 2 % 2, number // 4
        order = (WIDE, NARROW)[chunk]
        base = me ^ side
        core = base & 1
        for sub in range(8):
            place = 8 * arrived + sub
            mask = jnp.where(core == 0, chip_mask(order[0], place), chip_mask(order[1], place))
            chip = (base ^ mask) >> 1
            for start, width, mat, begin in routes(chunk, mats):
                half = mat.shape[1] // 2
                target = mat.at[
                    pl.ds(pl.multiple_of(chip * rows, rows), rows),
                    pl.ds(pl.multiple_of(core * half + begin, 128), width),
                ]
                source = piece.at[sub, :, pl.ds(start, width)]
                copies.append(pltpu.make_async_copy(source, target, in_sems.at[len(copies)]))
    for copy in copies:
        copy.start()
    kept = []
    per_side = len(copies) // 2
    for side in range(2):
        core = (me ^ side) & 1
        for copy in copies[side * per_side : (side + 1) * per_side]:
            copy.wait()
        for number, (mat, out_ref) in enumerate(zip(mats, out_refs)):
            half = mat.shape[1] // 2
            columns = pl.ds(pl.multiple_of(core * half, half), half)
            kept.append(
                pltpu.make_async_copy(
                    mat.at[:, columns], out_ref.at[:, columns], out_sems.at[2 * number + side]
                )
            )
            kept[-1].start()
        half = product_ref.shape[1] // 2

        def step(i, carry):
            columns = pl.ds(pl.multiple_of(core * half + i * tile, tile), tile)
            product_ref[:, columns] = jnp.dot(
                left_ref[...], mats[0][:, columns], preferred_element_type=jnp.float32
            )
            return carry

        lax.fori_loop(0, half // tile, step, 0)
    for copy in kept:
        copy.wait()


def gather_matmul(gather, routes, widths, left):
    pieces = gather.pieces()
    depth = pieces[0].shape[1] * DEVICES // 2
    mats = [(depth, width) for width in widths]
    return pl.pallas_call(
        functools.partial(gather_matmul_body, routes, len(widths), 512),
        out_shape=[jax.ShapeDtypeStruct(mat, jnp.bfloat16) for mat in mats]
        + [jax.ShapeDtypeStruct((left.shape[0], widths[0]), jnp.float32)],
        in_specs=[
            pl.BlockSpec(memory_space=pltpu.SMEM),
            pl.BlockSpec(memory_space=pltpu.VMEM),
        ]
        + [pl.BlockSpec(memory_space=pl.ANY)] * 8,
        out_specs=[pl.BlockSpec(memory_space=pl.ANY)] * len(widths)
        + [pl.BlockSpec(memory_space=pltpu.VMEM)],
        scratch_shapes=[pltpu.VMEM(mat, jnp.bfloat16) for mat in mats]
        + [pltpu.SemaphoreType.DMA((96,)), pltpu.SemaphoreType.DMA((2 * len(widths),))],
        compiler_params=pltpu.CompilerParams(vmem_limit_bytes=40 * 2**20),
        cost_estimate=HINT,
    )(gather.me.reshape(1), left, *pieces)


def whole_routes(cut, chunk, outs):
    half = outs[0].shape[1] // 2
    return ((0, (cut, half - cut)[chunk], outs[0], chunk * cut),)


def first_routes(chunk, outs):
    if chunk == 0:
        return ((0, outs[0].shape[1] // 2, outs[0], 0),)
    half = outs[1].shape[1] // 2
    return ((0, half, outs[1], 0), (half, outs[2].shape[1] // 2, outs[2], 0))


def place_of(bits, shard):
    place = shard & 1
    for t, b in enumerate(bits):
        place = place | ((shard >> b) & 1) << (t + 1)
    return place


def weight_grad_body(chunks, tile, me_ref, left_ref, right_ref, *refs):
    extra_refs = refs[: -2 * len(chunks)]
    outs = refs[-2 * len(chunks) :]
    me = me_ref[0]
    rows = outs[0].shape[1]
    half = right_ref.shape[1] // 2
    per_tile = tile // rows

    def step(i, carry):
        left = left_ref[:, pl.ds(pl.multiple_of(i * tile, tile), tile)].T
        for side in (1, 0):
            base = me ^ side
            core = base & 1
            right = right_ref[:, pl.ds(pl.multiple_of(core * half, half), half)]
            product = jnp.dot(left, right, preferred_element_type=jnp.float32).astype(
                jnp.bfloat16
            )
            for sub in range(per_tile):
                number = i * per_tile + sub
                shard = number ^ base
                for which, (order, begin, width) in enumerate(chunks):
                    place = jnp.where(
                        core == 0, place_of(order[0], shard), place_of(order[1], shard)
                    )
                    out_ref = outs[2 * which + side]
                    out_ref[place, :, :width] = product[
                        sub * rows : (sub + 1) * rows, begin : begin + width
                    ]
                    for extra_ref in extra_refs:
                        out_ref[place, :, width:] = extra_ref[number]
        return carry

    lax.fori_loop(0, left_ref.shape[1] // tile, step, 0, unroll=2)


def weight_grad(left, right, me, chunks, extra=()):
    depth = left.shape[1]
    rows = depth // DEVICES
    more = sum(e.shape[2] for e in extra)
    shapes = [
        jax.ShapeDtypeStruct((DEVICES, rows, width + more), jnp.bfloat16)
        for _, _, width in chunks
        for _ in range(2)
    ]
    outs = pl.pallas_call(
        functools.partial(weight_grad_body, chunks, 256),
        out_shape=shapes,
        in_specs=[pl.BlockSpec(memory_space=pltpu.SMEM)]
        + [pl.BlockSpec(memory_space=pltpu.VMEM)] * (2 + len(extra)),
        out_specs=[pl.BlockSpec(memory_space=pltpu.VMEM)] * len(shapes),
        compiler_params=pltpu.CompilerParams(vmem_limit_bytes=24 * 2**20),
        cost_estimate=HINT,
    )(me.reshape(1), left, right, *extra)
    return [tuple(outs[i : i + 2]) for i in range(0, len(outs), 2)]


def add_low(one, two):
    return (one.astype(jnp.float32) + two.astype(jnp.float32)).astype(jnp.bfloat16)


def halve_body(*refs):
    count = len(refs) // 6
    for which in range(count):
        held_low, held_high, low, high = refs[4 * which : 4 * which + 4]
        keep_ref, send_ref = refs[4 * count + 2 * which : 4 * count + 2 * which + 2]
        send_ref[...] = add_low(held_high[...], high[...])
        keep_ref[...] = add_low(held_low[...], low[...])


def halve(pairs):
    half = pairs[0][0].shape[0] // 2
    block = max(half // 2, 1)
    steps = half // block
    specs, outs, shapes, values = [], [], [], []
    for held, arrived in pairs:
        _, rows, columns = held.shape
        low = pl.BlockSpec((block, rows, columns), lambda i: (i, 0, 0))
        high = pl.BlockSpec((block, rows, columns), lambda i: (steps + i, 0, 0))
        specs += [low, high, low, high]
        outs += [low, low]
        shapes += [jax.ShapeDtypeStruct((half, rows, columns), jnp.bfloat16)] * 2
        values += [held, held, arrived, arrived]
    results = pl.pallas_call(
        halve_body,
        grid=(steps,),
        in_specs=specs,
        out_specs=outs,
        out_shape=shapes,
        compiler_params=pltpu.CompilerParams(vmem_limit_bytes=16 * 2**20),
        cost_estimate=HINT,
    )(*values)
    return results[0::2], results[1::2]


def first_norm_body(
    rows_ref, mixed_ref, matrix_ref, add_ref, gain_ref, shift_ref, low_ref, out_ref, normed_ref, inverse_ref
):
    branch = jnp.dot(mixed_ref[...], matrix_ref[...], preferred_element_type=jnp.float32)
    out, normed, inverse = norm_forward(
        rows_ref[...].astype(jnp.float32) + (branch + add_ref[...]), gain_ref[...], shift_ref[...]
    )
    low_ref[...] = out.astype(jnp.bfloat16)
    out_ref[...] = out
    normed_ref[...] = normed
    inverse_ref[...] = inverse


def first_norm(rows, mixed, matrix, add, gain, shift):
    block = 128
    tall = pl.BlockSpec((block, D), lambda i: (i, 0))
    whole = pl.BlockSpec((1, D), lambda i: (0, 0))
    return pl.pallas_call(
        first_norm_body,
        grid=(GROUP // block,),
        in_specs=[tall, tall, pl.BlockSpec((D, D), lambda i: (0, 0)), whole, whole, whole],
        out_specs=[tall, tall, tall, pl.BlockSpec((block, 1), lambda i: (i, 0))],
        out_shape=[
            jax.ShapeDtypeStruct((GROUP, D), jnp.bfloat16),
            jax.ShapeDtypeStruct((GROUP, D), jnp.float32),
            jax.ShapeDtypeStruct((GROUP, D), jnp.float32),
            jax.ShapeDtypeStruct((GROUP, 1), jnp.float32),
        ],
        compiler_params=pltpu.CompilerParams(vmem_limit_bytes=20 * 2**20),
        cost_estimate=HINT,
    )(rows, mixed, matrix, add, gain, shift)


def rows_back_body(grad_ref, matrix_ref, near_ref, far_ref):
    product = lax.dot_general(
        grad_ref[...],
        matrix_ref[...],
        (((1,), (1,)), ((), ())),
        preferred_element_type=jnp.float32,
    )
    near_ref[...] = product[:GROUP]
    far_ref[...] = product[GROUP:].astype(jnp.bfloat16)


def rows_back(grad, matrix):
    return pl.pallas_call(
        rows_back_body,
        grid=(4,),
        in_specs=[
            pl.BlockSpec((ROWS, 3 * D), lambda i: (0, 0)),
            pl.BlockSpec((D // 4, 3 * D), lambda i: (i, 0)),
        ],
        out_specs=[
            pl.BlockSpec((GROUP, D // 4), lambda i: (0, i)),
            pl.BlockSpec((REMOTE, D // 4), lambda i: (0, i)),
        ],
        out_shape=[
            jax.ShapeDtypeStruct((GROUP, D), jnp.float32),
            jax.ShapeDtypeStruct((REMOTE, D), jnp.bfloat16),
        ],
        compiler_params=pltpu.CompilerParams(vmem_limit_bytes=16 * 2**20),
        cost_estimate=HINT,
    )(grad, matrix)


def cut_grads(me, left, right, cut):
    half = right.shape[1] // 2
    return weight_grad(left, right, me, ((WIDE, 0, cut), (NARROW, cut, half - cut)))


class Scatter:
    def __init__(self, me, grads):
        self.me, self.stage = me, 4
        self.data = {"held": [keep for keep, _ in grads], "send": [send for _, send in grads]}

    def begin(self):
        self.data["arrived"] = [swap(piece, (1, 1)) for piece in self.data.pop("send")]

    def step(self):
        self.stage -= 1
        held, send = halve(list(zip(self.data["held"], self.data["arrived"])))
        if self.stage == 0:
            held, send = jnp.concatenate(held, axis=2), jnp.concatenate(send, axis=2)
            arrived = swap(send, stage_masks(WIDE, 0))
        else:
            arrived = [
                swap(piece, stage_masks(order, self.stage))
                for piece, order in zip(send, (WIDE, NARROW))
            ]
        self.data = {"held": held, "arrived": arrived}

    def near(self):
        held, arrived = self.data["held"], self.data["arrived"]
        send = add_low(held[1], arrived[1])
        held = held[0].astype(jnp.float32) + arrived[0].astype(jnp.float32)
        self.data = {"held": held, "arrived": swap(send, (1, 1))}

    def result(self):
        held, arrived = self.data["held"], self.data["arrived"].astype(jnp.float32)
        first = (self.me & 1) == 0
        return jnp.where(first, held, arrived), jnp.where(first, arrived, held)


def masked_pair(keys):
    first = lax.broadcasted_iota(jnp.int32, keys.shape, 1) < HEAD
    zeros = jnp.zeros_like(keys)
    return jnp.where(first, keys, zeros), jnp.where(first, zeros, keys)


PAIRS = 2
WIDTH = PAIRS * 128
STEPS = D // WIDTH


def attend_forward_body(query_docs, key_docs, query_ref, key_ref, value_ref, mixed_ref, log_ref):
    allowed = key_docs[...] == query_docs[...]
    for pair in range(PAIRS):
        columns = slice(pair * 128, (pair + 1) * 128)
        queries = query_ref[:, columns]
        value_rows = value_ref[:, columns].T
        results = []
        for head, keys in enumerate(masked_pair(key_ref[:, columns])):
            raw = lax.dot_general(
                keys, queries, (((1,), (1,)), ((), ())), preferred_element_type=jnp.float32
            )
            scores = jnp.where(allowed, raw * HEAD**-0.5, masked_score)
            peak = jnp.max(scores, axis=0, keepdims=True)
            terms = jnp.exp(scores - peak)
            total = jnp.sum(terms, axis=0, keepdims=True)
            weights = (terms * (1.0 / total)).astype(jnp.bfloat16)
            results.append(
                jnp.dot(
                    value_rows[head * HEAD : (head + 1) * HEAD],
                    weights,
                    preferred_element_type=jnp.float32,
                )
            )
            log_ref[pair, head : head + 1] = peak + jnp.log(total)
        mixed_ref[:, columns] = jnp.concatenate(results).T.astype(jnp.bfloat16)


def attend_specs():
    return [
        pl.BlockSpec((1, GROUP), lambda i: (0, 0)),
        pl.BlockSpec((ROWS, 1), lambda i: (0, 0)),
        pl.BlockSpec((GROUP, WIDTH), lambda i: (0, i)),
        pl.BlockSpec((ROWS, WIDTH), lambda i: (0, STEPS + i)),
        pl.BlockSpec((ROWS, WIDTH), lambda i: (0, 2 * STEPS + i)),
    ]


def attend_forward(query_docs, key_docs, projected):
    return pl.pallas_call(
        attend_forward_body,
        grid=(STEPS,),
        in_specs=attend_specs(),
        out_specs=[
            pl.BlockSpec((GROUP, WIDTH), lambda i: (0, i)),
            pl.BlockSpec((PAIRS, 2, GROUP), lambda i: (i, 0, 0)),
        ],
        out_shape=[
            jax.ShapeDtypeStruct((GROUP, D), jnp.bfloat16),
            jax.ShapeDtypeStruct((HEADS // 2, 2, GROUP), jnp.float32),
        ],
        compiler_params=pltpu.CompilerParams(vmem_limit_bytes=16 * 2**20),
        cost_estimate=HINT,
    )(query_docs, key_docs, projected, projected, projected)


def attend_backward_body(
    query_docs, key_docs, query_ref, key_ref, value_ref, upstream_ref, log_ref, grad_ref, sum_ref
):
    allowed = key_docs[...] == query_docs[...]
    across = (((1,), (1,)), ((), ()))
    wide = lax.broadcasted_iota(jnp.int32, (ROWS, 128), 1) < HEAD
    for pair in range(PAIRS):
        columns = slice(pair * 128, (pair + 1) * 128)
        queries, upstream = query_ref[:, columns], upstream_ref[:, columns]
        key_rows = key_ref[:, columns].T
        pairs = zip(masked_pair(key_ref[:, columns]), masked_pair(value_ref[:, columns]))
        query_parts, key_parts, value_parts = [], [], []
        for head, (keys, values) in enumerate(pairs):
            raw = lax.dot_general(keys, queries, across, preferred_element_type=jnp.float32)
            scores = jnp.where(allowed, raw * HEAD**-0.5, masked_score)
            probs = jnp.exp(scores - log_ref[pair, head : head + 1])
            grad_weights = lax.dot_general(
                values, upstream, across, preferred_element_type=jnp.float32
            )
            row_dot = jnp.sum(grad_weights * probs, axis=0, keepdims=True)
            grad_scores = (probs * (grad_weights - row_dot)).astype(jnp.bfloat16)
            weights = probs.astype(jnp.bfloat16)
            query_parts.append(
                jnp.dot(
                    key_rows[head * HEAD : (head + 1) * HEAD],
                    grad_scores,
                    preferred_element_type=jnp.float32,
                )
            )
            key_parts.append(jnp.dot(grad_scores, queries, preferred_element_type=jnp.float32))
            value_parts.append(jnp.dot(weights, upstream, preferred_element_type=jnp.float32))
        grad_queries = (jnp.concatenate(query_parts).T * HEAD**-0.5).astype(jnp.bfloat16)
        grad_keys = jnp.where(wide, key_parts[0], key_parts[1]) * HEAD**-0.5
        grad_values = jnp.where(wide, value_parts[0], value_parts[1]).astype(jnp.bfloat16)
        start = pl.program_id(0) * WIDTH + pair * 128
        query_at, key_at, value_at = (
            pl.ds(pl.multiple_of(start + part * D, 128), 128) for part in range(3)
        )
        grad_ref[:GROUP, query_at] = grad_queries
        grad_ref[GROUP:, query_at] = jnp.zeros((REMOTE, 128), jnp.bfloat16)
        grad_ref[:, key_at] = grad_keys.astype(jnp.bfloat16)
        grad_ref[:, value_at] = grad_values
        low = grad_queries.astype(jnp.float32)
        sum_ref[0, :, query_at] = jnp.sum(low, axis=0, keepdims=True)
        low = grad_values.astype(jnp.float32)
        sum_ref[1, :, query_at] = jnp.sum(low, axis=0, keepdims=True)


def attend_backward(query_docs, key_docs, projected, upstream, logs):
    return pl.pallas_call(
        attend_backward_body,
        grid=(STEPS,),
        in_specs=attend_specs()
        + [
            pl.BlockSpec((GROUP, WIDTH), lambda i: (0, i)),
            pl.BlockSpec((PAIRS, 2, GROUP), lambda i: (i, 0, 0)),
        ],
        out_specs=[
            pl.BlockSpec((ROWS, 3 * D), lambda i: (0, 0)),
            pl.BlockSpec((2, 1, D), lambda i: (0, 0, 0)),
        ],
        out_shape=[
            jax.ShapeDtypeStruct((ROWS, 3 * D), jnp.bfloat16),
            jax.ShapeDtypeStruct((2, 1, D), jnp.float32),
        ],
        compiler_params=pltpu.CompilerParams(vmem_limit_bytes=16 * 2**20),
        cost_estimate=HINT,
    )(query_docs, key_docs, projected, projected, projected, upstream, logs)


def pack_shard(vectors):
    rows = jnp.concatenate([vector.reshape(-1, 32) for vector in vectors])
    return jnp.pad(rows, ((0, 32 - rows.shape[0]), (0, 96)))


def unpack_shards(packed):
    rows = packed.reshape(DEVICES, 32, 256)[:, :12, :32].astype(jnp.float32)
    short = rows[:, :8].transpose(1, 0, 2).reshape(8, 1, D)
    return [short[i] for i in range(8)] + [rows[:, 8:].reshape(1, 4 * D)]


def pack_grads(short, long):
    rows = jnp.concatenate([vector.reshape(1, 8, 128) for vector in short])
    rows = jnp.repeat(rows.transpose(1, 0, 2), 4, axis=0)
    rows = jnp.concatenate([rows, long.reshape(DEVICES, 1, 128)], axis=1)
    return jnp.pad(rows, ((0, 0), (0, 23), (0, 0))).astype(jnp.bfloat16)


def fast_local(
    tokens,
    cotangent,
    doc_lengths,
    attend_weight,
    query_bias,
    value_bias,
    output_weight,
    output_bias,
    first_gain,
    first_shift,
    inner_weight,
    inner_bias,
    outer_weight,
    outer_bias,
    second_gain,
    second_shift,
):
    me = lax.axis_index(AXES)
    group_index = me >> 4
    small_shard = pack_shard(
        [
            query_bias,
            value_bias,
            output_bias,
            first_gain,
            first_shift,
            outer_bias,
            second_gain,
            second_shift,
            inner_bias,
        ]
    )
    attend_cut, inner_cut, outer_cut = 3 * D // 2, 1408, 384
    one = Gather(me, (attend_weight, output_weight), attend_cut, (small_shard,))
    sync((one,))

    one.depth()
    two = Gather(me, (inner_weight,), inner_cut)
    three = Gather(me, (outer_weight,), outer_cut)
    movers = (one, two, three)
    doc_ends = jnp.cumsum(doc_lengths[0])
    near_at = group_index * GROUP + lax.iota(jnp.int32, GROUP)
    far_at = jnp.where(group_index == 0, GROUP, 64) + lax.iota(jnp.int32, REMOTE)
    row_at = jnp.concatenate([near_at, far_at])
    row_docs = jnp.sum((row_at[:, None] >= doc_ends[None, :]).astype(jnp.int32), axis=1)
    query_docs, key_docs = row_docs[None, :GROUP], row_docs[:, None]
    near = tokens.reshape(GROUP, D)
    query_docs, key_docs, near = sync(movers, query_docs, key_docs, near)

    one.step(1)
    two.depth()
    far = lax.dynamic_slice(near, (64 * (1 - group_index), 0), (REMOTE, D))
    far = lax.ppermute(far, "seq", [(0, 1), (1, 0)])
    (far,) = sync((one, two), far)

    one.step(2)
    token_rows = jnp.concatenate([near, far])
    (token_rows,) = sync((one, two), token_rows)

    one.step(3)
    two.step(1)
    three.depth()
    sync(movers)

    one.share("held")
    one.share("arrived")
    sync((one,))

    two.step(2)
    three.step(1)
    attend_mat, output_mat, small_all, projected = gather_matmul(
        one, first_routes, (3 * D, D, 256), token_rows
    )
    (
        query_add,
        value_add,
        output_add,
        first_scale,
        first_offset,
        outer_add,
        second_scale,
        second_offset,
        inner_add,
    ) = unpack_shards(small_all)
    bias_row = jnp.concatenate([query_add, jnp.zeros((1, D), jnp.float32), value_add], axis=1)
    projected = (projected + bias_row).astype(jnp.bfloat16)
    (projected,) = sync((two, three), projected)

    two.step(3)
    two.share("held", (0,))
    three.step(2)
    attended, logs = attend_forward(query_docs, key_docs, projected)
    first_low, first_out, first_normed, first_inverse = first_norm(
        near, attended, output_mat, output_add, first_scale, first_offset
    )
    first_out, first_normed, first_inverse, first_low = sync(
        (two, three), first_out, first_normed, first_inverse, first_low
    )

    two.share("held", (1,))
    two.share("arrived")
    sync((two,))

    three.step(3)
    three.share("held")
    inner_mat, pre_act = gather_matmul(
        two, functools.partial(whole_routes, inner_cut), (4 * D,), first_low
    )
    pre_act = pre_act + inner_add
    cdf = 0.5 * (1.0 + lax.erf(pre_act * 0.5**0.5))
    gelu_slope = cdf + pre_act * jnp.exp(-0.5 * pre_act * pre_act) * 0.3989422804014327
    activated = (pre_act * cdf).astype(jnp.bfloat16)
    activated, gelu_slope = sync((three,), activated, gelu_slope)

    three.share("arrived")
    outer_mat, mlp_out = gather_matmul(
        three, functools.partial(whole_routes, outer_cut), (D,), activated
    )
    mlp_out = mlp_out + outer_add
    second_out, second_normed, second_inverse = norm_forward(
        first_out + mlp_out, second_scale, second_offset
    )
    layer_output = second_out.astype(jnp.bfloat16).reshape(1, GROUP, D)
    upstream = cotangent.reshape(GROUP, D).astype(jnp.float32)
    grad_two = norm_backward(upstream, second_normed, second_inverse, second_scale)
    grad_mlp = grad_two.astype(jnp.bfloat16)
    outer = Scatter(me, cut_grads(me, activated, grad_mlp, outer_cut))
    grad_mlp, grad_two, second_normed = sync((outer,), grad_mlp, grad_two, second_normed)

    outer.begin()
    grad_act = jnp.einsum("td,fd->tf", grad_mlp, outer_mat, preferred_element_type=jnp.float32)
    grad_pre = (grad_act * gelu_slope).astype(jnp.bfloat16)
    inner_sum = jnp.sum(grad_pre.astype(jnp.float32), axis=0)
    grad_pre, inner_sum, grad_mlp, second_normed = sync(
        (outer,), grad_pre, inner_sum, grad_mlp, second_normed
    )

    outer.step()
    inner = Scatter(me, cut_grads(me, first_low, grad_pre, inner_cut))
    second_sums = (
        jnp.sum(grad_mlp.astype(jnp.float32), axis=0),
        jnp.sum(upstream * second_normed, axis=0),
        jnp.sum(upstream, axis=0),
    )
    grad_first = (
        jnp.einsum("tf,df->td", grad_pre, inner_mat, preferred_element_type=jnp.float32) + grad_two
    )
    grad_hidden = norm_backward(grad_first, first_normed, first_inverse, first_scale)
    grad_branch = grad_hidden.astype(jnp.bfloat16)
    first_sums = (
        jnp.sum(grad_branch.astype(jnp.float32), axis=0),
        jnp.sum(grad_first * first_normed, axis=0),
        jnp.sum(grad_first, axis=0),
    )
    grad_attended = jnp.einsum(
        "te,de->td", grad_branch, output_mat, preferred_element_type=jnp.float32
    ).astype(jnp.bfloat16)
    first_sums, second_sums, grad_hidden, grad_branch, grad_attended = sync(
        (outer, inner), first_sums, second_sums, grad_hidden, grad_branch, grad_attended
    )

    inner.begin()
    outer.step()
    grad_projected, row_sums = attend_backward(
        query_docs, key_docs, projected, grad_attended, logs
    )
    grad_projected, row_sums = sync((outer, inner), grad_projected, row_sums)

    inner.step()
    outer.step()
    small = pack_grads([row_sums[0, 0], row_sums[1, 0], *first_sums, *second_sums], inner_sum)
    first = Scatter(
        me,
        weight_grad(token_rows, grad_projected, me, ((WIDE, 0, attend_cut),))
        + weight_grad(attended, grad_branch, me, ((NARROW, 0, D // 2),), (small,)),
    )
    movers = (outer, inner, first)
    sync(movers)

    first.begin()
    inner.step()
    row_grad, far_grad = rows_back(grad_projected, attend_mat)
    row_grad, far_grad = sync((inner, first), row_grad, far_grad)

    first.step()
    inner.step()
    outer.step()
    sync(movers)

    first.step()
    inner.step()
    outer.near()
    sync(movers)

    first.step()
    inner.near()
    sum_outer_mat = jnp.concatenate(outer.result(), axis=1)
    sum_outer_mat, far_grad = sync((inner, first), sum_outer_mat, far_grad)

    first.step()
    far_grad = lax.ppermute(far_grad, "seq", [(0, 1), (1, 0)])
    sum_inner_mat = jnp.concatenate(inner.result(), axis=1)
    sum_inner_mat, far_grad = sync((first,), sum_inner_mat, far_grad)

    first.near()
    filler = jnp.zeros((64, D), jnp.float32)
    far_grad = far_grad.astype(jnp.float32)
    far_grad = jnp.where(
        group_index == 0,
        jnp.concatenate([filler, far_grad]),
        jnp.concatenate([far_grad, filler]),
    )
    input_grad = grad_hidden + row_grad + far_grad
    halves = first.result()
    output_end = attend_cut + D // 2
    sum_attend_mat = jnp.concatenate([half[:, :attend_cut] for half in halves], axis=1)
    sum_output_mat = jnp.concatenate([half[:, attend_cut:output_end] for half in halves], axis=1)
    small_rows = halves[0][:, output_end:]
    own = lax.dynamic_slice(small_rows, (0, 32 * (me & 3)), (8, 32))
    (
        sum_query_add,
        sum_value_add,
        sum_output_add,
        sum_first_scale,
        sum_first_offset,
        sum_outer_add,
        sum_second_scale,
        sum_second_offset,
    ) = (own[i] for i in range(8))
    sum_inner_add = small_rows[8]
    return (
        layer_output,
        input_grad.reshape(1, GROUP, D),
        sum_attend_mat,
        sum_query_add,
        sum_value_add,
        sum_output_mat,
        sum_output_add,
        sum_first_scale,
        sum_first_offset,
        sum_inner_mat,
        sum_inner_add,
        sum_outer_mat,
        sum_outer_add,
        sum_second_scale,
        sum_second_offset,
    )


def solution(mesh):
    sizes = (mesh.shape["seq"], mesh.shape["dp"])
    return jax.shard_map(
        fast_local if sizes == (2, 16) else general_local,
        mesh=mesh,
        in_specs=(
            P("dp", "seq", None),
            P("dp", "seq", None),
            P("dp", None),
            P(("seq", "dp"), None),
            P(("seq", "dp")),
            P(("seq", "dp")),
            P(("seq", "dp"), None),
            P(("seq", "dp")),
            P(("seq", "dp")),
            P(("seq", "dp")),
            P(("seq", "dp"), None),
            P(("seq", "dp")),
            P(("seq", "dp"), None),
            P(("seq", "dp")),
            P(("seq", "dp")),
            P(("seq", "dp")),
        ),
        out_specs=(
            P("dp", "seq", None),
            P("dp", "seq", None),
            P(("seq", "dp"), None),
            P(("seq", "dp")),
            P(("seq", "dp")),
            P(("seq", "dp"), None),
            P(("seq", "dp")),
            P(("seq", "dp")),
            P(("seq", "dp")),
            P(("seq", "dp"), None),
            P(("seq", "dp")),
            P(("seq", "dp"), None),
            P(("seq", "dp")),
            P(("seq", "dp")),
            P(("seq", "dp")),
        ),
        check_vma=False,
    )
```
